128 devices in a mesh: blk: 32 (over z, y, core), rep: 4 (over x).
Axes of the slice: x: 4, y: 4, z: 4, core: 2. Of those that a mesh axis runs over, the one named last changes fastest.
Arguments:
- tiles: bfloat16 [4, 1024, 128, 128], P('rep', 'blk'), may hold values from -6 to 6
- tile_rows: int32 [4, 1024], P('rep', 'blk'), may hold values from 1 to 128
- tile_owner: int32 [4, 1024, 1], P('rep', 'blk'), may hold values from 0 to 31; in each aligned block of 32 rows (0 to 31, 32 to 63, ..., all dimensions but the last counted through in order) at most 2 rows name the same one
- tile_slot: int32 [4, 1024], P('rep', 'blk'), may hold values from 0 to 15
- neighbors: int32 [4, 128, 27], P('rep', 'blk'), may hold values from -1 to 11, as said below
- w_enc: bfloat16 [27, 128, 128], replicated, may hold values from -0.109375 to 0.109375
- w_coarse: bfloat16 [128, 128], replicated, may hold values from -0.5 to 0.5
- w_dec: bfloat16 [27, 128, 128], replicated, may hold values from -0.109375 to 0.109375
- cotangent: bfloat16 [4, 128, 512, 128], P('rep', 'blk'), may hold values from -0.01171875 to 0.01171875
Outputs:
- decoded: bfloat16 [4, 128, 512, 128], P('rep', 'blk')
- weight_grad: float32 [27, 128, 128], replicated
The draws below stay inside these ranges and needn't reach their ends.
Inputs may be any that keep to these rules, and one draw needn't show every extreme that they name: `tile_owner`: among the tiles of one index of blk, no owner is named by more than 2; some owner is named by exactly 2. `neighbors`: entry 13 of block g is 4 + g % 4. An entry e >= 0 names block e of the three consecutive blk indices index - 1, index, index + 1 laid end to end; -1 means no active neighbour.
All inputs are finite; a program needn't handle non-finite values.
Results may differ from the reference program's by a relative error of at most 0.013.
Values may be sent and summed in bfloat16 or wider, within the bound.
A program may use at most 64 MiB of HBM per device.

```python
import math
import jax
import jax.numpy as jnp
import numpy as np

C = 128
TROWS = 128
SIB = 4
BLK_DEV = 4
VOXELS = 512
TILES_DEV = 32
CAP = 2
NTILES = 1024
NBLOCKS = 128
N_BLK = 32
N_REP = 4


def draw_neighbors(key, part):
    key = jax.random.fold_in(key, 11)
    key_pick, key_keep = jax.random.split(key)
    shape = (N_REP, NBLOCKS, 27)
    chosen = jax.random.randint(key_pick, shape, 0, 3 * BLK_DEV)
    present = jax.random.randint(key_keep, shape, 0, 5) > 0
    lookup = jnp.where(present, chosen, -1)
    itself = BLK_DEV + jnp.arange(NBLOCKS, dtype=jnp.int32) % BLK_DEV
    centre = jnp.broadcast_to(itself[None, :], (N_REP, NBLOCKS))
    return lookup.at[:, :, 13].set(centre).astype(jnp.int32)


def set_ends(entries, key, low, top_value):
    longest = entries.shape.index(max(entries.shape))
    spots = []
    for shift in (0, 1):
        where = [jax.random.randint(jax.random.fold_in(key, axis), (), 0, length) for axis, length in enumerate(entries.shape)]
        where[longest] = (where[longest] + shift) % entries.shape[longest]
        spots.append(tuple(where))
    return entries.at[spots[0]].set(low).at[spots[1]].set(top_value)


def block_levels(stream_key, dims, pieces, smallest, top_value):
    def one(axis_at, shards_of):
        draws = jax.random.uniform(jax.random.fold_in(jax.random.fold_in(stream_key, 6), axis_at), (shards_of,), jnp.float32, smallest / len(pieces), top_value / len(pieces))
        return jnp.repeat(jnp.exp(draws), dims[axis_at] // shards_of).reshape((-1,) + (1,) * (len(dims) - axis_at - 1))

    level = one(*pieces[0])
    for cut in pieces[1:]:
        level = level * one(*cut)
    return level


def deal_out(key, own, number, rows, count, top, most, slope):
    order = jax.random.permutation(key, count)
    heavy_load, ordinary = load_shares(count, rows * top, most, slope, True), load_shares(count, rows * top, most, slope, False)
    places = jnp.arange(count)

    def named(tallies, offset_by):
        used = int((tallies > 0).sum())
        fixed = max(1, used // 4)
        passed = fixed + (places - fixed + offset_by * (used - fixed)) % max(1, count - fixed)
        return jnp.zeros((count,), jnp.int32).at[order[jnp.where(places < fixed, places, passed)]].set(jnp.asarray(tallies, jnp.int32))

    tallies = jnp.where(number % 4 == 0, named(heavy_load, number // 4), named(ordinary, number - number // 4 - 1))
    mixed = jax.random.permutation(jax.random.fold_in(own, 3), count)
    giver, taker = mixed[0:count // 2 * 2:2], mixed[1:count // 2 * 2:2]
    slack = jnp.minimum(tallies[giver] - 1, most - tallies[taker]) // 2
    slack = jnp.where((giver == order[0]) | (taker == order[0]) | (tallies[taker] == 0), 0, jnp.maximum(slack, 0))
    passed = jax.random.randint(jax.random.fold_in(own, 4), (count // 2,), 0, 1 << 20) % (slack + 1)
    tallies = tallies.at[giver].add(-passed).at[taker].add(passed)
    labels = jnp.searchsorted(jnp.cumsum(tallies), jnp.arange(rows * top), side="right").astype(jnp.int32)
    grid = labels.reshape(top, rows).T
    grid = grid[jax.random.permutation(jax.random.fold_in(own, 1), rows)]
    offset_by = jax.random.randint(jax.random.fold_in(own, 2), (rows, 1), 0, top)
    return jnp.take_along_axis(grid, (jnp.arange(top)[None, :] + offset_by) % top, axis=1)


def load_shares(count, total, limit, slope, full):
    portions = [(1 << 20) // math.isqrt(standing ** slope) + 1 for standing in range(1, count + 1)]
    largest = limit if full else min(limit, max(-(-total // count), total * portions[0] // sum(portions)))
    least = 1 if total - largest >= count - 1 else 0
    counts, surplus = [largest] + [least] * (count - 1), total - largest - least * (count - 1)
    while surplus > 0:
        movable = [i for i in range(1, count) if counts[i] < largest] or [i for i in range(1, count) if counts[i] < limit]
        pool, remaining = sum([portions[i] for i in movable]), surplus
        for i in movable:
            addition = min(limit - counts[i], max(1, remaining * portions[i] // pool), surplus)
            counts[i] = counts[i] + addition
            surplus = surplus - addition
    return np.array(counts)


def gaussian(own_key, shape, scale, bound, pieces=(), held_as=jnp.bfloat16):
    loudness = block_levels(own_key, shape, pieces, -0.22, 0.18) if pieces else 1.0
    values = jax.random.normal(own_key, shape, jnp.float32) * scale * loudness
    return jnp.minimum(jnp.maximum(values, -bound), bound).astype(held_as)


def setup_inputs(seed: int = 0) -> dict:
    key_list = jax.random.split(jax.random.key(seed), 10)
    tiles = gaussian(key_list[0], (N_REP, NTILES, TROWS, C), 1.0, 6.0, ((0, 4), (1, 32)))
    tile_rows = set_ends(jax.random.randint(key_list[1], (N_REP, NTILES), 1, 129), jax.random.fold_in(key_list[1], 1), 1, 128).astype(jnp.int32)
    tile_owner_keys = jax.random.split(jax.random.fold_in(key_list[2], 1), N_REP * NTILES // TILES_DEV)
    tile_owner_turns = jax.random.permutation(jax.random.fold_in(key_list[2], 3), N_REP * NTILES // TILES_DEV)
    tile_owner = jax.vmap(lambda own, number: deal_out(jax.random.fold_in(key_list[2], 2), own, number, TILES_DEV, N_BLK, 1, CAP, 2))(tile_owner_keys, tile_owner_turns).reshape((N_REP, NTILES, 1))
    tile_slot = set_ends(jax.random.randint(key_list[3], (N_REP, NTILES), 0, 4 * BLK_DEV), jax.random.fold_in(key_list[3], 1), 0, (4 * BLK_DEV) - 1).astype(jnp.int32)
    neighbors = draw_neighbors(jax.random.fold_in(key_list[9], 71), 0)
    w_enc = gaussian(key_list[5], (27, C, C), (27 * C) ** -0.5, 0.109375)
    w_coarse = gaussian(key_list[6], (C, C), C ** -0.5, 0.5)
    w_dec = gaussian(key_list[7], (27, C, C), (27 * C) ** -0.5, 0.109375)
    cotangent = gaussian(key_list[8], (N_REP, NBLOCKS, VOXELS, C), ((N_REP * NBLOCKS * VOXELS) ** -0.5), 0.01171875, ((0, 4), (1, 32)))
    return {"tiles": tiles, "tile_rows": tile_rows, "tile_owner": tile_owner, "tile_slot": tile_slot, "neighbors": neighbors, "w_enc": w_enc, "w_coarse": w_coarse, "w_dec": w_dec, "cotangent": cotangent}


OFFSETS = [(off_x, off_y, off_z) for off_x in (-1, 0, 1) for off_y in (-1, 0, 1) for off_z in (-1, 0, 1)]


def span(offset):
    if offset < 0:
        return slice(7, 8)
    if offset > 0:
        return slice(0, 1)
    return slice(0, 8)


def padded_blocks(volume, lookup):
    count = volume.shape[0]
    home = (jnp.arange(count, dtype=jnp.int32) // BLK_DEV - 1) * BLK_DEV
    target = home[:, None] + lookup
    present = (lookup >= 0) & (target >= 0) & (target < count)
    safe_target = jnp.clip(target, 0, count - 1).astype(jnp.int32)
    layers = []
    for off_x in (-1, 0, 1):
        planes = []
        for off_y in (-1, 0, 1):
            cells = []
            for off_z in (-1, 0, 1):
                column = (off_x + 1) * 9 + (off_y + 1) * 3 + off_z + 1
                slab = volume[:, span(off_x), span(off_y), span(off_z)]
                picked = jnp.take(slab, safe_target[:, column], axis=0)
                cells.append(jnp.where(present[:, column][:, None, None, None, None], picked, jnp.zeros((), volume.dtype)))
            planes.append(jnp.concatenate(cells, axis=3))
        layers.append(jnp.concatenate(planes, axis=2))
    return jnp.concatenate(layers, axis=1)


def shifted(padded, column):
    off_x, off_y, off_z = OFFSETS[column]
    piece = padded[:, off_x + 1:off_x + 9, off_y + 1:off_y + 9, off_z + 1:off_z + 9]
    return piece.reshape(-1, padded.shape[-1])


def convolve(padded, weight):
    total = jnp.zeros((padded.shape[0] * 512, padded.shape[-1]), jnp.float32)
    for column in range(27):
        total = total + jnp.dot(shifted(padded, column), weight[column], preferred_element_type=jnp.float32)
    return total


def one_slab(tiles, tile_rows, tile_owner, tile_slot, neighbors, w_enc, w_coarse, w_dec, cotangent):
    count = neighbors.shape[0]
    width = tiles.shape[-1]
    lanes = jnp.arange(tiles.shape[1], dtype=jnp.int32)
    masked = jnp.where(lanes[None, :, None] < tile_rows[:, None, None], tiles, jnp.zeros((), tiles.dtype))
    quarter = (tile_owner[:, 0] * (4 * BLK_DEV) + tile_slot).astype(jnp.int32)
    landed = jax.ops.segment_sum(masked.astype(jnp.float32), quarter, num_segments=4 * count)
    voxels = landed.astype(jnp.bfloat16).reshape(count, 8, 8, 8, width)
    encoded = jax.nn.relu(convolve(padded_blocks(voxels, neighbors), w_enc)).astype(jnp.bfloat16)
    encoded = encoded.reshape(count, 8, 8, 8, width)
    pooled = encoded.astype(jnp.float32).reshape(count, 4, 2, 4, 2, 4, 2, width).mean(axis=(2, 4, 6))
    grouped = pooled.reshape(count // (SIB * BLK_DEV), SIB, BLK_DEV, 4, 4, 4, width)
    summed = jnp.sum(grouped, axis=1, keepdims=True) / SIB
    sibling = jnp.broadcast_to(summed, grouped.shape).reshape(count * 64, width).astype(jnp.bfloat16)
    coarse = jax.nn.relu(jnp.dot(sibling, w_coarse, preferred_element_type=jnp.float32))
    coarse = coarse.reshape(count, 4, 4, 4, width)
    upsampled = jnp.repeat(jnp.repeat(jnp.repeat(coarse, 2, axis=1), 2, axis=2), 2, axis=3)
    joined = (encoded.astype(jnp.float32) + upsampled).astype(jnp.bfloat16)
    padded = padded_blocks(joined, neighbors)
    decoded = (convolve(padded, w_dec) + joined.reshape(-1, width).astype(jnp.float32)).astype(jnp.bfloat16)
    flat_cot = cotangent.reshape(-1, width)
    grads = jnp.stack([jnp.dot(shifted(padded, column).T, flat_cot, preferred_element_type=jnp.float32) for column in range(27)])
    return decoded.reshape(count, 512, width), grads


def reference(tiles, tile_rows, tile_owner, tile_slot, neighbors, w_enc, w_coarse, w_dec, cotangent):
    outputs = []
    grad_total = jnp.zeros((27, tiles.shape[-1], tiles.shape[-1]), jnp.float32)
    for slab in range(N_REP):
        decoded, grads = one_slab(tiles[slab], tile_rows[slab], tile_owner[slab], tile_slot[slab], neighbors[slab], w_enc, w_coarse, w_dec, cotangent[slab])
        outputs.append(decoded)
        grad_total = grad_total + grads
    return jnp.stack(outputs), grad_total
```

```python
import functools

import jax
import jax.numpy as jnp
from jax import lax
from jax.experimental import pallas as pl
from jax.experimental.pallas import tpu as pltpu
from jax.sharding import PartitionSpec as P

C = 128
CAP = 2
BLK = 4
SIB = 4
F32 = jnp.float32
BF16 = jnp.bfloat16
MESH = pl.DeviceIdType.MESH
VMEM_LIMIT = 48 * 1024 * 1024


def at_blk(index):
    return {"blk": index}


def at_rep(index):
    return {"rep": index}


def bucket_kernel(count, peers, owner_ref, rows_ref, slot_ref, tiles_ref, out_ref, label_ref, used):
    def clear(o, carry):
        used[o] = 0
        for r in range(CAP):
            label_ref[o, 0, r] = -1
        return carry

    lax.fori_loop(0, peers, clear, 0)
    row = lax.broadcasted_iota(jnp.int32, (C, C), 0)

    def place(t, carry):
        owner = owner_ref[t]
        rank = used[owner]
        used[owner] = rank + 1
        label_ref[owner, 0, rank] = slot_ref[t]
        tile = tiles_ref[t].astype(F32)
        out_ref[owner, rank] = jnp.where(row < rows_ref[t], tile, 0.0).astype(BF16)
        return carry

    lax.fori_loop(0, count, place, 0)


def exchange_kernel(peers, out_ref, label_ref, in_ref, in_label_ref, sems, local_sems):
    me = lax.axis_index("blk")
    barrier = pltpu.get_barrier_semaphore()

    def greet(d, carry):
        pl.semaphore_signal(
            barrier, inc=1, device_id=at_blk(lax.rem(me + d, peers)), device_id_type=MESH
        )
        return carry

    lax.fori_loop(1, peers, greet, 0)
    pl.semaphore_wait(barrier, peers - 1)

    def copies(d):
        peer = lax.rem(me + d, peers)
        yield pltpu.make_async_remote_copy(
            src_ref=label_ref.at[peer],
            dst_ref=in_label_ref.at[me],
            send_sem=sems.at[0, d],
            recv_sem=sems.at[1, d],
            device_id=at_blk(peer),
            device_id_type=MESH,
        )
        yield pltpu.make_async_remote_copy(
            src_ref=out_ref.at[peer],
            dst_ref=in_ref.at[me],
            send_sem=sems.at[2, d],
            recv_sem=sems.at[3, d],
            device_id=at_blk(peer),
            device_id_type=MESH,
        )

    def send(d, carry):
        for copy in copies(d):
            copy.start()
        return carry

    lax.fori_loop(1, peers, send, 0)
    own = [
        pltpu.make_async_copy(out_ref.at[me], in_ref.at[me], local_sems.at[0]),
        pltpu.make_async_copy(label_ref.at[me], in_label_ref.at[me], local_sems.at[1]),
    ]
    for copy in own:
        copy.start()
    for copy in own:
        copy.wait()

    def finish(d, carry):
        for copy in copies(d):
            copy.wait()
        return carry

    lax.fori_loop(1, peers, finish, 0)


def landing_kernel(peers, label_ref, tiles_ref, vox_ref, total):
    total[...] = jnp.zeros_like(total)

    def land(i, carry):
        source, rank = i // CAP, i % CAP
        quarter = label_ref[source, 0, rank]

        @pl.when(quarter >= 0)
        def _():
            total[quarter] += tiles_ref[source, rank].astype(F32)

        return carry

    lax.fori_loop(0, peers * CAP, land, 0)
    vox_ref[...] = total[...].astype(BF16)


def fill_weights(w_ref, big):
    zero = jnp.zeros((C, C), BF16)
    for u in range(4):
        for dy in range(3):
            for dz in range(3):
                for half in range(2):
                    dx = u - half
                    tap = w_ref[dx * 9 + dy * 3 + dz] if 0 <= dx <= 2 else zero
                    big[u * 3 + dy, dz * C : dz * C + C, half * C : half * C + C] = tap


def fill_shifts(tab_ref, field, shifts):
    level = lax.broadcasted_iota(jnp.int32, (10, 8, C), 1)

    def body(i, carry):
        pair, plane = i // 10, i % 10
        first = jnp.where(plane == 0, 0, jnp.where(plane == 9, 2, 1))
        at = lax.rem(plane + 7, 8)
        parts = []
        for j in range(2):
            base = (2 * pair + j) * 27 + first * 9
            cells = []
            for c in range(3):
                low = field[tab_ref[base + c], at, 48:64].astype(F32)[8:16]
                mid = field[tab_ref[base + 3 + c], at].astype(F32)
                high = field[tab_ref[base + 6 + c], at, 0:16].astype(F32)[0:8]
                cells.append(jnp.concatenate([low, mid, high], axis=0).reshape(10, 8, C))
            parts.append(
                (
                    pltpu.roll(jnp.where(level == 7, cells[0], cells[1]), 1, 1),
                    cells[1],
                    pltpu.roll(jnp.where(level == 0, cells[2], cells[1]), 7, 1),
                )
            )
        for c in range(3):
            both = jnp.concatenate([parts[0][c], parts[1][c]], axis=1).astype(BF16)
            shifts[pair, lax.rem(plane, 2), plane // 2, :, :, c * C : c * C + C] = both
        return carry

    lax.fori_loop(0, 20, body, 0)


def operand(shifts, pair, u, dy):
    return shifts[pair, u % 2, u // 2 : u // 2 + 4, dy : dy + 8].reshape(512, 3 * C)


def convolve(shifts, big, pair):
    total = jnp.zeros((512, 2 * C), F32)
    for u in range(4):
        for dy in range(3):
            total = total + jnp.dot(
                operand(shifts, pair, u, dy), big[u * 3 + dy], preferred_element_type=F32
            )
    return total.reshape(4, 8, 2, 8, 2 * C)


def level_kernel(
    peers,
    reps,
    tab_ref,
    vox_ref,
    wenc_ref,
    wcoarse_ref,
    wdec_ref,
    cot_ref,
    dec_ref,
    grad_ref,
    field,
    field2,
    shifts,
    big,
    big2,
    wdec,
    cot,
    cot_t,
    encoded,
    pooled,
    pooled_in,
    part,
    half_in,
    half,
    whole,
    piece_in,
    piece_own,
    piece_x,
    load_sems,
    halo_send,
    halo_recv,
    sib_send,
    sib_recv,
    core_send,
    core_recv,
    plane_send,
    plane_recv,
    x_send,
    x_recv,
):
    me = lax.axis_index("blk")
    rep = lax.axis_index("rep")
    chips = peers // 2
    core, chip = lax.rem(me, 2), me // 2
    other = me + 1 - 2 * core
    right, left = lax.rem(me + 1, peers), lax.rem(me + peers - 1, peers)
    half_rows = 27 * C // 2
    piece_rows = piece_own.shape[0]

    loads = [
        pltpu.make_async_copy(cot_ref, cot, load_sems.at[0]),
        pltpu.make_async_copy(wdec_ref, wdec, load_sems.at[1]),
    ]
    for load in loads:
        load.start()

    def sibling(step):
        return me // SIB * SIB + lax.rem(me + step, SIB)

    def plane_peer(step):
        return 2 * lax.rem(chip + step, chips) + core

    def rep_peer(step):
        return lax.rem(rep + step, reps)

    barrier = pltpu.get_barrier_semaphore()

    def greet(where):
        pl.semaphore_signal(barrier, inc=1, device_id=where, device_id_type=MESH)

    greet(at_blk(right))
    greet(at_blk(left))
    for step in range(1, SIB):
        greet(at_blk(sibling(step)))
    greet(at_blk(other))

    def greet_plane(step, carry):
        greet(at_blk(plane_peer(step)))
        return carry

    lax.fori_loop(1, chips, greet_plane, 0)
    for step in range(1, reps):
        greet(at_rep(rep_peer(step)))
    pl.semaphore_wait(barrier, 2 + SIB - 1 + 1 + chips - 1 + reps - 1)

    def halo(source, target, at):
        return [
            pltpu.make_async_remote_copy(
                src_ref=source,
                dst_ref=target.at[0:BLK],
                send_sem=halo_send.at[at],
                recv_sem=halo_recv.at[at],
                device_id=at_blk(right),
                device_id_type=MESH,
            ),
            pltpu.make_async_remote_copy(
                src_ref=source,
                dst_ref=target.at[2 * BLK : 3 * BLK],
                send_sem=halo_send.at[at + 1],
                recv_sem=halo_recv.at[at + 1],
                device_id=at_blk(left),
                device_id_type=MESH,
            ),
        ]

    moves = halo(vox_ref, field, 0)
    for move in moves:
        move.start()
    field[BLK : 2 * BLK] = vox_ref[...]
    field[3 * BLK] = jnp.zeros((8, 64, C), BF16)
    field2[3 * BLK] = jnp.zeros((8, 64, C), BF16)
    fill_weights(wenc_ref, big)
    loads[1].wait()
    fill_weights(wdec, big2)
    loads[0].wait()
    for pair in range(2):
        for parity in range(2):
            rows = [
                jnp.concatenate(
                    [
                        cot[2 * pair + j, parity + 2 * xh].astype(F32).reshape(8, 1, 8, C)
                        for j in range(2)
                    ],
                    axis=1,
                ).reshape(128, C)
                for xh in range(4)
            ]
            for xh in range(4):
                cot_t[pair, parity * C : parity * C + C, xh * 128 : xh * 128 + 128] = rows[
                    xh
                ].T.astype(BF16)
    for move in moves:
        move.wait()

    fill_shifts(tab_ref, field, shifts)
    level = lax.broadcasted_iota(jnp.int32, (8, C), 0)
    even = lax.rem(level, 2) == 0

    def encode(pair, carry):
        total = convolve(shifts, big, pair)
        rounded = jnp.maximum(total, 0.0).astype(BF16).astype(F32)
        for j in range(2):
            for xh in range(4):
                for half_x in range(2):
                    encoded[2 * pair + j, 2 * xh + half_x] = (
                        rounded[xh, :, j, :, half_x * C : half_x * C + C]
                        .reshape(64, C)
                        .astype(BF16)
                    )
                flat = rounded[xh, :, j, :, :C] + rounded[xh, :, j, :, C:]
                flat = flat.reshape(4, 2, 8, C)
                flat = flat[:, 0] + flat[:, 1]
                folded = [
                    flat[y]
                    + jnp.where(even, pltpu.roll(flat[y], 7, 0), pltpu.roll(flat[y], 1, 0))
                    for y in range(4)
                ]
                packed = [
                    jnp.where(even, folded[2 * y], folded[2 * y + 1]) * 0.125 for y in range(2)
                ]
                pooled[2 * pair + j, xh] = jnp.concatenate(packed, axis=0).astype(BF16)
        return carry

    lax.fori_loop(0, 2, encode, 0)

    moves = [
        pltpu.make_async_remote_copy(
            src_ref=pooled,
            dst_ref=pooled_in.at[step - 1],
            send_sem=sib_send.at[step - 1],
            recv_sem=sib_recv.at[step - 1],
            device_id=at_blk(sibling(step)),
            device_id_type=MESH,
        )
        for step in range(1, SIB)
    ]
    for move in moves:
        move.start()
    for move in moves:
        move.wait()

    def join(block, carry):
        mean = pooled[block].astype(F32)
        for step in range(SIB - 1):
            mean = mean + pooled_in[step, block].astype(F32)
        mean = (mean * (1.0 / SIB)).astype(BF16).reshape(64, C)
        coarse = jnp.maximum(jnp.dot(mean, wcoarse_ref[...], preferred_element_type=F32), 0.0)
        coarse = coarse.reshape(4, 2, 8, C)
        for xh in range(4):
            ups = []
            for y in range(2):
                tile = coarse[xh, y]
                for up in (
                    jnp.where(even, tile, pltpu.roll(tile, 1, 0)),
                    jnp.where(even, pltpu.roll(tile, 7, 0), tile),
                ):
                    ups += [up, up]
            ups = jnp.concatenate(ups, axis=0)
            for half_x in range(2):
                x = 2 * xh + half_x
                field2[BLK + block, x] = (encoded[block, x].astype(F32) + ups).astype(BF16)
        return carry

    lax.fori_loop(0, BLK, join, 0)

    moves = halo(field2.at[BLK : 2 * BLK], field2, 2)
    for move in moves:
        move.start()
    for move in moves:
        move.wait()
    fill_shifts(tab_ref, field2, shifts)

    def tap_row(dy, carry):
        sums = []
        for u in range(4):
            total = jnp.zeros((2 * C, 3 * C), F32)
            for pair in range(2):
                rows = shifts[pair, u % 2, u // 2 : u // 2 + 4, pl.ds(dy, 8)].reshape(512, 3 * C)
                total = total + jnp.dot(cot_t[pair], rows, preferred_element_type=F32)
            sums.append(total)
        for dx in range(3):
            taps = sums[dx][:C] + sums[dx + 1][C:]
            for dz in range(3):
                tap = taps[:, dz * C : dz * C + C].T.astype(BF16)
                part[pl.ds(pl.multiple_of((dx * 9 + dz) * C + dy * 3 * C, C), C)] = tap
        return carry

    lax.fori_loop(0, 3, tap_row, 0)

    mine = pl.multiple_of(core * half_rows, 16)
    theirs = pl.multiple_of((1 - core) * half_rows, 16)
    swap = pltpu.make_async_remote_copy(
        src_ref=part.at[pl.ds(theirs, half_rows)],
        dst_ref=half_in,
        send_sem=core_send.at[0],
        recv_sem=core_recv.at[0],
        device_id=at_blk(other),
        device_id_type=MESH,
    )
    swap.start()

    def decode(pair):
        total = convolve(shifts, big2, pair)
        for j in range(2):
            for xh in range(4):
                for half_x in range(2):
                    x = 2 * xh + half_x
                    piece = total[xh, :, j, :, half_x * C : half_x * C + C].reshape(64, C)
                    block = 2 * pair + j
                    dec_ref[block, x] = (piece + field2[BLK + block, x].astype(F32)).astype(BF16)

    decode(0)
    swap.wait()
    half[0:half_rows] = (
        part[pl.ds(mine, half_rows)].astype(F32) + half_in[...].astype(F32)
    ).astype(BF16)
    if chips * piece_rows > half_rows:
        half[half_rows:] = jnp.zeros((chips * piece_rows - half_rows, C), BF16)

    def piece_at(index):
        return pl.ds(pl.multiple_of(index * piece_rows, 16), piece_rows)

    def scatter(step):
        return pltpu.make_async_remote_copy(
            src_ref=half.at[piece_at(lax.rem(chip + step, chips))],
            dst_ref=piece_in.at[chip],
            send_sem=plane_send.at[0, step],
            recv_sem=plane_recv.at[0, step],
            device_id=at_blk(plane_peer(step)),
            device_id_type=MESH,
        )

    def gather(step):
        return pltpu.make_async_remote_copy(
            src_ref=piece_own,
            dst_ref=whole.at[piece_at(chip)],
            send_sem=plane_send.at[1, step],
            recv_sem=plane_recv.at[1, step],
            device_id=at_blk(plane_peer(step)),
            device_id_type=MESH,
        )

    def start_all(make):
        def body(step, carry):
            make(step).start()
            return carry

        lax.fori_loop(1, chips, body, 0)

    def wait_all(make):
        def body(step, carry):
            make(step).wait()
            return carry

        lax.fori_loop(1, chips, body, 0)

    start_all(scatter)
    decode(1)
    piece_in[chip] = half[piece_at(chip)]
    wait_all(scatter)

    def add(index, total):
        return total + piece_in[index].astype(F32)

    total = lax.fori_loop(0, chips, add, jnp.zeros((piece_rows, C), F32))
    piece_x[rep] = total.astype(BF16)
    moves = [
        pltpu.make_async_remote_copy(
            src_ref=piece_x.at[rep],
            dst_ref=piece_x.at[rep],
            send_sem=x_send.at[step - 1],
            recv_sem=x_recv.at[step - 1],
            device_id=at_rep(rep_peer(step)),
            device_id_type=MESH,
        )
        for step in range(1, reps)
    ]
    for move in moves:
        move.start()
    for move in moves:
        move.wait()
    total = piece_x[0].astype(F32)
    for index in range(1, reps):
        total = total + piece_x[index].astype(F32)
    piece_own[...] = total.astype(BF16)
    start_all(gather)
    whole[piece_at(chip)] = piece_own[...]
    wait_all(gather)
    swap = pltpu.make_async_remote_copy(
        src_ref=whole.at[0:half_rows],
        dst_ref=grad_ref.at[pl.ds(mine, half_rows)],
        send_sem=core_send.at[1],
        recv_sem=core_recv.at[1],
        device_id=at_blk(other),
        device_id_type=MESH,
    )
    swap.start()
    keep = pltpu.make_async_copy(
        whole.at[0:half_rows], grad_ref.at[pl.ds(mine, half_rows)], load_sems.at[2]
    )
    keep.start()
    keep.wait()
    swap.wait()


def local(
    peers,
    reps,
    tiles,
    tile_rows,
    tile_owner,
    tile_slot,
    neighbors,
    w_enc,
    w_coarse,
    w_dec,
    cotangent,
):
    count = tiles.shape[1]
    smem = pl.BlockSpec(memory_space=pltpu.SMEM)
    vmem = pl.BlockSpec(memory_space=pltpu.VMEM)
    anywhere = pl.BlockSpec(memory_space=pl.ANY)
    outgoing, labels = pl.pallas_call(
        functools.partial(bucket_kernel, count, peers),
        out_shape=(
            jax.ShapeDtypeStruct((peers, CAP, C, C), BF16),
            jax.ShapeDtypeStruct((peers, 1, C), jnp.int32),
        ),
        in_specs=[smem, smem, smem, vmem],
        out_specs=(vmem, smem),
        scratch_shapes=[pltpu.SMEM((peers,), jnp.int32)],
        compiler_params=pltpu.CompilerParams(vmem_limit_bytes=VMEM_LIMIT),
        name="bucket",
    )(tile_owner.reshape(count), tile_rows.reshape(count), tile_slot.reshape(count), tiles[0])
    arrived, arrived_labels = pl.pallas_call(
        functools.partial(exchange_kernel, peers),
        out_shape=(
            jax.ShapeDtypeStruct((peers, CAP, C, C), BF16),
            jax.ShapeDtypeStruct((peers, 1, C), jnp.int32),
        ),
        in_specs=[anywhere, anywhere],
        out_specs=(anywhere, anywhere),
        scratch_shapes=[
            pltpu.SemaphoreType.DMA((4, peers)),
            pltpu.SemaphoreType.DMA((2,)),
        ],
        compiler_params=pltpu.CompilerParams(
            collective_id=0, has_side_effects=True, vmem_limit_bytes=VMEM_LIMIT
        ),
        name="exchange",
    )(outgoing, labels)
    voxels = pl.pallas_call(
        functools.partial(landing_kernel, peers),
        out_shape=jax.ShapeDtypeStruct((4 * BLK, C, C), BF16),
        in_specs=[smem, vmem],
        out_specs=vmem,
        scratch_shapes=[pltpu.VMEM((4 * BLK, C, C), F32)],
        compiler_params=pltpu.CompilerParams(vmem_limit_bytes=VMEM_LIMIT),
        name="landing",
    )(arrived_labels, arrived)

    me = lax.axis_index("blk")
    lookup = neighbors[0]
    beside = lookup // BLK - 1 + me
    table = jnp.where((lookup >= 0) & (beside >= 0) & (beside < peers), lookup, 3 * BLK)
    chips = peers // 2
    half_rows = 27 * C // 2
    piece_rows = -(-half_rows // (16 * chips)) * 16
    dma = pltpu.SemaphoreType.DMA
    decoded, grads = pl.pallas_call(
        functools.partial(level_kernel, peers, reps),
        out_shape=(
            jax.ShapeDtypeStruct((BLK, 8, 64, C), BF16),
            jax.ShapeDtypeStruct((27 * C, C), BF16),
        ),
        in_specs=[smem, vmem, vmem, vmem, anywhere, anywhere],
        out_specs=(vmem, anywhere),
        scratch_shapes=[
            pltpu.VMEM((3 * BLK + 1, 8, 64, C), BF16),
            pltpu.VMEM((3 * BLK + 1, 8, 64, C), BF16),
            pltpu.VMEM((2, 2, 5, 10, 16, 3 * C), BF16),
            pltpu.VMEM((12, 3 * C, 2 * C), BF16),
            pltpu.VMEM((12, 3 * C, 2 * C), BF16),
            pltpu.VMEM((27, C, C), BF16),
            pltpu.VMEM((BLK, 8, 64, C), BF16),
            pltpu.VMEM((2, 2 * C, 512), BF16),
            pltpu.VMEM((BLK, 8, 64, C), BF16),
            pltpu.VMEM((BLK, 4, 16, C), BF16),
            pltpu.VMEM((SIB - 1, BLK, 4, 16, C), BF16),
            pltpu.VMEM((27 * C, C), BF16),
            pltpu.VMEM((half_rows, C), BF16),
            pltpu.VMEM((chips * piece_rows, C), BF16),
            pltpu.VMEM((chips * piece_rows, C), BF16),
            pltpu.VMEM((chips, piece_rows, C), BF16),
            pltpu.VMEM((piece_rows, C), BF16),
            pltpu.VMEM((reps, piece_rows, C), BF16),
            dma((3,)),
            dma((4,)),
            dma((4,)),
            dma((SIB - 1,)),
            dma((SIB - 1,)),
            dma((2,)),
            dma((2,)),
            dma((2, chips)),
            dma((2, chips)),
            dma((reps - 1,)),
            dma((reps - 1,)),
        ],
        compiler_params=pltpu.CompilerParams(
            collective_id=1, has_side_effects=True, vmem_limit_bytes=VMEM_LIMIT
        ),
        name="level",
    )(
        table.reshape(-1),
        voxels.reshape(BLK, 8, 64, C),
        w_enc,
        w_coarse,
        w_dec,
        cotangent[0].reshape(BLK, 8, 64, C),
    )
    return decoded.reshape(1, BLK, 512, C), grads.astype(F32).reshape(27, C, C)


def solution(mesh):
    placed = (
        P("rep", "blk", None, None),
        P("rep", "blk"),
        P("rep", "blk", None),
        P("rep", "blk"),
        P("rep", "blk", None),
        P(),
        P(),
        P(),
        P("rep", "blk", None, None),
    )
    return jax.shard_map(
        functools.partial(local, mesh.shape["blk"], mesh.shape["rep"]),
        mesh=mesh,
        in_specs=placed,
        out_specs=(P("rep", "blk", None, None), P()),
        check_vma=False,
    )
```

```python
import functools
import math

import jax
import jax.numpy as jnp
from jax import lax
from jax.experimental import pallas as pl
from jax.experimental.pallas import tpu as pltpu
from jax.sharding import PartitionSpec as P

C = 128
CAP = 2
BLK = 4
SIB = 4
F32 = jnp.float32
BF16 = jnp.bfloat16
MESH = pl.DeviceIdType.MESH
VMEM_LIMIT = 48 * 1024 * 1024


def at_blk(index):
    return {"blk": index}


def at_rep(index):
    return {"rep": index}


def fill_weights(w_ref, big):
    zero = jnp.zeros((C, C), BF16)
    for u in range(4):
        for dy in range(3):
            for dz in range(3):
                for half in range(2):
                    dx = u - half
                    tap = w_ref[dx * 9 + dy * 3 + dz] if 0 <= dx <= 2 else zero
                    big[u * 3 + dy, dz * C : dz * C + C, half * C : half * C + C] = tap


def fill_shifts(tab_ref, field, shifts):
    level = lax.broadcasted_iota(jnp.int32, (10, 8, C), 1)

    def body(i, carry):
        pair, plane = i // 10, i % 10
        first = jnp.where(plane == 0, 0, jnp.where(plane == 9, 2, 1))
        at = lax.rem(plane + 7, 8)
        parts = []
        for j in range(2):
            base = (2 * pair + j) * 27 + first * 9
            cells = []
            for c in range(3):
                low = field[tab_ref[base + c], at, 48:64].astype(F32)[8:16]
                mid = field[tab_ref[base + 3 + c], at].astype(F32)
                high = field[tab_ref[base + 6 + c], at, 0:16].astype(F32)[0:8]
                cells.append(jnp.concatenate([low, mid, high], axis=0).reshape(10, 8, C))
            parts.append(
                (
                    pltpu.roll(jnp.where(level == 7, cells[0], cells[1]), 1, 1),
                    cells[1],
                    pltpu.roll(jnp.where(level == 0, cells[2], cells[1]), 7, 1),
                )
            )
        for c in range(3):
            both = jnp.concatenate([parts[0][c], parts[1][c]], axis=1).astype(BF16)
            shifts[pair, lax.rem(plane, 2), plane // 2, :, :, c * C : c * C + C] = both
        return carry

    lax.fori_loop(0, 20, body, 0)


def operand(shifts, pair, u, dy):
    return shifts[pair, u % 2, u // 2 : u // 2 + 4, dy : dy + 8].reshape(512, 3 * C)


def convolve(shifts, big, pair):
    total = jnp.zeros((512, 2 * C), F32)
    for u in range(4):
        for dy in range(3):
            total = total + jnp.dot(
                operand(shifts, pair, u, dy), big[u * 3 + dy], preferred_element_type=F32
            )
    return total.reshape(4, 8, 2, 8, 2 * C)


def kernel(
    count,
    peers,
    reps,
    rows_hbm,
    owner_hbm,
    slot_hbm,
    neighbors_hbm,
    tiles_hbm,
    wenc_hbm,
    wcoarse_ref,
    wdec_hbm,
    cot_hbm,
    dec_ref,
    grad_ref,
    rows_s,
    owner_s,
    slot_s,
    neighbors_s,
    table_s,
    places_v,
    places_s,
    tiles,
    outgoing,
    outgoing_label,
    arrived,
    arrived_label,
    landed,
    field,
    encoded,
    shifts,
    big,
    big2,
    wenc,
    wdec,
    cot,
    cot_t,
    pooled,
    pooled_in,
    means,
    part,
    half_in,
    half,
    piece_in,
    piece_x,
    piece_own,
    load_sems,
    tile_sems,
    label_sems,
    halo_sems,
    encoded_sems,
    sibling_sems,
    mean_sems,
    core_sems,
    plane_sems,
    x_sems,
    gather_sems,
    forward_sems,
):
    me = lax.axis_index("blk")
    rep = lax.axis_index("rep")
    chips = peers // 2
    side = math.isqrt(chips)
    core, chip = lax.rem(me, 2), me // 2
    chip_y, chip_z = lax.rem(chip, side), chip // side
    other = me + 1 - 2 * core
    right, left = lax.rem(me + 1, peers), lax.rem(me + peers - 1, peers)

    loads = [
        pltpu.make_async_copy(source, target, load_sems.at[i])
        for i, (source, target) in enumerate(
            [
                (owner_hbm, owner_s),
                (rows_hbm, rows_s),
                (slot_hbm, slot_s),
                (tiles_hbm, tiles),
                (neighbors_hbm, neighbors_s),
                (wenc_hbm, wenc),
                (wdec_hbm, wdec),
                (cot_hbm, cot),
            ]
        )
    ]
    for load in loads:
        load.start()

    def remote(source, target, sems, at, where):
        return pltpu.make_async_remote_copy(
            src_ref=source,
            dst_ref=target,
            send_sem=sems.at[(0, *at)],
            recv_sem=sems.at[(1, *at)],
            device_id=where,
            device_id_type=MESH,
        )

    def sibling(step):
        return me // SIB * SIB + lax.rem(me + step, SIB)

    def plane_peer(step):
        return 2 * lax.rem(chip + step, chips) + core

    def rep_peer(step):
        return lax.rem(rep + step, reps)

    barrier = pltpu.get_barrier_semaphore()

    def greet(step, carry):
        pl.semaphore_signal(
            barrier, inc=1, device_id=at_blk(lax.rem(me + step, peers)), device_id_type=MESH
        )
        return carry

    lax.fori_loop(1, peers, greet, 0)
    for step in range(1, reps):
        pl.semaphore_signal(
            barrier, inc=1, device_id=at_rep(rep_peer(step)), device_id_type=MESH
        )

    loads[0].wait()
    lane = lax.broadcasted_iota(jnp.int32, (8, C), 1)

    def note(t, carry):
        first, second = carry
        hit = lane == owner_s[0, t]
        second = jnp.where(hit & (first >= 0), t, second)
        first = jnp.where(hit & (first < 0), t, first)
        return first, second

    none = jnp.full((8, C), -1, jnp.int32)
    first, second = lax.fori_loop(0, count, note, (none, none))
    places_v[...] = jnp.where(lax.broadcasted_iota(jnp.int32, (8, C), 0) == 0, first, second)
    move = pltpu.make_async_copy(places_v, places_s, load_sems.at[8])
    move.start()
    loads[1].wait()
    loads[2].wait()
    move.wait()
    loads[3].wait()
    row = lax.broadcasted_iota(jnp.int32, (C, C), 0)

    def bucket(owner):
        for rank in range(CAP):
            tile = places_s[rank, owner]
            at = jnp.maximum(tile, 0)
            live = jnp.where(tile >= 0, rows_s[0, at], 0)
            outgoing[owner, rank] = jnp.where(row < live, tiles[at].astype(F32), 0.0).astype(BF16)
            outgoing_label[owner, rank : rank + 1] = jnp.full((1, C), slot_s[0, at], jnp.int32)

    def chip_beside(step, sign):
        k = step // 2
        move_y = lax.rem(k, side)
        move_z = lax.rem(k // side + move_y, side)
        return side * lax.rem(chip_z + side + sign * move_z, side) + lax.rem(
            chip_y + side + sign * move_y, side
        )

    def target_of(step):
        return 2 * chip_beside(step, 1 - 2 * core) + lax.rem(core + step, 2)

    def source_of(step):
        from_core = lax.rem(core + step, 2)
        return 2 * chip_beside(step, 2 * from_core - 1) + from_core

    def label_move(step):
        peer = target_of(step)
        return remote(
            outgoing_label.at[peer], arrived_label.at[me], label_sems, (step,), at_blk(peer)
        )

    def tile_move(step):
        peer = target_of(step)
        return remote(outgoing.at[peer], arrived.at[me], tile_sems, (step,), at_blk(peer))

    pl.semaphore_wait(barrier, peers - 1 + reps - 1)

    def send(step, carry):
        bucket(target_of(step))
        label_move(step).start()
        tile_move(step).start()
        return carry

    lax.fori_loop(2, peers, send, 0)
    lax.fori_loop(1, 2, send, 0)
    bucket(me)

    landed[...] = jnp.zeros_like(landed)

    def land(labels, tiles_at):
        rows = [labels[rank : rank + 1] for rank in range(CAP)]
        for at in range(0, C, 32):
            pieces = [tiles_at[rank, at : at + 32].astype(F32) for rank in range(CAP)]
            for quarter in range(4 * BLK):
                total = landed[quarter, at : at + 32]
                for rank in range(CAP):
                    total = total + jnp.where(rows[rank] == quarter, pieces[rank], 0.0)
                landed[quarter, at : at + 32] = total

    land(outgoing_label[me], outgoing.at[me])
    loads[4].wait()

    def look(block, carry):
        for column in range(27):
            entry = neighbors_s[block, column]
            beside = me + entry // BLK - 1
            keep = (entry >= 0) & (beside >= 0) & (beside < peers)
            table_s[block * 27 + column] = jnp.where(keep, entry, 3 * BLK)
        return carry

    lax.fori_loop(0, BLK, look, 0)
    field[3 * BLK] = jnp.zeros((8, 64, C), BF16)
    loads[5].wait()
    fill_weights(wenc, big)
    loads[6].wait()
    fill_weights(wdec, big2)
    loads[7].wait()
    for pair in range(2):
        for parity in range(2):
            for xh in range(4):
                rows = [
                    cot[2 * pair + j, parity + 2 * xh].astype(F32).reshape(8, 1, 8, C)
                    for j in range(2)
                ]
                rows = jnp.concatenate(rows, axis=1).reshape(128, C)
                cot_t[pair, parity * C : parity * C + C, xh * 128 : xh * 128 + 128] = rows.T.astype(
                    BF16
                )

    def arrive(step, carry):
        source = source_of(step)
        label_move(step).wait_send()
        tile_move(step).wait_send()
        remote(
            outgoing_label.at[me], arrived_label.at[source], label_sems, (step,), at_blk(source)
        ).wait_recv()
        remote(outgoing.at[me], arrived.at[source], tile_sems, (step,), at_blk(source)).wait_recv()
        land(arrived_label[source], arrived.at[source])
        return carry

    lax.fori_loop(1, 2, arrive, 0)
    lax.fori_loop(2, peers, arrive, 0)
    for quarter in range(4 * BLK):
        planes = landed[quarter].astype(BF16).reshape(2, 64, C)
        x = 2 * (quarter % 4)
        field[BLK + quarter // 4, x : x + 2] = planes

    own = field.at[BLK : 2 * BLK]
    moves = [
        remote(own, field.at[0:BLK], halo_sems, (0,), at_blk(right)),
        remote(own, field.at[2 * BLK : 3 * BLK], halo_sems, (1,), at_blk(left)),
    ]
    for move in moves:
        move.start()
    for move in moves:
        move.wait()

    fill_shifts(table_s, field, shifts)
    level = lax.broadcasted_iota(jnp.int32, (8, C), 0)
    even = lax.rem(level, 2) == 0

    def sibling_moves(pair):
        at = pl.ds(2 * pair, 2)
        return [
            remote(
                pooled.at[at],
                pooled_in.at[step - 1, at],
                sibling_sems,
                (pair, step - 1),
                at_blk(sibling(step)),
            )
            for step in range(1, SIB)
        ]

    def halo_moves(pair):
        at = pl.ds(2 * pair, 2)
        source = encoded.at[pl.ds(BLK + 2 * pair, 2)]
        return [
            remote(source, encoded.at[at], encoded_sems, (pair, 0), at_blk(right)),
            remote(
                source,
                encoded.at[pl.ds(2 * BLK + 2 * pair, 2)],
                encoded_sems,
                (pair, 1),
                at_blk(left),
            ),
        ]

    def encode(pair, carry):
        total = convolve(shifts, big, pair)
        rounded = jnp.maximum(total, 0.0).astype(BF16).astype(F32)
        for j in range(2):
            for xh in range(4):
                for half_x in range(2):
                    encoded[BLK + 2 * pair + j, 2 * xh + half_x] = (
                        rounded[xh, :, j, :, half_x * C : half_x * C + C]
                        .reshape(64, C)
                        .astype(BF16)
                    )
                flat = rounded[xh, :, j, :, :C] + rounded[xh, :, j, :, C:]
                flat = flat.reshape(4, 2, 8, C)
                flat = flat[:, 0] + flat[:, 1]
                folded = [
                    flat[y]
                    + jnp.where(even, pltpu.roll(flat[y], 7, 0), pltpu.roll(flat[y], 1, 0))
                    for y in range(4)
                ]
                packed = [
                    jnp.where(even, folded[2 * y], folded[2 * y + 1]) * 0.125 for y in range(2)
                ]
                pooled[2 * pair + j, xh] = jnp.concatenate(packed, axis=0).astype(BF16)
        for move in sibling_moves(pair) + halo_moves(pair):
            move.start()
        return carry

    lax.fori_loop(0, 2, encode, 0)

    for pair in range(2):
        for move in sibling_moves(pair):
            move.wait()
    mean = pooled[...].astype(F32)
    for step in range(SIB - 1):
        mean = mean + pooled_in[step].astype(F32)
    means[1] = (mean * (1.0 / SIB)).astype(BF16)
    mean_moves = [
        remote(means.at[1], means.at[0], mean_sems, (0,), at_blk(right)),
        remote(means.at[1], means.at[2], mean_sems, (1,), at_blk(left)),
    ]
    for move in mean_moves:
        move.start()

    def join(side_of):
        coarse = jnp.dot(
            means[side_of].reshape(BLK * 64, C), wcoarse_ref[...], preferred_element_type=F32
        )
        coarse = jnp.maximum(coarse, 0.0).reshape(BLK, 4, 2, 8, C)
        for block in range(BLK):
            for xh in range(4):
                ups = []
                for y in range(2):
                    tile = coarse[block, xh, y]
                    for up in (
                        jnp.where(even, tile, pltpu.roll(tile, 1, 0)),
                        jnp.where(even, pltpu.roll(tile, 7, 0), tile),
                    ):
                        ups += [up, up]
                ups = jnp.concatenate(ups, axis=0)
                for half_x in range(2):
                    x = 2 * xh + half_x
                    at = BLK * side_of + block
                    field[at, x] = (encoded[at, x].astype(F32) + ups).astype(BF16)

    join(1)
    for move in mean_moves:
        move.wait()
    for pair in range(2):
        for move in halo_moves(pair):
            move.wait()
    join(0)
    join(2)
    fill_shifts(table_s, field, shifts)

    group_half = half_in.shape[1]
    piece_rows = piece_own.shape[1]
    active = group_half // piece_rows

    def swap(group):
        return remote(
            part.at[group, pl.ds(pl.multiple_of((1 - core) * group_half, 16), group_half)],
            half_in.at[group],
            core_sems,
            (group,),
            at_blk(other),
        )

    def piece_at(index):
        return pl.ds(pl.multiple_of(index * piece_rows, 16), piece_rows)

    def final_at(group, side_of, index):
        start = side_of * group_half + index * piece_rows
        start = start // (3 * C) * (9 * C) + group * (3 * C) + lax.rem(start, 3 * C)
        return pl.ds(pl.multiple_of(start, 16), piece_rows)

    def to_chip(step):
        return lax.rem(chip + step, chips)

    def from_chip(step):
        return lax.rem(chip + chips - step, chips)

    def scatter(group, step):
        return remote(
            half.at[group, piece_at(to_chip(step))],
            piece_in.at[group, chip],
            plane_sems,
            (group, step),
            at_blk(plane_peer(step)),
        )

    def scattered(group, step):
        return remote(
            half.at[group, piece_at(0)],
            piece_in.at[group, from_chip(step)],
            plane_sems,
            (group, step),
            at_blk(2 * from_chip(step) + core),
        )

    def gather(group, step):
        return remote(
            piece_own.at[group],
            grad_ref.at[final_at(group, core, chip)],
            gather_sems,
            (group, step),
            at_blk(plane_peer(step)),
        )

    def gathered(group, step):
        return remote(
            piece_own.at[group],
            grad_ref.at[final_at(group, core, from_chip(step))],
            gather_sems,
            (group, step),
            at_blk(2 * from_chip(step) + core),
        )

    def forward(group, index):
        at = final_at(group, core, index)
        return remote(
            grad_ref.at[at], grad_ref.at[at], forward_sems, (group, index), at_blk(other)
        )

    def forwarded(group, index):
        at = final_at(group, 1 - core, index)
        return remote(
            grad_ref.at[at], grad_ref.at[at], forward_sems, (group, index), at_blk(other)
        )

    def each_step(action):
        def body(step, carry):
            action(step)
            return carry

        lax.fori_loop(1, chips, body, 0)

    def halve(group):
        swap(group).wait()
        mine = pl.ds(pl.multiple_of(core * group_half, 16), group_half)
        half[group] = (part[group, mine].astype(F32) + half_in[group].astype(F32)).astype(BF16)

        def start(step):
            @pl.when(to_chip(step) < active)
            def _():
                scatter(group, step).start()

        each_step(start)

    def tap_row(dy, carry):
        @pl.when(dy < 3)
        def _():
            sums = []
            for u in range(4):
                total = jnp.zeros((2 * C, 3 * C), F32)
                for pair in range(2):
                    rows = shifts[pair, u % 2, u // 2 : u // 2 + 4, pl.ds(dy, 8)]
                    total = total + jnp.dot(
                        cot_t[pair], rows.reshape(512, 3 * C), preferred_element_type=F32
                    )
                sums.append(total)
            for dx in range(3):
                taps = sums[dx][:C] + sums[dx + 1][C:]
                for dz in range(3):
                    at = (dx * 3 + dz) * C
                    part[dy, at : at + C] = taps[:, dz * C : dz * C + C].T.astype(BF16)
            swap(dy).start()

        @pl.when(dy > 0)
        def _():
            halve(dy - 1)

        return carry

    lax.fori_loop(0, 4, tap_row, 0)

    def decode(pair):
        total = convolve(shifts, big2, pair)
        for j in range(2):
            for xh in range(4):
                for half_x in range(2):
                    x = 2 * xh + half_x
                    piece = total[xh, :, j, :, half_x * C : half_x * C + C].reshape(64, C)
                    block = 2 * pair + j
                    dec_ref[block, x] = (piece + field[BLK + block, x].astype(F32)).astype(BF16)

    def x_moves(group):
        return [
            remote(
                piece_x.at[group, rep],
                piece_x.at[group, rep],
                x_sems,
                (group, step - 1),
                at_rep(rep_peer(step)),
            )
            for step in range(1, reps)
        ]

    def reduce_piece(group, carry):
        def sent(step):
            @pl.when(to_chip(step) < active)
            def _():
                scatter(group, step).wait_send()

        each_step(sent)

        @pl.when(chip < active)
        def _():
            def come(step):
                scattered(group, step).wait_recv()

            each_step(come)
            piece_in[group, chip] = half[group, piece_at(chip)]

            def add(index, total):
                return total + piece_in[group, index].astype(F32)

            total = lax.fori_loop(0, chips, add, jnp.zeros((piece_rows, C), F32))
            piece_x[group, rep] = total.astype(BF16)
            for move in x_moves(group):
                move.start()

        return carry

    def spread_piece(group, carry):
        @pl.when(chip < active)
        def _():
            for move in x_moves(group):
                move.wait()
            total = piece_x[group, 0].astype(F32)
            for index in range(1, reps):
                total = total + piece_x[group, index].astype(F32)
            piece_own[group] = total.astype(BF16)

            def start(step):
                gather(group, step).start()

            each_step(start)
            keep = pltpu.make_async_copy(
                piece_own.at[group], grad_ref.at[final_at(group, core, chip)], load_sems.at[9]
            )
            keep.start()
            keep.wait()
            forward(group, chip).start()

        return carry

    def forward_pieces(group, carry):
        def come(step):
            @pl.when(from_chip(step) < active)
            def _():
                gathered(group, step).wait_recv()
                forward(group, from_chip(step)).start()

        each_step(come)
        return carry

    def finish(group, carry):
        @pl.when(chip < active)
        def _():
            def sent(step):
                gather(group, step).wait_send()

            each_step(sent)

        def body(index, inner):
            forward(group, index).wait_send()
            forwarded(group, index).wait_recv()
            return inner

        lax.fori_loop(0, active, body, 0)
        return carry

    decode(0)
    decode(1)
    for stage in (reduce_piece, spread_piece, forward_pieces, finish):
        lax.fori_loop(0, 3, stage, 0)


def local(
    peers,
    reps,
    tiles,
    tile_rows,
    tile_owner,
    tile_slot,
    neighbors,
    w_enc,
    w_coarse,
    w_dec,
    cotangent,
):
    count = tiles.shape[1]
    chips = peers // 2
    group_half = 9 * C // 2
    piece_rows = min(
        rows for rows in (16, 48, 64, 192, 576) if rows * chips >= group_half
    )
    vmem = pl.BlockSpec(memory_space=pltpu.VMEM)
    anywhere = pl.BlockSpec(memory_space=pl.ANY)
    dma = pltpu.SemaphoreType.DMA
    decoded, grads = pl.pallas_call(
        functools.partial(kernel, count, peers, reps),
        out_shape=(
            jax.ShapeDtypeStruct((BLK, 8, 64, C), BF16),
            jax.ShapeDtypeStruct((27 * C, C), BF16),
        ),
        in_specs=[anywhere] * 6 + [vmem] + [anywhere] * 2,
        out_specs=(vmem, anywhere),
        scratch_shapes=[
            pltpu.SMEM((1, count), jnp.int32),
            pltpu.SMEM((1, count), jnp.int32),
            pltpu.SMEM((1, count), jnp.int32),
            pltpu.SMEM((BLK, 27), jnp.int32),
            pltpu.SMEM((BLK * 27,), jnp.int32),
            pltpu.VMEM((8, C), jnp.int32),
            pltpu.SMEM((8, C), jnp.int32),
            pltpu.VMEM((count, C, C), BF16),
            pltpu.VMEM((peers, CAP, C, C), BF16),
            pltpu.VMEM((peers, CAP, C), jnp.int32),
            pltpu.VMEM((peers, CAP, C, C), BF16),
            pltpu.VMEM((peers, CAP, C), jnp.int32),
            pltpu.VMEM((4 * BLK, C, C), F32),
            pltpu.VMEM((3 * BLK + 1, 8, 64, C), BF16),
            pltpu.VMEM((3 * BLK, 8, 64, C), BF16),
            pltpu.VMEM((2, 2, 5, 10, 16, 3 * C), BF16),
            pltpu.VMEM((12, 3 * C, 2 * C), BF16),
            pltpu.VMEM((12, 3 * C, 2 * C), BF16),
            pltpu.VMEM((27, C, C), BF16),
            pltpu.VMEM((27, C, C), BF16),
            pltpu.VMEM((BLK, 8, 64, C), BF16),
            pltpu.VMEM((2, 2 * C, 512), BF16),
            pltpu.VMEM((BLK, 4, 16, C), BF16),
            pltpu.VMEM((SIB - 1, BLK, 4, 16, C), BF16),
            pltpu.VMEM((3, BLK, 4, 16, C), BF16),
            pltpu.VMEM((3, 9 * C, C), BF16),
            pltpu.VMEM((3, group_half, C), BF16),
            pltpu.VMEM((3, group_half, C), BF16),
            pltpu.VMEM((3, chips, piece_rows, C), BF16),
            pltpu.VMEM((3, reps, piece_rows, C), BF16),
            pltpu.VMEM((3, piece_rows, C), BF16),
            dma((10,)),
            dma((2, peers)),
            dma((2, peers)),
            dma((2, 2)),
            dma((2, 2, 2)),
            dma((2, 2, SIB - 1)),
            dma((2, 2)),
            dma((2, 3)),
            dma((2, 3, chips)),
            dma((2, 3, reps - 1)),
            dma((2, 3, chips)),
            dma((2, 3, chips)),
        ],
        compiler_params=pltpu.CompilerParams(
            collective_id=0, has_side_effects=True, vmem_limit_bytes=VMEM_LIMIT
        ),
        name="level",
    )(
        tile_rows,
        tile_owner.reshape(1, count),
        tile_slot,
        neighbors[0],
        tiles[0],
        w_enc,
        w_coarse,
        w_dec,
        cotangent[0].reshape(BLK, 8, 64, C),
    )
    return decoded.reshape(1, BLK, 512, C), grads.astype(F32).reshape(27, C, C)


def solution(mesh):
    placed = (
        P("rep", "blk", None, None),
        P("rep", "blk"),
        P("rep", "blk", None),
        P("rep", "blk"),
        P("rep", "blk", None),
        P(),
        P(),
        P(),
        P("rep", "blk", None, None),
    )
    return jax.shard_map(
        functools.partial(local, mesh.shape["blk"], mesh.shape["rep"]),
        mesh=mesh,
        in_specs=placed,
        out_specs=(P("rep", "blk", None, None), P()),
        check_vma=False,
    )
```

```python
import functools
import math

import jax
import jax.numpy as jnp
from jax import lax
from jax.experimental import pallas as pl
from jax.experimental.pallas import tpu as pltpu
from jax.sharding import PartitionSpec as P

C = 128
CAP = 2
BLK = 4
SIB = 4
F32 = jnp.float32
BF16 = jnp.bfloat16
MESH = pl.DeviceIdType.MESH
VMEM_LIMIT = 48 * 1024 * 1024


def at_blk(index):
    return {"blk": index}


def at_rep(index):
    return {"rep": index}


def fill_weights(w_ref, big):
    zero = jnp.zeros((C, C), BF16)
    for u in range(4):
        for dy in range(3):
            for dz in range(3):
                for half in range(2):
                    dx = u - half
                    tap = w_ref[dx * 9 + dy * 3 + dz] if 0 <= dx <= 2 else zero
                    big[u * 3 + dy, dz * C : dz * C + C, half * C : half * C + C] = tap


def fill_shifts(tab_ref, field, shifts):
    level = lax.broadcasted_iota(jnp.int32, (10, 8, C), 1)

    def body(i, carry):
        pair, plane = i // 10, i % 10
        first = jnp.where(plane == 0, 0, jnp.where(plane == 9, 2, 1))
        at = lax.rem(plane + 7, 8)
        parts = []
        for j in range(2):
            base = (2 * pair + j) * 27 + first * 9
            cells = []
            for c in range(3):
                low = field[tab_ref[base + c], at, 48:64].astype(F32)[8:16]
                mid = field[tab_ref[base + 3 + c], at].astype(F32)
                high = field[tab_ref[base + 6 + c], at, 0:16].astype(F32)[0:8]
                cells.append(jnp.concatenate([low, mid, high], axis=0).reshape(10, 8, C))
            parts.append(
                (
                    pltpu.roll(jnp.where(level == 7, cells[0], cells[1]), 1, 1),
                    cells[1],
                    pltpu.roll(jnp.where(level == 0, cells[2], cells[1]), 7, 1),
                )
            )
        for c in range(3):
            both = jnp.concatenate([parts[0][c], parts[1][c]], axis=1).astype(BF16)
            shifts[pair, lax.rem(plane, 2), plane // 2, :, :, c * C : c * C + C] = both
        return carry

    lax.fori_loop(0, 20, body, 0)


def operand(shifts, pair, u, dy):
    return shifts[pair, u % 2, u // 2 : u // 2 + 4, dy : dy + 8].reshape(512, 3 * C)


def convolve(shifts, big, pair):
    total = jnp.zeros((512, 2 * C), F32)
    for u in range(4):
        for dy in range(3):
            total = total + jnp.dot(
                operand(shifts, pair, u, dy), big[u * 3 + dy], preferred_element_type=F32
            )
    return total.reshape(4, 8, 2, 8, 2 * C)


def kernel(
    count,
    peers,
    reps,
    rows_hbm,
    owner_hbm,
    slot_hbm,
    neighbors_hbm,
    tiles_hbm,
    wenc_hbm,
    wcoarse_ref,
    wdec_hbm,
    cot_hbm,
    dec_ref,
    grad_ref,
    rows_s,
    owner_s,
    slot_s,
    neighbors_s,
    table_s,
    places_v,
    places_s,
    tiles,
    outgoing,
    outgoing_label,
    arrived,
    arrived_label,
    landed,
    field,
    encoded,
    shifts,
    big,
    big2,
    wenc,
    wdec,
    cot,
    cot_t,
    pooled,
    means,
    part,
    half_in,
    half,
    piece_in,
    piece_x,
    piece_own,
    load_sems,
    tile_sems,
    label_sems,
    halo_sems,
    encoded_sems,
    sibling_sems,
    mean_sems,
    core_sems,
    plane_sems,
    x_sems,
    gather_sems,
    forward_sems,
):
    me = lax.axis_index("blk")
    rep = lax.axis_index("rep")
    chips = peers // 2
    side = math.isqrt(chips)
    core, chip = lax.rem(me, 2), me // 2
    chip_y, chip_z = lax.rem(chip, side), chip // side
    other = me + 1 - 2 * core
    right, left = lax.rem(me + 1, peers), lax.rem(me + peers - 1, peers)

    loads = [
        pltpu.make_async_copy(source, target, load_sems.at[i])
        for i, (source, target) in enumerate(
            [
                (owner_hbm, owner_s),
                (rows_hbm, rows_s),
                (slot_hbm, slot_s),
                (tiles_hbm, tiles),
                (neighbors_hbm, neighbors_s),
                (wenc_hbm, wenc),
                (wdec_hbm, wdec),
                (cot_hbm, cot),
            ]
        )
    ]
    for load in loads:
        load.start()

    def remote(source, target, send_sem, recv_sem, where):
        return pltpu.make_async_remote_copy(
            src_ref=source,
            dst_ref=target,
            send_sem=send_sem,
            recv_sem=recv_sem,
            device_id=where,
            device_id_type=MESH,
        )

    def drain(ref, sem):
        pltpu.make_async_copy(ref, ref, sem).wait()

    turn = lax.rem(me, SIB)
    across = me - turn + lax.rem(turn + 2, SIB)

    def plane_peer(step):
        return 2 * lax.rem(chip + step, chips) + core

    def rep_peer(step):
        return lax.rem(rep + step, reps)

    barrier = pltpu.get_barrier_semaphore()

    def greet(step, carry):
        pl.semaphore_signal(
            barrier, inc=1, device_id=at_blk(lax.rem(me + step, peers)), device_id_type=MESH
        )
        return carry

    lax.fori_loop(1, peers, greet, 0)
    for step in range(1, reps):
        pl.semaphore_signal(
            barrier, inc=1, device_id=at_rep(rep_peer(step)), device_id_type=MESH
        )

    loads[0].wait()
    lane = lax.broadcasted_iota(jnp.int32, (8, C), 1)

    def note(t, carry):
        first, second = carry
        hit = lane == owner_s[0, t]
        second = jnp.where(hit & (first >= 0), t, second)
        first = jnp.where(hit & (first < 0), t, first)
        return first, second

    none = jnp.full((8, C), -1, jnp.int32)
    first, second = lax.fori_loop(0, count, note, (none, none))
    places_v[...] = jnp.where(lax.broadcasted_iota(jnp.int32, (8, C), 0) == 0, first, second)
    move = pltpu.make_async_copy(places_v, places_s, load_sems.at[8])
    move.start()
    loads[1].wait()
    loads[2].wait()
    move.wait()
    loads[3].wait()
    row = lax.broadcasted_iota(jnp.int32, (C, C), 0)

    def bucket(owner):
        for rank in range(CAP):
            tile = places_s[rank, owner]
            at = jnp.maximum(tile, 0)
            live = jnp.where(tile >= 0, rows_s[0, at], 0)
            outgoing[owner, rank] = jnp.where(row < live, tiles[at].astype(F32), 0.0).astype(BF16)
            outgoing_label[owner, rank : rank + 1] = jnp.full((1, C), slot_s[0, at], jnp.int32)

    def chip_beside(step, sign):
        k = step // 2
        move_y = lax.rem(k, side)
        move_z = lax.rem(k // side + move_y, side)
        return side * lax.rem(chip_z + side + sign * move_z, side) + lax.rem(
            chip_y + side + sign * move_y, side
        )

    def target_of(step):
        return 2 * chip_beside(step, 1 - 2 * core) + lax.rem(core + step, 2)

    def source_of(step):
        from_core = lax.rem(core + step, 2)
        return 2 * chip_beside(step, 2 * from_core - 1) + from_core

    def label_move(step):
        peer = target_of(step)
        return remote(
            outgoing_label.at[peer],
            arrived_label.at[me],
            label_sems.at[0],
            label_sems.at[1],
            at_blk(peer),
        )

    def tile_move(step):
        peer = target_of(step)
        return remote(
            outgoing.at[peer], arrived.at[me], tile_sems.at[0], tile_sems.at[step], at_blk(peer)
        )

    pl.semaphore_wait(barrier, peers - 1 + reps - 1)

    def send(step, carry):
        bucket(target_of(step))
        label_move(step).start()
        tile_move(step).start()
        return carry

    lax.fori_loop(2, peers, send, 0)
    lax.fori_loop(1, 2, send, 0)
    bucket(me)

    landed[...] = jnp.zeros_like(landed)

    def land(labels, tiles_at):
        rows = [labels[rank : rank + 1] for rank in range(CAP)]
        for at in range(0, C, 32):
            pieces = [tiles_at[rank, at : at + 32].astype(F32) for rank in range(CAP)]
            for quarter in range(4 * BLK):
                total = landed[quarter, at : at + 32]
                for rank in range(CAP):
                    total = total + jnp.where(rows[rank] == quarter, pieces[rank], 0.0)
                landed[quarter, at : at + 32] = total

    land(outgoing_label[me], outgoing.at[me])
    loads[4].wait()

    def look(block, carry):
        for column in range(27):
            entry = neighbors_s[block, column]
            beside = me + entry // BLK - 1
            keep = (entry >= 0) & (beside >= 0) & (beside < peers)
            table_s[block * 27 + column] = jnp.where(keep, entry, 3 * BLK)
        return carry

    lax.fori_loop(0, BLK, look, 0)
    field[3 * BLK] = jnp.zeros((8, 64, C), BF16)
    loads[5].wait()
    fill_weights(wenc, big)
    loads[6].wait()
    fill_weights(wdec, big2)
    loads[7].wait()
    for pair in range(2):
        for parity in range(2):
            for xh in range(4):
                rows = [
                    cot[2 * pair + j, parity + 2 * xh].astype(F32).reshape(8, 1, 8, C)
                    for j in range(2)
                ]
                rows = jnp.concatenate(rows, axis=1).reshape(128, C)
                cot_t[pair, parity * C : parity * C + C, xh * 128 : xh * 128 + 128] = rows.T.astype(
                    BF16
                )

    def arrive(step, carry):
        source = source_of(step)
        drain(arrived.at[source], tile_sems.at[step])
        land(arrived_label[source], arrived.at[source])
        return carry

    drain(arrived_label.at[0 : peers - 1], label_sems.at[1])
    lax.fori_loop(1, 2, arrive, 0)
    lax.fori_loop(2, peers, arrive, 0)
    for quarter in range(4 * BLK):
        planes = landed[quarter].astype(BF16).reshape(2, 64, C)
        x = 2 * (quarter % 4)
        field[BLK + quarter // 4, x : x + 2] = planes

    own = field.at[BLK : 2 * BLK]
    for target, where in ((field.at[0:BLK], right), (field.at[2 * BLK : 3 * BLK], left)):
        remote(own, target, halo_sems.at[0], halo_sems.at[1], at_blk(where)).start()
    drain(field.at[0 : 2 * BLK], halo_sems.at[1])
    drain(field.at[0 : 2 * BLK], halo_sems.at[0])

    fill_shifts(table_s, field, shifts)
    level = lax.broadcasted_iota(jnp.int32, (8, C), 0)
    even = lax.rem(level, 2) == 0

    def sibling_move(pair, where, kind):
        piece = pooled.at[turn, pl.ds(2 * pair, 2)]
        return remote(
            piece, piece, sibling_sems.at[0], sibling_sems.at[1 + kind], at_blk(where)
        )

    def halo_moves(pair):
        source = encoded.at[pl.ds(BLK + 2 * pair, 2)]
        return [
            remote(
                source,
                encoded.at[pl.ds(first + 2 * pair, 2)],
                encoded_sems.at[0],
                encoded_sems.at[1],
                at_blk(where),
            )
            for first, where in ((0, right), (2 * BLK, left))
        ]

    def encode(pair, carry):
        total = convolve(shifts, big, pair)
        rounded = jnp.maximum(total, 0.0).astype(BF16).astype(F32)
        for j in range(2):
            for xh in range(4):
                for half_x in range(2):
                    encoded[BLK + 2 * pair + j, 2 * xh + half_x] = (
                        rounded[xh, :, j, :, half_x * C : half_x * C + C]
                        .reshape(64, C)
                        .astype(BF16)
                    )
                flat = rounded[xh, :, j, :, :C] + rounded[xh, :, j, :, C:]
                flat = flat.reshape(4, 2, 8, C)
                flat = flat[:, 0] + flat[:, 1]
                folded = [
                    flat[y]
                    + jnp.where(even, pltpu.roll(flat[y], 7, 0), pltpu.roll(flat[y], 1, 0))
                    for y in range(4)
                ]
                packed = [
                    jnp.where(even, folded[2 * y], folded[2 * y + 1]) * 0.125 for y in range(2)
                ]
                pooled[turn, 2 * pair + j, xh] = jnp.concatenate(packed, axis=0).astype(BF16)
        sibling_move(pair, across, pair).start()
        sibling_move(pair, other, 2).start()
        for move in halo_moves(pair):
            move.start()
        return carry

    lax.fori_loop(0, 2, encode, 0)

    opposite = lax.rem(turn + 2, SIB)
    for pair in range(2):
        piece = pooled.at[opposite, 2 * pair : 2 * pair + 2]
        drain(piece, sibling_sems.at[1 + pair])
        remote(piece, piece, sibling_sems.at[0], sibling_sems.at[4], at_blk(other)).start()
    drain(pooled.at[0], sibling_sems.at[3])
    drain(pooled.at[0], sibling_sems.at[4])
    mean = pooled[0].astype(F32)
    for step in range(1, SIB):
        mean = mean + pooled[step].astype(F32)
    means[1] = (mean * (1.0 / SIB)).astype(BF16)

    def mean_move(side_of, where):
        return remote(
            means.at[1], means.at[side_of], mean_sems.at[0], mean_sems.at[1], at_blk(where)
        )

    @pl.when(turn == SIB - 1)
    def _():
        mean_move(0, right).start()
        means[0] = means[1]

    @pl.when(turn == 0)
    def _():
        mean_move(2, left).start()
        means[2] = means[1]

    @pl.when((turn != 0) & (turn != SIB - 1))
    def _():
        means[0] = means[1]
        means[2] = means[1]

    def join(side_of):
        coarse = jnp.dot(
            means[side_of].reshape(BLK * 64, C), wcoarse_ref[...], preferred_element_type=F32
        )
        coarse = jnp.maximum(coarse, 0.0).reshape(BLK, 4, 2, 8, C)
        for block in range(BLK):
            for xh in range(4):
                ups = []
                for y in range(2):
                    tile = coarse[block, xh, y]
                    for up in (
                        jnp.where(even, tile, pltpu.roll(tile, 1, 0)),
                        jnp.where(even, pltpu.roll(tile, 7, 0), tile),
                    ):
                        ups += [up, up]
                ups = jnp.concatenate(ups, axis=0)
                for half_x in range(2):
                    x = 2 * xh + half_x
                    at = BLK * side_of + block
                    field[at, x] = (encoded[at, x].astype(F32) + ups).astype(BF16)

    join(1)

    @pl.when((turn == 0) | (turn == SIB - 1))
    def _():
        drain(means.at[1], mean_sems.at[0])
        drain(means.at[1], mean_sems.at[1])

    drain(encoded.at[0 : 2 * BLK], encoded_sems.at[1])
    join(0)
    join(2)
    fill_shifts(table_s, field, shifts)

    group_half = half_in.shape[1]
    piece_rows = piece_own.shape[1]
    active = group_half // piece_rows

    def swap(group):
        return remote(
            part.at[group, pl.ds(pl.multiple_of((1 - core) * group_half, 16), group_half)],
            half_in.at[group],
            core_sems.at[0],
            core_sems.at[1 + group],
            at_blk(other),
        )

    def piece_at(index):
        return pl.ds(pl.multiple_of(index * piece_rows, 16), piece_rows)

    def final_at(group, side_of, index):
        start = side_of * group_half + index * piece_rows
        start = start // (3 * C) * (9 * C) + group * (3 * C) + lax.rem(start, 3 * C)
        return pl.ds(pl.multiple_of(start, 16), piece_rows)

    def to_chip(step):
        return lax.rem(chip + step, chips)

    def from_chip(step):
        return lax.rem(chip + chips - step, chips)

    def scatter(group, step):
        return remote(
            half.at[group, piece_at(to_chip(step))],
            piece_in.at[group, chip],
            plane_sems.at[0],
            plane_sems.at[1 + group],
            at_blk(plane_peer(step)),
        )

    def gather(group, step):
        return remote(
            piece_own.at[group],
            grad_ref.at[final_at(group, core, chip)],
            gather_sems.at[0],
            gather_sems.at[1 + group],
            at_blk(plane_peer(step)),
        )

    def forward(group, index):
        at = final_at(group, core, index)
        return remote(
            grad_ref.at[at], grad_ref.at[at], forward_sems.at[0], forward_sems.at[1], at_blk(other)
        )

    def each_step(action):
        def body(step, carry):
            action(step)
            return carry

        lax.fori_loop(1, chips, body, 0)

    def halve(group):
        drain(half_in.at[group], core_sems.at[1 + group])
        mine = pl.ds(pl.multiple_of(core * group_half, 16), group_half)
        half[group] = (part[group, mine].astype(F32) + half_in[group].astype(F32)).astype(BF16)

        def start(step):
            @pl.when(to_chip(step) < active)
            def _():
                scatter(group, step).start()

        each_step(start)

    def tap_row(dy, carry):
        @pl.when(dy < 3)
        def _():
            sums = []
            for u in range(4):
                total = jnp.zeros((2 * C, 3 * C), F32)
                for pair in range(2):
                    rows = shifts[pair, u % 2, u // 2 : u // 2 + 4, pl.ds(dy, 8)]
                    total = total + jnp.dot(
                        cot_t[pair], rows.reshape(512, 3 * C), preferred_element_type=F32
                    )
                sums.append(total)
            for dx in range(3):
                taps = sums[dx][:C] + sums[dx + 1][C:]
                for dz in range(3):
                    at = (dx * 3 + dz) * C
                    part[dy, at : at + C] = taps[:, dz * C : dz * C + C].T.astype(BF16)
            swap(dy).start()

        @pl.when(dy > 0)
        def _():
            halve(dy - 1)

        return carry

    lax.fori_loop(0, 4, tap_row, 0)

    def decode(pair):
        total = convolve(shifts, big2, pair)
        for j in range(2):
            for xh in range(4):
                for half_x in range(2):
                    x = 2 * xh + half_x
                    piece = total[xh, :, j, :, half_x * C : half_x * C + C].reshape(64, C)
                    block = 2 * pair + j
                    dec_ref[block, x] = (piece + field[BLK + block, x].astype(F32)).astype(BF16)

    def x_moves(group):
        return [
            remote(
                piece_x.at[group, rep],
                piece_x.at[group, rep],
                x_sems.at[0],
                x_sems.at[1 + group],
                at_rep(rep_peer(step)),
            )
            for step in range(1, reps)
        ]

    def reduce_piece(group):
        @pl.when(chip < active)
        def _():
            drain(piece_in.at[group, 0 : chips - 1], plane_sems.at[1 + group])
            piece_in[group, chip] = half[group, piece_at(chip)]

            def add(index, total):
                return total + piece_in[group, index].astype(F32)

            total = lax.fori_loop(0, chips, add, jnp.zeros((piece_rows, C), F32))
            piece_x[group, rep] = total.astype(BF16)
            for move in x_moves(group):
                move.start()

    def spread_piece(group):
        @pl.when(chip < active)
        def _():
            drain(piece_x.at[group, 0 : reps - 1], x_sems.at[1 + group])
            total = piece_x[group, 0].astype(F32)
            for index in range(1, reps):
                total = total + piece_x[group, index].astype(F32)
            piece_own[group] = total.astype(BF16)

            def start(step):
                gather(group, step).start()

            each_step(start)
            keep = pltpu.make_async_copy(
                piece_own.at[group], grad_ref.at[final_at(group, core, chip)], load_sems.at[9]
            )
            keep.start()
            keep.wait()
            forward(group, chip).start()

    def forward_pieces(group):
        @pl.when(chip < active)
        def _():
            drain(piece_in.at[group, 0 : active - 1], gather_sems.at[1 + group])

        @pl.when(chip >= active)
        def _():
            drain(piece_in.at[group, 0:active], gather_sems.at[1 + group])

        def come(step):
            @pl.when(from_chip(step) < active)
            def _():
                forward(group, from_chip(step)).start()

        each_step(come)

    def finish():
        drain(grad_ref.at[0 : 3 * group_half], forward_sems.at[1])
        drain(grad_ref.at[0 : 3 * group_half], forward_sems.at[0])
        drain(arrived_label.at[0 : peers - 1], label_sems.at[0])
        drain(arrived.at[0 : peers - 1], tile_sems.at[0])
        drain(pooled.at[0:3], sibling_sems.at[0])
        drain(encoded.at[0 : 2 * BLK], encoded_sems.at[0])
        drain(half_in, core_sems.at[0])

        @pl.when(chip < active)
        def _():
            drain(piece_in.at[:, 0 : active - 1], plane_sems.at[0])
            drain(piece_x.at[:, 0 : reps - 1], x_sems.at[0])
            drain(piece_in.at[:, 0 : chips - 1], gather_sems.at[0])

        @pl.when(chip >= active)
        def _():
            drain(piece_in.at[:, 0:active], plane_sems.at[0])

    reduce_piece(0)
    decode(0)
    spread_piece(0)
    reduce_piece(1)
    decode(1)
    spread_piece(1)
    reduce_piece(2)
    forward_pieces(0)
    spread_piece(2)
    forward_pieces(1)
    forward_pieces(2)
    finish()


def local(
    peers,
    reps,
    tiles,
    tile_rows,
    tile_owner,
    tile_slot,
    neighbors,
    w_enc,
    w_coarse,
    w_dec,
    cotangent,
):
    count = tiles.shape[1]
    chips = peers // 2
    group_half = 9 * C // 2
    piece_rows = min(
        rows for rows in (16, 48, 64, 192, 576) if rows * chips >= group_half
    )
    vmem = pl.BlockSpec(memory_space=pltpu.VMEM)
    anywhere = pl.BlockSpec(memory_space=pltpu.HBM)
    dma = pltpu.SemaphoreType.DMA
    decoded, grads = pl.pallas_call(
        functools.partial(kernel, count, peers, reps),
        out_shape=(
            jax.ShapeDtypeStruct((BLK, 8, 64, C), BF16),
            jax.ShapeDtypeStruct((27 * C, C), BF16),
        ),
        in_specs=[anywhere] * 6 + [vmem] + [anywhere] * 2,
        out_specs=(vmem, anywhere),
        scratch_shapes=[
            pltpu.SMEM((1, count), jnp.int32),
            pltpu.SMEM((1, count), jnp.int32),
            pltpu.SMEM((1, count), jnp.int32),
            pltpu.SMEM((BLK, 27), jnp.int32),
            pltpu.SMEM((BLK * 27,), jnp.int32),
            pltpu.VMEM((8, C), jnp.int32),
            pltpu.SMEM((8, C), jnp.int32),
            pltpu.VMEM((count, C, C), BF16),
            pltpu.VMEM((peers, CAP, C, C), BF16),
            pltpu.VMEM((peers, CAP, C), jnp.int32),
            pltpu.VMEM((peers, CAP, C, C), BF16),
            pltpu.VMEM((peers, CAP, C), jnp.int32),
            pltpu.VMEM((4 * BLK, C, C), F32),
            pltpu.VMEM((3 * BLK + 1, 8, 64, C), BF16),
            pltpu.VMEM((3 * BLK, 8, 64, C), BF16),
            pltpu.VMEM((2, 2, 5, 10, 16, 3 * C), BF16),
            pltpu.VMEM((12, 3 * C, 2 * C), BF16),
            pltpu.VMEM((12, 3 * C, 2 * C), BF16),
            pltpu.VMEM((27, C, C), BF16),
            pltpu.VMEM((27, C, C), BF16),
            pltpu.VMEM((BLK, 8, 64, C), BF16),
            pltpu.VMEM((2, 2 * C, 512), BF16),
            pltpu.VMEM((SIB, BLK, 4, 16, C), BF16),
            pltpu.VMEM((3, BLK, 4, 16, C), BF16),
            pltpu.VMEM((3, 9 * C, C), BF16),
            pltpu.VMEM((3, group_half, C), BF16),
            pltpu.VMEM((3, group_half, C), BF16),
            pltpu.VMEM((3, chips, piece_rows, C), BF16),
            pltpu.VMEM((3, reps, piece_rows, C), BF16),
            pltpu.VMEM((3, piece_rows, C), BF16),
            dma((10,)),
            dma((peers,)),
            dma((2,)),
            dma((2,)),
            dma((2,)),
            dma((5,)),
            dma((2,)),
            dma((4,)),
            dma((4,)),
            dma((4,)),
            dma((4,)),
            dma((2,)),
        ],
        compiler_params=pltpu.CompilerParams(
            collective_id=0, has_side_effects=True, vmem_limit_bytes=VMEM_LIMIT
        ),
        name="level",
    )(
        tile_rows,
        tile_owner.reshape(1, count),
        tile_slot,
        neighbors[0],
        tiles[0],
        w_enc,
        w_coarse,
        w_dec,
        cotangent[0].reshape(BLK, 8, 64, C),
    )
    return decoded.reshape(1, BLK, 512, C), grads.astype(F32).reshape(27, C, C)


def solution(mesh):
    placed = (
        P("rep", "blk", None, None),
        P("rep", "blk"),
        P("rep", "blk", None),
        P("rep", "blk"),
        P("rep", "blk", None),
        P(),
        P(),
        P(),
        P("rep", "blk", None, None),
    )
    return jax.shard_map(
        functools.partial(local, mesh.shape["blk"], mesh.shape["rep"]),
        mesh=mesh,
        in_specs=placed,
        out_specs=(P("rep", "blk", None, None), P()),
        check_vma=False,
    )
```

```python
import functools
import math

import jax
import jax.numpy as jnp
from jax import lax
from jax.experimental import pallas as pl
from jax.experimental.pallas import tpu as pltpu
from jax.sharding import PartitionSpec as P

C = 128
CAP = 2
BLK = 4
SIB = 4
F32 = jnp.float32
BF16 = jnp.bfloat16
MESH = pl.DeviceIdType.MESH
WINDOW = 16
VMEM_LIMIT = 63 * 1024 * 1024


def at_blk(index):
    return {"blk": index}


def at_rep(index):
    return {"rep": index}


def fill_weights(w_ref, big):
    zero = jnp.zeros((C, C), BF16)
    for u in range(4):
        for dy in range(3):
            for dz in range(3):
                for half in range(2):
                    dx = u - half
                    tap = w_ref[dx * 9 + dy * 3 + dz] if 0 <= dx <= 2 else zero
                    big[u * 3 + dy, dz * C : dz * C + C, half * C : half * C + C] = tap


def fill_shifts(tab_ref, field, shifts):
    level = lax.broadcasted_iota(jnp.int32, (10, 8, C), 1)

    def body(i, carry):
        pair, plane = i // 10, i % 10
        first = jnp.where(plane == 0, 0, jnp.where(plane == 9, 2, 1))
        at = lax.rem(plane + 7, 8)
        parts = []
        for j in range(2):
            base = (2 * pair + j) * 27 + first * 9
            cells = []
            for c in range(3):
                low = field[tab_ref[base + c], at, 48:64].astype(F32)[8:16]
                mid = field[tab_ref[base + 3 + c], at].astype(F32)
                high = field[tab_ref[base + 6 + c], at, 0:16].astype(F32)[0:8]
                cells.append(jnp.concatenate([low, mid, high], axis=0).reshape(10, 8, C))
            parts.append(
                (
                    pltpu.roll(jnp.where(level == 7, cells[0], cells[1]), 1, 1),
                    cells[1],
                    pltpu.roll(jnp.where(level == 0, cells[2], cells[1]), 7, 1),
                )
            )
        for c in range(3):
            both = jnp.concatenate([parts[0][c], parts[1][c]], axis=1).astype(BF16)
            shifts[pair, lax.rem(plane, 2), plane // 2, :, :, c * C : c * C + C] = both
        return carry

    lax.fori_loop(0, 20, body, 0)


def operand(shifts, pair, u, dy):
    return shifts[pair, u % 2, u // 2 : u // 2 + 4, dy : dy + 8].reshape(512, 3 * C)


def convolve(shifts, big, pair):
    taps = [operand(shifts, pair, u, dy) for u in range(4) for dy in range(3)]
    total = jnp.dot(
        jnp.concatenate(taps, axis=1),
        big[...].reshape(36 * C, 2 * C),
        preferred_element_type=F32,
    )
    return total.reshape(4, 8, 2, 8, 2 * C)


def kernel(
    count,
    peers,
    reps,
    rows_hbm,
    owner_hbm,
    slot_hbm,
    neighbors_hbm,
    tiles_hbm,
    wenc_hbm,
    wcoarse_ref,
    wdec_hbm,
    cot_hbm,
    dec_ref,
    grad_ref,
    rows_s,
    owner_s,
    slot_s,
    neighbors_s,
    table_s,
    places_v,
    places_s,
    tiles,
    outgoing,
    outgoing_label,
    arrived,
    arrived_label,
    landed,
    field,
    encoded,
    shifts,
    big,
    big2,
    wenc,
    wdec,
    cot,
    cot_t,
    pooled,
    means,
    part,
    half_in,
    half,
    piece_in,
    piece_x,
    piece_own,
    whole,
    load_sems,
    tile_sems,
    label_sems,
    halo_sems,
    encoded_sems,
    sibling_sems,
    mean_sems,
    core_sems,
    plane_sems,
    x_sems,
    gather_sems,
    forward_sems,
):
    me = lax.axis_index("blk")
    rep = lax.axis_index("rep")
    chips = peers // 2
    side = math.isqrt(chips)
    core, chip = lax.rem(me, 2), me // 2
    chip_y, chip_z = lax.rem(chip, side), chip // side
    other = me + 1 - 2 * core
    right, left = lax.rem(me + 1, peers), lax.rem(me + peers - 1, peers)

    loads = [
        pltpu.make_async_copy(source, target, load_sems.at[i])
        for i, (source, target) in enumerate(
            [
                (owner_hbm, owner_s),
                (rows_hbm, rows_s),
                (slot_hbm, slot_s),
                (tiles_hbm, tiles),
                (neighbors_hbm, neighbors_s),
                (wenc_hbm, wenc),
                (wdec_hbm, wdec),
                (cot_hbm, cot),
            ]
        )
    ]
    for load in loads:
        load.start()

    def remote(source, target, send_sem, recv_sem, where):
        return pltpu.make_async_remote_copy(
            src_ref=source,
            dst_ref=target,
            send_sem=send_sem,
            recv_sem=recv_sem,
            device_id=where,
            device_id_type=MESH,
        )

    def drain(ref, sem):
        pltpu.make_async_copy(ref, ref, sem).wait()

    turn = lax.rem(me, SIB)
    across = me - turn + lax.rem(turn + 2, SIB)

    def plane_peer(step):
        return 2 * lax.rem(chip + step, chips) + core

    def rep_peer(step):
        return lax.rem(rep + step, reps)

    barrier = pltpu.get_barrier_semaphore()

    def greet(step, carry):
        pl.semaphore_signal(
            barrier, inc=1, device_id=at_blk(lax.rem(me + step, peers)), device_id_type=MESH
        )
        return carry

    lax.fori_loop(1, peers, greet, 0)
    for step in range(1, reps):
        pl.semaphore_signal(
            barrier, inc=1, device_id=at_rep(rep_peer(step)), device_id_type=MESH
        )

    loads[0].wait()
    lane = lax.broadcasted_iota(jnp.int32, (8, C), 1)

    def note(t, carry):
        first, second = carry
        hit = lane == owner_s[0, t]
        second = jnp.where(hit & (first >= 0), t, second)
        first = jnp.where(hit & (first < 0), t, first)
        return first, second

    none = jnp.full((8, C), -1, jnp.int32)
    first, second = lax.fori_loop(0, count, note, (none, none))
    places_v[...] = jnp.where(lax.broadcasted_iota(jnp.int32, (8, C), 0) == 0, first, second)
    move = pltpu.make_async_copy(places_v, places_s, load_sems.at[8])
    move.start()
    loads[1].wait()
    loads[2].wait()
    move.wait()
    loads[3].wait()
    row = lax.broadcasted_iota(jnp.int32, (C, C), 0)

    def bucket(owner):
        for rank in range(CAP):
            tile = places_s[rank, owner]
            at = jnp.maximum(tile, 0)
            live = jnp.where(tile >= 0, rows_s[0, at], 0)
            outgoing[owner, rank] = jnp.where(row < live, tiles[at].astype(F32), 0.0).astype(BF16)
            outgoing_label[owner, rank : rank + 1] = jnp.full((1, C), slot_s[0, at], jnp.int32)

    def chip_beside(step, sign):
        k = step // 2
        move_y = lax.rem(k, side)
        move_z = lax.rem(k // side + move_y, side)
        return side * lax.rem(chip_z + side + sign * move_z, side) + lax.rem(
            chip_y + side + sign * move_y, side
        )

    def target_of(step):
        return 2 * chip_beside(step, 1 - 2 * core) + lax.rem(core + step, 2)

    def source_of(step):
        from_core = lax.rem(core + step, 2)
        return 2 * chip_beside(step, 2 * from_core - 1) + from_core

    def label_move(step):
        peer = target_of(step)
        return remote(
            outgoing_label.at[peer],
            arrived_label.at[me],
            label_sems.at[0],
            label_sems.at[step],
            at_blk(peer),
        )

    def tile_move(step):
        peer = target_of(step)
        return remote(
            outgoing.at[peer], arrived.at[me], tile_sems.at[0], tile_sems.at[step], at_blk(peer)
        )

    pl.semaphore_wait(barrier, peers - 1 + reps - 1)

    def step_of(i):
        return 1 + lax.rem(i + 1, peers - 1)

    def send(i, carry):
        step = step_of(i)
        bucket(target_of(step))
        label_move(step).start()
        tile_move(step).start()
        return carry

    lax.fori_loop(0, WINDOW, send, 0)
    bucket(me)

    landed[...] = jnp.zeros_like(landed)

    def land(labels, tiles_at):
        rows = [labels[rank : rank + 1] for rank in range(CAP)]
        for at in range(0, C, 32):
            pieces = [tiles_at[rank, at : at + 32].astype(F32) for rank in range(CAP)]
            for quarter in range(4 * BLK):
                total = landed[quarter, at : at + 32]
                for rank in range(CAP):
                    total = total + jnp.where(rows[rank] == quarter, pieces[rank], 0.0)
                landed[quarter, at : at + 32] = total

    land(outgoing_label[me], outgoing.at[me])
    loads[4].wait()

    def look(block, carry):
        for column in range(27):
            entry = neighbors_s[block, column]
            beside = me + entry // BLK - 1
            keep = (entry >= 0) & (beside >= 0) & (beside < peers)
            table_s[block * 27 + column] = jnp.where(keep, entry, 3 * BLK)
        return carry

    lax.fori_loop(0, BLK, look, 0)
    field[3 * BLK] = jnp.zeros((8, 64, C), BF16)
    loads[5].wait()
    fill_weights(wenc, big)
    loads[6].wait()
    fill_weights(wdec, big2)
    loads[7].wait()
    for pair in range(2):
        for parity in range(2):
            for xh in range(4):
                rows = [
                    cot[2 * pair + j, parity + 2 * xh].astype(F32).reshape(8, 1, 8, C)
                    for j in range(2)
                ]
                rows = jnp.concatenate(rows, axis=1).reshape(128, C)
                cot_t[pair, parity * C : parity * C + C, xh * 128 : xh * 128 + 128] = rows.T.astype(
                    BF16
                )

    def arrive(i, carry):
        step = step_of(i)
        source = source_of(step)
        drain(arrived.at[source], tile_sems.at[step])
        drain(arrived_label.at[source], label_sems.at[step])

        @pl.when(i + WINDOW < peers - 1)
        def _():
            send(i + WINDOW, 0)

        land(arrived_label[source], arrived.at[source])
        return carry

    lax.fori_loop(0, peers - 1, arrive, 0)
    for quarter in range(4 * BLK):
        planes = landed[quarter].astype(BF16).reshape(2, 64, C)
        x = 2 * (quarter % 4)
        field[BLK + quarter // 4, x : x + 2] = planes

    own = field.at[BLK : 2 * BLK]
    for target, where in ((field.at[0:BLK], right), (field.at[2 * BLK : 3 * BLK], left)):
        remote(own, target, halo_sems.at[0], halo_sems.at[1], at_blk(where)).start()
    drain(field.at[0 : 2 * BLK], halo_sems.at[1])
    drain(field.at[0 : 2 * BLK], halo_sems.at[0])

    fill_shifts(table_s, field, shifts)
    level = lax.broadcasted_iota(jnp.int32, (8, C), 0)
    even = lax.rem(level, 2) == 0

    def sibling_move(pair, where, kind):
        piece = pooled.at[turn, pl.ds(2 * pair, 2)]
        return remote(
            piece, piece, sibling_sems.at[0], sibling_sems.at[1 + kind], at_blk(where)
        )

    def halo_moves(pair):
        source = encoded.at[pl.ds(BLK + 2 * pair, 2)]
        return [
            remote(
                source,
                encoded.at[pl.ds(first + 2 * pair, 2)],
                encoded_sems.at[0],
                encoded_sems.at[1],
                at_blk(where),
            )
            for first, where in ((0, right), (2 * BLK, left))
        ]

    def encode(pair, carry):
        total = convolve(shifts, big, pair)
        rounded = jnp.maximum(total, 0.0).astype(BF16).astype(F32)
        for j in range(2):
            for xh in range(4):
                for half_x in range(2):
                    encoded[BLK + 2 * pair + j, 2 * xh + half_x] = (
                        rounded[xh, :, j, :, half_x * C : half_x * C + C]
                        .reshape(64, C)
                        .astype(BF16)
                    )
                flat = rounded[xh, :, j, :, :C] + rounded[xh, :, j, :, C:]
                flat = flat.reshape(4, 2, 8, C)
                flat = flat[:, 0] + flat[:, 1]
                folded = [
                    flat[y]
                    + jnp.where(even, pltpu.roll(flat[y], 7, 0), pltpu.roll(flat[y], 1, 0))
                    for y in range(4)
                ]
                packed = [
                    jnp.where(even, folded[2 * y], folded[2 * y + 1]) * 0.125 for y in range(2)
                ]
                pooled[turn, 2 * pair + j, xh] = jnp.concatenate(packed, axis=0).astype(BF16)
        sibling_move(pair, across, pair).start()
        sibling_move(pair, other, 2).start()
        for move in halo_moves(pair):
            move.start()
        return carry

    lax.fori_loop(0, 2, encode, 0)

    opposite = lax.rem(turn + 2, SIB)
    for pair in range(2):
        piece = pooled.at[opposite, 2 * pair : 2 * pair + 2]
        drain(piece, sibling_sems.at[1 + pair])
        remote(piece, piece, sibling_sems.at[0], sibling_sems.at[4], at_blk(other)).start()
    drain(pooled.at[0], sibling_sems.at[3])
    drain(pooled.at[0], sibling_sems.at[4])
    mean = pooled[0].astype(F32)
    for step in range(1, SIB):
        mean = mean + pooled[step].astype(F32)
    means[1] = (mean * (1.0 / SIB)).astype(BF16)

    def mean_move(side_of, where):
        return remote(
            means.at[1], means.at[side_of], mean_sems.at[0], mean_sems.at[1], at_blk(where)
        )

    @pl.when(turn == SIB - 1)
    def _():
        mean_move(0, right).start()
        means[0] = means[1]

    @pl.when(turn == 0)
    def _():
        mean_move(2, left).start()
        means[2] = means[1]

    @pl.when((turn != 0) & (turn != SIB - 1))
    def _():
        means[0] = means[1]
        means[2] = means[1]

    def join(side_of):
        coarse = jnp.dot(
            means[side_of].reshape(BLK * 64, C), wcoarse_ref[...], preferred_element_type=F32
        )
        coarse = jnp.maximum(coarse, 0.0).reshape(BLK, 4, 2, 8, C)
        for block in range(BLK):
            for xh in range(4):
                ups = []
                for y in range(2):
                    tile = coarse[block, xh, y]
                    for up in (
                        jnp.where(even, tile, pltpu.roll(tile, 1, 0)),
                        jnp.where(even, pltpu.roll(tile, 7, 0), tile),
                    ):
                        ups += [up, up]
                ups = jnp.concatenate(ups, axis=0)
                for half_x in range(2):
                    x = 2 * xh + half_x
                    at = BLK * side_of + block
                    field[at, x] = (encoded[at, x].astype(F32) + ups).astype(BF16)

    join(1)

    @pl.when((turn == 0) | (turn == SIB - 1))
    def _():
        drain(means.at[1], mean_sems.at[0])
        drain(means.at[1], mean_sems.at[1])

    drain(encoded.at[0 : 2 * BLK], encoded_sems.at[1])
    join(0)
    join(2)
    fill_shifts(table_s, field, shifts)

    group_half = half_in.shape[1]
    piece_rows = piece_own.shape[1]
    active = group_half // piece_rows

    def swap(group):
        return remote(
            part.at[group, pl.ds(pl.multiple_of((1 - core) * group_half, 16), group_half)],
            half_in.at[group],
            core_sems.at[0],
            core_sems.at[1 + group],
            at_blk(other),
        )

    def piece_at(index):
        return pl.ds(pl.multiple_of(index * piece_rows, 16), piece_rows)

    def final_at(group, side_of, index):
        start = side_of * group_half + index * piece_rows
        start = start // (3 * C) * (9 * C) + group * (3 * C) + lax.rem(start, 3 * C)
        return pl.ds(pl.multiple_of(start, 16), piece_rows)

    def to_chip(step):
        return lax.rem(chip + step, chips)

    def from_chip(step):
        return lax.rem(chip + chips - step, chips)

    def scatter(group, step):
        return remote(
            half.at[group, piece_at(to_chip(step))],
            piece_in.at[group, chip],
            plane_sems.at[0],
            plane_sems.at[1 + group],
            at_blk(plane_peer(step)),
        )

    def gather(group, step):
        return remote(
            piece_own.at[group],
            whole.at[final_at(group, core, chip)],
            gather_sems.at[0],
            gather_sems.at[1 + group],
            at_blk(plane_peer(step)),
        )

    def forward(group, index):
        at = final_at(group, core, index)
        return remote(
            whole.at[at], whole.at[at], forward_sems.at[0],
            forward_sems.at[1 + group],
            at_blk(other),

        )

    def each_step(action):
        def body(step, carry):
            action(step)
            return carry

        lax.fori_loop(1, chips, body, 0)

    def halve(group):
        drain(half_in.at[group], core_sems.at[1 + group])
        mine = pl.ds(pl.multiple_of(core * group_half, 16), group_half)
        half[group] = (part[group, mine].astype(F32) + half_in[group].astype(F32)).astype(BF16)

        def start(step):
            @pl.when(to_chip(step) < active)
            def _():
                scatter(group, step).start()

        each_step(start)

    def tap_row(dy, carry):
        @pl.when(dy < 3)
        def _():
            sums = []
            for u in range(4):
                total = jnp.zeros((2 * C, 3 * C), F32)
                for pair in range(2):
                    rows = shifts[pair, u % 2, u // 2 : u // 2 + 4, pl.ds(dy, 8)]
                    total = total + jnp.dot(
                        cot_t[pair], rows.reshape(512, 3 * C), preferred_element_type=F32
                    )
                sums.append(total)
            for dx in range(3):
                taps = sums[dx][:C] + sums[dx + 1][C:]
                for dz in range(3):
                    at = (dx * 3 + dz) * C
                    part[dy, at : at + C] = taps[:, dz * C : dz * C + C].T.astype(BF16)
            swap(dy).start()

        @pl.when(dy > 0)
        def _():
            halve(dy - 1)

        return carry

    lax.fori_loop(0, 4, tap_row, 0)

    def decode(pair):
        total = convolve(shifts, big2, pair)
        for j in range(2):
            for xh in range(4):
                for half_x in range(2):
                    x = 2 * xh + half_x
                    piece = total[xh, :, j, :, half_x * C : half_x * C + C].reshape(64, C)
                    block = 2 * pair + j
                    dec_ref[block, x] = (piece + field[BLK + block, x].astype(F32)).astype(BF16)

    def x_moves(group):
        return [
            remote(
                piece_x.at[group, rep],
                piece_x.at[group, rep],
                x_sems.at[0],
                x_sems.at[1 + group],
                at_rep(rep_peer(step)),
            )
            for step in range(1, reps)
        ]

    def reduce_piece(group):
        @pl.when(chip < active)
        def _():
            drain(piece_in.at[group, 0 : chips - 1], plane_sems.at[1 + group])
            piece_in[group, chip] = half[group, piece_at(chip)]

            def add(index, total):
                return total + piece_in[group, index].astype(F32)

            total = lax.fori_loop(0, chips, add, jnp.zeros((piece_rows, C), F32))
            piece_x[group, rep] = total.astype(BF16)
            for move in x_moves(group):
                move.start()

    def spread_piece(group):
        @pl.when(chip < active)
        def _():
            drain(piece_x.at[group, 0 : reps - 1], x_sems.at[1 + group])
            total = piece_x[group, 0].astype(F32)
            for index in range(1, reps):
                total = total + piece_x[group, index].astype(F32)
            piece_own[group] = total.astype(BF16)

            def start(step):
                gather(group, step).start()

            each_step(start)
            whole[final_at(group, core, chip)] = piece_own[group]
            forward(group, chip).start()

    def forward_pieces(group):
        @pl.when(chip < active)
        def _():
            drain(piece_in.at[group, 0 : active - 1], gather_sems.at[1 + group])

        @pl.when(chip >= active)
        def _():
            drain(piece_in.at[group, 0:active], gather_sems.at[1 + group])

        def come(step):
            @pl.when(from_chip(step) < active)
            def _():
                forward(group, from_chip(step)).start()

        each_step(come)

    def finish():
        for group in range(3):
            drain(half_in.at[group], forward_sems.at[1 + group])
            for dx in range(3):
                at = pl.ds(dx * 9 * C + group * 3 * C, 3 * C)
                pltpu.make_async_copy(whole.at[at], grad_ref.at[at], load_sems.at[9]).start()
        drain(whole, load_sems.at[9])
        drain(half_in, forward_sems.at[0])
        drain(arrived_label.at[0 : peers - 1], label_sems.at[0])
        drain(arrived.at[0 : peers - 1], tile_sems.at[0])
        drain(pooled.at[0:3], sibling_sems.at[0])
        drain(encoded.at[0 : 2 * BLK], encoded_sems.at[0])
        drain(half_in, core_sems.at[0])

        @pl.when(chip < active)
        def _():
            drain(piece_in.at[:, 0 : active - 1], plane_sems.at[0])
            drain(piece_x.at[:, 0 : reps - 1], x_sems.at[0])
            drain(piece_in.at[:, 0 : chips - 1], gather_sems.at[0])

        @pl.when(chip >= active)
        def _():
            drain(piece_in.at[:, 0:active], plane_sems.at[0])

    decode(0)
    reduce_piece(0)
    reduce_piece(1)
    decode(1)
    reduce_piece(2)
    for stage in (spread_piece, forward_pieces):
        for group in range(3):
            stage(group)
    finish()


def local(
    peers,
    reps,
    tiles,
    tile_rows,
    tile_owner,
    tile_slot,
    neighbors,
    w_enc,
    w_coarse,
    w_dec,
    cotangent,
):
    count = tiles.shape[1]
    chips = peers // 2
    group_half = 9 * C // 2
    piece_rows = min(
        rows for rows in (16, 48, 64, 192, 576) if rows * chips >= group_half
    )
    vmem = pl.BlockSpec(memory_space=pltpu.VMEM)
    anywhere = pl.BlockSpec(memory_space=pltpu.HBM)
    dma = pltpu.SemaphoreType.DMA
    decoded, grads = pl.pallas_call(
        functools.partial(kernel, count, peers, reps),
        out_shape=(
            jax.ShapeDtypeStruct((BLK, 8, 64, C), BF16),
            jax.ShapeDtypeStruct((27 * C, C), BF16),
        ),
        in_specs=[anywhere] * 6 + [vmem] + [anywhere] * 2,
        out_specs=(vmem, anywhere),
        scratch_shapes=[
            pltpu.SMEM((1, count), jnp.int32),
            pltpu.SMEM((1, count), jnp.int32),
            pltpu.SMEM((1, count), jnp.int32),
            pltpu.SMEM((BLK, 27), jnp.int32),
            pltpu.SMEM((BLK * 27,), jnp.int32),
            pltpu.VMEM((8, C), jnp.int32),
            pltpu.SMEM((8, C), jnp.int32),
            pltpu.VMEM((count, C, C), BF16),
            pltpu.VMEM((peers, CAP, C, C), BF16),
            pltpu.VMEM((peers, CAP, C), jnp.int32),
            pltpu.VMEM((peers, CAP, C, C), BF16),
            pltpu.VMEM((peers, CAP, C), jnp.int32),
            pltpu.VMEM((4 * BLK, C, C), F32),
            pltpu.VMEM((3 * BLK + 1, 8, 64, C), BF16),
            pltpu.VMEM((3 * BLK, 8, 64, C), BF16),
            pltpu.VMEM((2, 2, 5, 10, 16, 3 * C), BF16),
            pltpu.VMEM((12, 3 * C, 2 * C), BF16),
            pltpu.VMEM((12, 3 * C, 2 * C), BF16),
            pltpu.VMEM((27, C, C), BF16),
            pltpu.VMEM((27, C, C), BF16),
            pltpu.VMEM((BLK, 8, 64, C), BF16),
            pltpu.VMEM((2, 2 * C, 512), BF16),
            pltpu.VMEM((SIB, BLK, 4, 16, C), BF16),
            pltpu.VMEM((3, BLK, 4, 16, C), BF16),
            pltpu.VMEM((3, 9 * C, C), BF16),
            pltpu.VMEM((3, group_half, C), BF16),
            pltpu.VMEM((3, group_half, C), BF16),
            pltpu.VMEM((3, chips, piece_rows, C), BF16),
            pltpu.VMEM((3, reps, piece_rows, C), BF16),
            pltpu.VMEM((3, piece_rows, C), BF16),
            pltpu.VMEM((27 * C, C), BF16),
            dma((10,)),
            dma((peers,)),
            dma((peers,)),
            dma((2,)),
            dma((2,)),
            dma((5,)),
            dma((2,)),
            dma((4,)),
            dma((4,)),
            dma((4,)),
            dma((4,)),
            dma((4,)),
        ],
        compiler_params=pltpu.CompilerParams(
            collective_id=0, has_side_effects=True, vmem_limit_bytes=VMEM_LIMIT
        ),
        name="level",
    )(
        tile_rows,
        tile_owner.reshape(1, count),
        tile_slot,
        neighbors[0],
        tiles[0],
        w_enc,
        w_coarse,
        w_dec,
        cotangent[0].reshape(BLK, 8, 64, C),
    )
    return decoded.reshape(1, BLK, 512, C), grads.astype(F32).reshape(27, C, C)


def solution(mesh):
    placed = (
        P("rep", "blk", None, None),
        P("rep", "blk"),
        P("rep", "blk", None),
        P("rep", "blk"),
        P("rep", "blk", None),
        P(),
        P(),
        P(),
        P("rep", "blk", None, None),
    )
    return jax.shard_map(
        functools.partial(local, mesh.shape["blk"], mesh.shape["rep"]),
        mesh=mesh,
        in_specs=placed,
        out_specs=(P("rep", "blk", None, None), P()),
        check_vma=False,
    )
```

```python
import functools
import math

import jax
import jax.numpy as jnp
from jax import lax
from jax.experimental import pallas as pl
from jax.experimental.pallas import tpu as pltpu
from jax.sharding import PartitionSpec as P

C = 128
CAP = 2
BLK = 4
SIB = 4
F32 = jnp.float32
BF16 = jnp.bfloat16
MESH = pl.DeviceIdType.MESH
WINDOW = 16
VMEM_LIMIT = 48 * 1024 * 1024


def at_blk(index):
    return {"blk": index}


def at_rep(index):
    return {"rep": index}


def fill_weights(w_ref, big):
    zero = jnp.zeros((C, C), BF16)
    for u in range(4):
        for dy in range(3):
            for dz in range(3):
                for half in range(2):
                    dx = u - half
                    tap = w_ref[dx * 9 + dy * 3 + dz] if 0 <= dx <= 2 else zero
                    big[u * 3 + dy, dz * C : dz * C + C, half * C : half * C + C] = tap


def fill_shifts(tab_ref, field, shifts):
    level = lax.broadcasted_iota(jnp.int32, (10, 8, C), 1)

    def body(i, carry):
        pair, plane = i // 10, i % 10
        first = jnp.where(plane == 0, 0, jnp.where(plane == 9, 2, 1))
        at = lax.rem(plane + 7, 8)
        parts = []
        for j in range(2):
            base = (2 * pair + j) * 27 + first * 9
            cells = []
            for c in range(3):
                low = field[tab_ref[base + c], at, 48:64].astype(F32)[8:16]
                mid = field[tab_ref[base + 3 + c], at].astype(F32)
                high = field[tab_ref[base + 6 + c], at, 0:16].astype(F32)[0:8]
                cells.append(jnp.concatenate([low, mid, high], axis=0).reshape(10, 8, C))
            parts.append(
                (
                    pltpu.roll(jnp.where(level == 7, cells[0], cells[1]), 1, 1),
                    cells[1],
                    pltpu.roll(jnp.where(level == 0, cells[2], cells[1]), 7, 1),
                )
            )
        for c in range(3):
            both = jnp.concatenate([parts[0][c], parts[1][c]], axis=1).astype(BF16)
            shifts[pair, lax.rem(plane, 2), plane // 2, :, :, c * C : c * C + C] = both
        return carry

    lax.fori_loop(0, 20, body, 0)


def operand(shifts, pair, u, dy):
    return shifts[pair, u % 2, u // 2 : u // 2 + 4, dy : dy + 8].reshape(512, 3 * C)


def convolve(shifts, big, pair):
    taps = [operand(shifts, pair, u, dy) for u in range(4) for dy in range(3)]
    total = jnp.dot(
        jnp.concatenate(taps, axis=1),
        big[...].reshape(36 * C, 2 * C),
        preferred_element_type=F32,
    )
    return total.reshape(4, 8, 2, 8, 2 * C)


def kernel(
    count,
    peers,
    reps,
    rows_hbm,
    owner_hbm,
    slot_hbm,
    neighbors_hbm,
    tiles_hbm,
    wenc_hbm,
    wcoarse_ref,
    wdec_hbm,
    cot_hbm,
    dec_ref,
    grad_ref,
    rows_s,
    owner_s,
    slot_s,
    neighbors_s,
    table_s,
    places_v,
    places_s,
    tiles,
    outgoing,
    outgoing_label,
    arrived,
    arrived_label,
    landed,
    field,
    encoded,
    shifts,
    big,
    big2,
    wenc,
    wdec,
    cot,
    cot_t,
    pooled,
    means,
    part,
    half_in,
    half,
    piece_in,
    piece_x,
    piece_own,
    whole,
    load_sems,
    tile_sems,
    label_sems,
    halo_sems,
    encoded_sems,
    sibling_sems,
    mean_sems,
    core_sems,
    plane_sems,
    x_sems,
    gather_sems,
    forward_sems,
):
    me = lax.axis_index("blk")
    rep = lax.axis_index("rep")
    chips = peers // 2
    side = math.isqrt(chips)
    core, chip = lax.rem(me, 2), me // 2
    chip_y, chip_z = lax.rem(chip, side), chip // side
    other = me + 1 - 2 * core
    right, left = lax.rem(me + 1, peers), lax.rem(me + peers - 1, peers)

    loads = [
        pltpu.make_async_copy(source, target, load_sems.at[i])
        for i, (source, target) in enumerate(
            [
                (owner_hbm, owner_s),
                (rows_hbm, rows_s),
                (slot_hbm, slot_s),
                (tiles_hbm, tiles),
                (neighbors_hbm, neighbors_s),
                (wenc_hbm, wenc),
                (wdec_hbm, wdec),
                (cot_hbm, cot),
            ]
        )
    ]
    for load in loads:
        load.start()

    def remote(source, target, send_sem, recv_sem, where):
        return pltpu.make_async_remote_copy(
            src_ref=source,
            dst_ref=target,
            send_sem=send_sem,
            recv_sem=recv_sem,
            device_id=where,
            device_id_type=MESH,
        )

    def drain(ref, sem):
        pltpu.make_async_copy(ref, ref, sem).wait()

    turn = lax.rem(me, SIB)
    across = me - turn + lax.rem(turn + 2, SIB)

    def plane_peer(step):
        return 2 * lax.rem(chip + step, chips) + core

    def rep_peer(step):
        return lax.rem(rep + step, reps)

    barrier = pltpu.get_barrier_semaphore()

    def greet(step, carry):
        pl.semaphore_signal(
            barrier, inc=1, device_id=at_blk(lax.rem(me + step, peers)), device_id_type=MESH
        )
        return carry

    lax.fori_loop(1, peers, greet, 0)
    for step in range(1, reps):
        pl.semaphore_signal(
            barrier, inc=1, device_id=at_rep(rep_peer(step)), device_id_type=MESH
        )

    loads[0].wait()
    lane = lax.broadcasted_iota(jnp.int32, (8, C), 1)

    def note(t, carry):
        first, second = carry
        hit = lane == owner_s[0, t]
        second = jnp.where(hit & (first >= 0), t, second)
        first = jnp.where(hit & (first < 0), t, first)
        return first, second

    none = jnp.full((8, C), -1, jnp.int32)
    first, second = lax.fori_loop(0, count, note, (none, none))
    places_v[...] = jnp.where(lax.broadcasted_iota(jnp.int32, (8, C), 0) == 0, first, second)
    move = pltpu.make_async_copy(places_v, places_s, load_sems.at[8])
    move.start()
    loads[1].wait()
    loads[2].wait()
    move.wait()
    loads[3].wait()
    row = lax.broadcasted_iota(jnp.int32, (C, C), 0)

    def bucket(owner):
        for rank in range(CAP):
            tile = places_s[rank, owner]
            at = jnp.maximum(tile, 0)
            live = jnp.where(tile >= 0, rows_s[0, at], 0)
            outgoing[owner, rank] = jnp.where(row < live, tiles[at].astype(F32), 0.0).astype(BF16)
            outgoing_label[owner, rank : rank + 1] = jnp.full((1, C), slot_s[0, at], jnp.int32)

    def chip_beside(step, sign):
        k = step // 2
        move_y = lax.rem(k, side)
        move_z = lax.rem(k // side + move_y, side)
        return side * lax.rem(chip_z + side + sign * move_z, side) + lax.rem(
            chip_y + side + sign * move_y, side
        )

    def target_of(step):
        return 2 * chip_beside(step, 1 - 2 * core) + lax.rem(core + step, 2)

    def source_of(step):
        from_core = lax.rem(core + step, 2)
        return 2 * chip_beside(step, 2 * from_core - 1) + from_core

    def label_move(step):
        peer = target_of(step)
        return remote(
            outgoing_label.at[peer],
            arrived_label.at[me],
            label_sems.at[0],
            label_sems.at[step],
            at_blk(peer),
        )

    def tile_move(step):
        peer = target_of(step)
        return remote(
            outgoing.at[peer], arrived.at[me], tile_sems.at[0], tile_sems.at[step], at_blk(peer)
        )

    pl.semaphore_wait(barrier, peers - 1 + reps - 1)

    def step_of(i):
        return 1 + lax.rem(i + 1, peers - 1)

    def send(i, carry):
        step = step_of(i)
        bucket(target_of(step))
        label_move(step).start()
        tile_move(step).start()
        return carry

    lax.fori_loop(0, WINDOW, send, 0)
    bucket(me)

    landed[...] = jnp.zeros_like(landed)

    def land(labels, tiles_at):
        rows = [labels[rank : rank + 1] for rank in range(CAP)]
        for at in range(0, C, 32):
            pieces = [tiles_at[rank, at : at + 32].astype(F32) for rank in range(CAP)]
            for quarter in range(4 * BLK):
                total = landed[quarter, at : at + 32]
                for rank in range(CAP):
                    total = total + jnp.where(rows[rank] == quarter, pieces[rank], 0.0)
                landed[quarter, at : at + 32] = total

    land(outgoing_label[me], outgoing.at[me])
    loads[4].wait()

    def look(block, carry):
        for column in range(27):
            entry = neighbors_s[block, column]
            beside = me + entry // BLK - 1
            keep = (entry >= 0) & (beside >= 0) & (beside < peers)
            table_s[block * 27 + column] = jnp.where(keep, entry, 3 * BLK)
        return carry

    lax.fori_loop(0, BLK, look, 0)
    field[3 * BLK] = jnp.zeros((8, 64, C), BF16)
    loads[5].wait()
    fill_weights(wenc, big)
    loads[6].wait()
    fill_weights(wdec, big2)
    loads[7].wait()
    for pair in range(2):
        for parity in range(2):
            for xh in range(4):
                rows = [
                    cot[2 * pair + j, parity + 2 * xh].astype(F32).reshape(8, 1, 8, C)
                    for j in range(2)
                ]
                rows = jnp.concatenate(rows, axis=1).reshape(128, C)
                at = pair * 512 + xh * 128
                cot_t[parity * C : parity * C + C, at : at + 128] = rows.T.astype(BF16)

    def arrive(i, carry):
        step = step_of(i)
        source = source_of(step)
        drain(arrived.at[source], tile_sems.at[step])
        drain(arrived_label.at[source], label_sems.at[step])

        @pl.when(i + WINDOW < peers - 1)
        def _():
            send(i + WINDOW, 0)

        land(arrived_label[source], arrived.at[source])
        return carry

    lax.fori_loop(0, peers - 1, arrive, 0)
    for quarter in range(4 * BLK):
        planes = landed[quarter].astype(BF16).reshape(2, 64, C)
        x = 2 * (quarter % 4)
        field[BLK + quarter // 4, x : x + 2] = planes

    own = field.at[BLK : 2 * BLK]
    for target, where in ((field.at[0:BLK], right), (field.at[2 * BLK : 3 * BLK], left)):
        remote(own, target, halo_sems.at[0], halo_sems.at[1], at_blk(where)).start()
    drain(field.at[0 : 2 * BLK], halo_sems.at[1])
    drain(field.at[0 : 2 * BLK], halo_sems.at[0])

    fill_shifts(table_s, field, shifts)
    level = lax.broadcasted_iota(jnp.int32, (8, C), 0)
    even = lax.rem(level, 2) == 0

    def sibling_move(pair, where, kind):
        piece = pooled.at[turn, pl.ds(2 * pair, 2)]
        return remote(
            piece, piece, sibling_sems.at[0], sibling_sems.at[1 + kind], at_blk(where)
        )

    def halo_moves(pair):
        source = encoded.at[pl.ds(BLK + 2 * pair, 2)]
        return [
            remote(
                source,
                encoded.at[pl.ds(first + 2 * pair, 2)],
                encoded_sems.at[0],
                encoded_sems.at[1],
                at_blk(where),
            )
            for first, where in ((0, right), (2 * BLK, left))
        ]

    def encode(pair, carry):
        total = convolve(shifts, big, pair)
        rounded = jnp.maximum(total, 0.0).astype(BF16).astype(F32)
        for j in range(2):
            for xh in range(4):
                for half_x in range(2):
                    encoded[BLK + 2 * pair + j, 2 * xh + half_x] = (
                        rounded[xh, :, j, :, half_x * C : half_x * C + C]
                        .reshape(64, C)
                        .astype(BF16)
                    )
                flat = rounded[xh, :, j, :, :C] + rounded[xh, :, j, :, C:]
                flat = flat.reshape(4, 2, 8, C)
                flat = flat[:, 0] + flat[:, 1]
                folded = [
                    flat[y]
                    + jnp.where(even, pltpu.roll(flat[y], 7, 0), pltpu.roll(flat[y], 1, 0))
                    for y in range(4)
                ]
                packed = [
                    jnp.where(even, folded[2 * y], folded[2 * y + 1]) * 0.125 for y in range(2)
                ]
                pooled[turn, 2 * pair + j, xh] = jnp.concatenate(packed, axis=0).astype(BF16)
        sibling_move(pair, across, pair).start()
        sibling_move(pair, other, 2).start()
        for move in halo_moves(pair):
            move.start()
        return carry

    lax.fori_loop(0, 2, encode, 0)

    opposite = lax.rem(turn + 2, SIB)
    for pair in range(2):
        piece = pooled.at[opposite, 2 * pair : 2 * pair + 2]
        drain(piece, sibling_sems.at[1 + pair])
        remote(piece, piece, sibling_sems.at[0], sibling_sems.at[4], at_blk(other)).start()
    drain(pooled.at[0], sibling_sems.at[3])
    drain(pooled.at[0], sibling_sems.at[4])
    mean = pooled[0].astype(F32)
    for step in range(1, SIB):
        mean = mean + pooled[step].astype(F32)
    means[1] = (mean * (1.0 / SIB)).astype(BF16)

    def mean_move(side_of, where):
        return remote(
            means.at[1], means.at[side_of], mean_sems.at[0], mean_sems.at[1], at_blk(where)
        )

    @pl.when(turn == SIB - 1)
    def _():
        mean_move(0, right).start()
        means[0] = means[1]

    @pl.when(turn == 0)
    def _():
        mean_move(2, left).start()
        means[2] = means[1]

    @pl.when((turn != 0) & (turn != SIB - 1))
    def _():
        means[0] = means[1]
        means[2] = means[1]

    def join(side_of):
        coarse = jnp.dot(
            means[side_of].reshape(BLK * 64, C), wcoarse_ref[...], preferred_element_type=F32
        )
        coarse = jnp.maximum(coarse, 0.0).reshape(BLK, 4, 2, 8, C)
        for block in range(BLK):
            for xh in range(4):
                ups = []
                for y in range(2):
                    tile = coarse[block, xh, y]
                    for up in (
                        jnp.where(even, tile, pltpu.roll(tile, 1, 0)),
                        jnp.where(even, pltpu.roll(tile, 7, 0), tile),
                    ):
                        ups += [up, up]
                ups = jnp.concatenate(ups, axis=0)
                for half_x in range(2):
                    x = 2 * xh + half_x
                    at = BLK * side_of + block
                    field[at, x] = (encoded[at, x].astype(F32) + ups).astype(BF16)

    join(1)

    @pl.when((turn == 0) | (turn == SIB - 1))
    def _():
        drain(means.at[1], mean_sems.at[0])
        drain(means.at[1], mean_sems.at[1])

    drain(encoded.at[0 : 2 * BLK], encoded_sems.at[1])
    join(0)
    join(2)
    fill_shifts(table_s, field, shifts)

    group_half = half_in.shape[1]
    piece_rows = piece_own.shape[1]
    active = group_half // piece_rows

    def swap(group):
        return remote(
            part.at[group, pl.ds(pl.multiple_of((1 - core) * group_half, 16), group_half)],
            half_in.at[group],
            core_sems.at[0],
            core_sems.at[1 + group],
            at_blk(other),
        )

    def piece_at(index):
        return pl.ds(pl.multiple_of(index * piece_rows, 16), piece_rows)

    def final_at(group, side_of, index):
        start = side_of * group_half + index * piece_rows
        start = start // (3 * C) * (9 * C) + group * (3 * C) + lax.rem(start, 3 * C)
        return pl.ds(pl.multiple_of(start, 16), piece_rows)

    def to_chip(step):
        return lax.rem(chip + step, chips)

    def from_chip(step):
        return lax.rem(chip + chips - step, chips)

    def scatter(group, step):
        return remote(
            half.at[group, piece_at(to_chip(step))],
            piece_in.at[group, chip],
            plane_sems.at[0],
            plane_sems.at[1 + group],
            at_blk(plane_peer(step)),
        )

    def gather(group, step):
        return remote(
            piece_own.at[group],
            whole.at[final_at(group, core, chip)],
            gather_sems.at[0],
            gather_sems.at[1 + group],
            at_blk(plane_peer(step)),
        )

    def forward(group, index):
        at = final_at(group, core, index)
        return remote(
            whole.at[at], whole.at[at], forward_sems.at[0],
            forward_sems.at[1 + group],
            at_blk(other),

        )

    def each_step(action):
        def body(step, carry):
            action(step)
            return carry

        lax.fori_loop(1, chips, body, 0)

    def halve(group):
        drain(half_in.at[group], core_sems.at[1 + group])
        mine = pl.ds(pl.multiple_of(core * group_half, 16), group_half)
        half[group] = (part[group, mine].astype(F32) + half_in[group].astype(F32)).astype(BF16)

        def start(step):
            @pl.when(to_chip(step) < active)
            def _():
                scatter(group, step).start()

        each_step(start)

    def tap_row(dy, carry):
        @pl.when(dy < 3)
        def _():
            rows = [
                jnp.concatenate(
                    [
                        shifts[pair, u % 2, u // 2 : u // 2 + 4, pl.ds(dy, 8)].reshape(512, 3 * C)
                        for pair in range(2)
                    ],
                    axis=0,
                )
                for u in range(4)
            ]
            sums = jnp.dot(
                cot_t[...], jnp.concatenate(rows, axis=1), preferred_element_type=F32
            )
            for tap in range(9):
                at = tap * C
                total = sums[:C, at : at + C] + sums[C:, at + 3 * C : at + 4 * C]
                part[dy, at : at + C] = total.astype(BF16).T
            swap(dy).start()

        @pl.when(dy > 0)
        def _():
            halve(dy - 1)

        return carry

    lax.fori_loop(0, 4, tap_row, 0)

    def decode(pair):
        total = convolve(shifts, big2, pair)
        for j in range(2):
            for xh in range(4):
                for half_x in range(2):
                    x = 2 * xh + half_x
                    piece = total[xh, :, j, :, half_x * C : half_x * C + C].reshape(64, C)
                    block = 2 * pair + j
                    dec_ref[block, x] = (piece + field[BLK + block, x].astype(F32)).astype(BF16)

    def x_moves(group):
        return [
            remote(
                piece_x.at[group, rep],
                piece_x.at[group, rep],
                x_sems.at[0],
                x_sems.at[1 + group],
                at_rep(rep_peer(step)),
            )
            for step in range(1, reps)
        ]

    def reduce_piece(group):
        @pl.when(chip < active)
        def _():
            drain(piece_in.at[group, 0 : chips - 1], plane_sems.at[1 + group])
            piece_in[group, chip] = half[group, piece_at(chip)]

            def add(index, total):
                return total + piece_in[group, index].astype(F32)

            total = lax.fori_loop(0, chips, add, jnp.zeros((piece_rows, C), F32))
            piece_x[group, rep] = total.astype(BF16)
            for move in x_moves(group):
                move.start()

    def spread_piece(group):
        @pl.when(chip < active)
        def _():
            drain(piece_x.at[group, 0 : reps - 1], x_sems.at[1 + group])
            total = piece_x[group, 0].astype(F32)
            for index in range(1, reps):
                total = total + piece_x[group, index].astype(F32)
            piece_own[group] = total.astype(BF16)

            def start(step):
                gather(group, step).start()

            each_step(start)
            whole[final_at(group, core, chip)] = piece_own[group]
            forward(group, chip).start()

    def forward_pieces(group):
        @pl.when(chip < active)
        def _():
            drain(piece_in.at[group, 0 : active - 1], gather_sems.at[1 + group])

        @pl.when(chip >= active)
        def _():
            drain(piece_in.at[group, 0:active], gather_sems.at[1 + group])

        def come(step):
            @pl.when(from_chip(step) < active)
            def _():
                forward(group, from_chip(step)).start()

        each_step(come)

    def finish():
        for group in range(3):
            drain(half_in.at[group], forward_sems.at[1 + group])
            for dx in range(3):
                at = pl.ds(dx * 9 * C + group * 3 * C, 3 * C)
                pltpu.make_async_copy(whole.at[at], grad_ref.at[at], load_sems.at[9]).start()
        drain(whole, load_sems.at[9])
        drain(half_in, forward_sems.at[0])
        drain(arrived_label.at[0 : peers - 1], label_sems.at[0])
        drain(arrived.at[0 : peers - 1], tile_sems.at[0])
        drain(pooled.at[0:3], sibling_sems.at[0])
        drain(encoded.at[0 : 2 * BLK], encoded_sems.at[0])
        drain(half_in, core_sems.at[0])

        @pl.when(chip < active)
        def _():
            drain(piece_in.at[:, 0 : active - 1], plane_sems.at[0])
            drain(piece_x.at[:, 0 : reps - 1], x_sems.at[0])
            drain(piece_in.at[:, 0 : chips - 1], gather_sems.at[0])

        @pl.when(chip >= active)
        def _():
            drain(piece_in.at[:, 0:active], plane_sems.at[0])

    decode(0)
    reduce_piece(0)
    reduce_piece(1)
    decode(1)
    spread_piece(0)
    spread_piece(1)
    reduce_piece(2)
    spread_piece(2)
    for group in range(3):
        forward_pieces(group)
    finish()


def local(
    peers,
    reps,
    tiles,
    tile_rows,
    tile_owner,
    tile_slot,
    neighbors,
    w_enc,
    w_coarse,
    w_dec,
    cotangent,
):
    count = tiles.shape[1]
    chips = peers // 2
    group_half = 9 * C // 2
    piece_rows = min(
        rows for rows in (16, 48, 64, 192, 576) if rows * chips >= group_half
    )
    vmem = pl.BlockSpec(memory_space=pltpu.VMEM)
    anywhere = pl.BlockSpec(memory_space=pltpu.HBM)
    dma = pltpu.SemaphoreType.DMA
    decoded, grads = pl.pallas_call(
        functools.partial(kernel, count, peers, reps),
        out_shape=(
            jax.ShapeDtypeStruct((BLK, 8, 64, C), BF16),
            jax.ShapeDtypeStruct((27 * C, C), BF16),
        ),
        in_specs=[anywhere] * 6 + [vmem] + [anywhere] * 2,
        out_specs=(vmem, anywhere),
        scratch_shapes=[
            pltpu.SMEM((1, count), jnp.int32),
            pltpu.SMEM((1, count), jnp.int32),
            pltpu.SMEM((1, count), jnp.int32),
            pltpu.SMEM((BLK, 27), jnp.int32),
            pltpu.SMEM((BLK * 27,), jnp.int32),
            pltpu.VMEM((8, C), jnp.int32),
            pltpu.SMEM((8, C), jnp.int32),
            pltpu.VMEM((count, C, C), BF16),
            pltpu.VMEM((peers, CAP, C, C), BF16),
            pltpu.VMEM((peers, CAP, C), jnp.int32),
            pltpu.VMEM((peers, CAP, C, C), BF16),
            pltpu.VMEM((peers, CAP, C), jnp.int32),
            pltpu.VMEM((4 * BLK, C, C), F32),
            pltpu.VMEM((3 * BLK + 1, 8, 64, C), BF16),
            pltpu.VMEM((3 * BLK, 8, 64, C), BF16),
            pltpu.VMEM((2, 2, 5, 10, 16, 3 * C), BF16),
            pltpu.VMEM((12, 3 * C, 2 * C), BF16),
            pltpu.VMEM((12, 3 * C, 2 * C), BF16),
            pltpu.VMEM((27, C, C), BF16),
            pltpu.VMEM((27, C, C), BF16),
            pltpu.VMEM((BLK, 8, 64, C), BF16),
            pltpu.VMEM((2 * C, 1024), BF16),
            pltpu.VMEM((SIB, BLK, 4, 16, C), BF16),
            pltpu.VMEM((3, BLK, 4, 16, C), BF16),
            pltpu.VMEM((3, 9 * C, C), BF16),
            pltpu.VMEM((3, group_half, C), BF16),
            pltpu.VMEM((3, group_half, C), BF16),
            pltpu.VMEM((3, chips, piece_rows, C), BF16),
            pltpu.VMEM((3, reps, piece_rows, C), BF16),
            pltpu.VMEM((3, piece_rows, C), BF16),
            pltpu.VMEM((27 * C, C), BF16),
            dma((10,)),
            dma((peers,)),
            dma((peers,)),
            dma((2,)),
            dma((2,)),
            dma((5,)),
            dma((2,)),
            dma((4,)),
            dma((4,)),
            dma((4,)),
            dma((4,)),
            dma((4,)),
        ],
        compiler_params=pltpu.CompilerParams(
            collective_id=0, has_side_effects=True, vmem_limit_bytes=VMEM_LIMIT
        ),
        name="level",
    )(
        *[
            pltpu.with_memory_space_constraint(operand, pltpu.HBM)
            for operand in (
                tile_rows,
                tile_owner.reshape(1, count),
                tile_slot,
                neighbors[0],
                tiles[0],
                w_enc,
                w_coarse,
                w_dec,
                cotangent[0].reshape(BLK, 8, 64, C),
            )
        ]
    )
    return decoded.reshape(1, BLK, 512, C), grads.astype(F32).reshape(27, C, C)


def solution(mesh):
    placed = (
        P("rep", "blk", None, None),
        P("rep", "blk"),
        P("rep", "blk", None),
        P("rep", "blk"),
        P("rep", "blk", None),
        P(),
        P(),
        P(),
        P("rep", "blk", None, None),
    )
    return jax.shard_map(
        functools.partial(local, mesh.shape["blk"], mesh.shape["rep"]),
        mesh=mesh,
        in_specs=placed,
        out_specs=(P("rep", "blk", None, None), P()),
        check_vma=False,
    )
```

```python
import functools
import math

import jax
import jax.numpy as jnp
from jax import lax
from jax.experimental import pallas as pl
from jax.experimental.pallas import tpu as pltpu
from jax.sharding import PartitionSpec as P

C = 128
CAP = 2
BLK = 4
SIB = 4
F32 = jnp.float32
BF16 = jnp.bfloat16
MESH = pl.DeviceIdType.MESH
WINDOW = 16
VMEM_LIMIT = 48 * 1024 * 1024


def at_blk(index):
    return {"blk": index}


def at_rep(index):
    return {"rep": index}


def fill_weights(w_ref, big):
    zero = jnp.zeros((C, C), BF16)
    for u in range(4):
        for dy in range(3):
            for dz in range(3):
                for half in range(2):
                    dx = u - half
                    tap = w_ref[dx * 9 + dy * 3 + dz] if 0 <= dx <= 2 else zero
                    big[u * 3 + dy, dz * C : dz * C + C, half * C : half * C + C] = tap


def fill_shifts(tab_ref, field, shifts):
    level = lax.broadcasted_iota(jnp.int32, (10, 8, C), 1)

    def body(i, carry):
        pair, plane = i // 10, i % 10
        first = jnp.where(plane == 0, 0, jnp.where(plane == 9, 2, 1))
        at = lax.rem(plane + 7, 8)
        parts = []
        for j in range(2):
            base = (2 * pair + j) * 27 + first * 9
            cells = []
            for c in range(3):
                low = field[tab_ref[base + c], at, 48:64].astype(F32)[8:16]
                mid = field[tab_ref[base + 3 + c], at].astype(F32)
                high = field[tab_ref[base + 6 + c], at, 0:16].astype(F32)[0:8]
                cells.append(jnp.concatenate([low, mid, high], axis=0).reshape(10, 8, C))
            parts.append(
                (
                    pltpu.roll(jnp.where(level == 7, cells[0], cells[1]), 1, 1),
                    cells[1],
                    pltpu.roll(jnp.where(level == 0, cells[2], cells[1]), 7, 1),
                )
            )
        for c in range(3):
            both = jnp.concatenate([parts[0][c], parts[1][c]], axis=1).astype(BF16)
            shifts[pair, lax.rem(plane, 2), plane // 2, :, :, c * C : c * C + C] = both
        return carry

    lax.fori_loop(0, 20, body, 0)


def operand(shifts, pair, u, dy):
    return shifts[pair, u % 2, u // 2 : u // 2 + 4, dy : dy + 8].reshape(512, 3 * C)


def convolve(shifts, big, pair):
    taps = [operand(shifts, pair, u, dy) for u in range(4) for dy in range(3)]
    total = jnp.dot(
        jnp.concatenate(taps, axis=1),
        big[...].reshape(36 * C, 2 * C),
        preferred_element_type=F32,
    )
    return total.reshape(4, 8, 2, 8, 2 * C)


def kernel(
    count,
    peers,
    reps,
    rows_hbm,
    owner_hbm,
    slot_hbm,
    neighbors_hbm,
    tiles_hbm,
    wenc_hbm,
    wcoarse_ref,
    wdec_hbm,
    cot_hbm,
    dec_ref,
    grad_ref,
    rows_s,
    owner_s,
    slot_s,
    neighbors_s,
    table_s,
    places_v,
    places_s,
    tiles,
    outgoing,
    outgoing_label,
    arrived,
    arrived_label,
    landed,
    field,
    encoded,
    shifts,
    big,
    big2,
    wenc,
    wdec,
    cot,
    cot_t,
    pooled,
    means,
    part,
    half_in,
    half,
    piece_in,
    piece_x,
    piece_own,
    ends,
    ends_in,
    ends2,
    ends2_in,
    load_sems,
    tile_sems,
    label_sems,
    halo_sems,
    encoded_sems,
    sibling_sems,
    mean_sems,
    core_sems,
    plane_sems,
    x_sems,
    gather_sems,
    forward_sems,
):
    me = lax.axis_index("blk")
    rep = lax.axis_index("rep")
    chips = peers // 2
    side = math.isqrt(chips)
    core, chip = lax.rem(me, 2), me // 2
    chip_y, chip_z = lax.rem(chip, side), chip // side
    other = me + 1 - 2 * core
    right, left = lax.rem(me + 1, peers), lax.rem(me + peers - 1, peers)

    loads = [
        pltpu.make_async_copy(source, target, load_sems.at[i])
        for i, (source, target) in enumerate(
            [
                (owner_hbm, owner_s),
                (rows_hbm, rows_s),
                (slot_hbm, slot_s),
                (tiles_hbm, tiles),
                (neighbors_hbm, neighbors_s),
                (wenc_hbm, wenc),
                (wdec_hbm, wdec),
                (cot_hbm, cot),
            ]
        )
    ]
    for load in loads:
        load.start()

    def remote(source, target, send_sem, recv_sem, where):
        return pltpu.make_async_remote_copy(
            src_ref=source,
            dst_ref=target,
            send_sem=send_sem,
            recv_sem=recv_sem,
            device_id=where,
            device_id_type=MESH,
        )

    def drain(ref, sem):
        pltpu.make_async_copy(ref, ref, sem).wait()

    turn = lax.rem(me, SIB)
    across = me - turn + lax.rem(turn + 2, SIB)

    def plane_peer(step):
        return 2 * lax.rem(chip + step, chips) + core

    def rep_peer(step):
        return lax.rem(rep + step, reps)

    barrier = pltpu.get_barrier_semaphore()

    def greet(step, carry):
        pl.semaphore_signal(
            barrier, inc=1, device_id=at_blk(lax.rem(me + step, peers)), device_id_type=MESH
        )
        return carry

    lax.fori_loop(1, peers, greet, 0)
    for step in range(1, reps):
        pl.semaphore_signal(
            barrier, inc=1, device_id=at_rep(rep_peer(step)), device_id_type=MESH
        )

    loads[0].wait()
    lane = lax.broadcasted_iota(jnp.int32, (8, C), 1)

    def note(t, carry):
        first, second = carry
        hit = lane == owner_s[0, t]
        second = jnp.where(hit & (first >= 0), t, second)
        first = jnp.where(hit & (first < 0), t, first)
        return first, second

    none = jnp.full((8, C), -1, jnp.int32)
    first, second = lax.fori_loop(0, count, note, (none, none))
    places_v[...] = jnp.where(lax.broadcasted_iota(jnp.int32, (8, C), 0) == 0, first, second)
    move = pltpu.make_async_copy(places_v, places_s, load_sems.at[8])
    move.start()
    loads[1].wait()
    loads[2].wait()
    move.wait()
    loads[3].wait()
    row = lax.broadcasted_iota(jnp.int32, (C, C), 0)

    def bucket(owner):
        for rank in range(CAP):
            tile = places_s[rank, owner]
            at = jnp.maximum(tile, 0)
            live = jnp.where(tile >= 0, rows_s[0, at], 0)
            outgoing[owner, rank] = jnp.where(row < live, tiles[at].astype(F32), 0.0).astype(BF16)
            outgoing_label[owner, rank : rank + 1] = jnp.full((1, C), slot_s[0, at], jnp.int32)

    def chip_beside(step, sign):
        k = step // 2
        move_y = lax.rem(k, side)
        move_z = lax.rem(k // side + move_y, side)
        return side * lax.rem(chip_z + side + sign * move_z, side) + lax.rem(
            chip_y + side + sign * move_y, side
        )

    def target_of(step):
        return 2 * chip_beside(step, 1 - 2 * core) + lax.rem(core + step, 2)

    def source_of(step):
        from_core = lax.rem(core + step, 2)
        return 2 * chip_beside(step, 2 * from_core - 1) + from_core

    def label_move(step):
        peer = target_of(step)
        return remote(
            outgoing_label.at[peer],
            arrived_label.at[me],
            label_sems.at[0],
            label_sems.at[step],
            at_blk(peer),
        )

    def tile_move(step):
        peer = target_of(step)
        return remote(
            outgoing.at[peer], arrived.at[me], tile_sems.at[0], tile_sems.at[step], at_blk(peer)
        )

    pl.semaphore_wait(barrier, peers - 1 + reps - 1)

    def step_of(i):
        return 1 + lax.rem(i + 1, peers - 1)

    def send(i, carry):
        step = step_of(i)
        bucket(target_of(step))
        label_move(step).start()
        tile_move(step).start()
        return carry

    lax.fori_loop(0, WINDOW, send, 0)
    bucket(me)

    landed[...] = jnp.zeros_like(landed)

    def land(labels, tiles_at):
        rows = [labels[rank : rank + 1] for rank in range(CAP)]
        for at in range(0, C, 32):
            pieces = [tiles_at[rank, at : at + 32].astype(F32) for rank in range(CAP)]
            for quarter in range(4 * BLK):
                total = landed[quarter, at : at + 32]
                for rank in range(CAP):
                    total = total + jnp.where(rows[rank] == quarter, pieces[rank], 0.0)
                landed[quarter, at : at + 32] = total

    land(outgoing_label[me], outgoing.at[me])
    loads[4].wait()

    def look(block, carry):
        for column in range(27):
            entry = neighbors_s[block, column]
            beside = me + entry // BLK - 1
            keep = (entry >= 0) & (beside >= 0) & (beside < peers)
            table_s[block * 27 + column] = jnp.where(keep, entry, 3 * BLK)
        return carry

    lax.fori_loop(0, BLK, look, 0)
    field[3 * BLK] = jnp.zeros((8, 64, C), BF16)
    loads[5].wait()
    fill_weights(wenc, big)
    loads[6].wait()
    fill_weights(wdec, big2)
    loads[7].wait()
    for pair in range(2):
        for parity in range(2):
            for xh in range(4):
                rows = [
                    cot[2 * pair + j, parity + 2 * xh].astype(F32).reshape(8, 1, 8, C)
                    for j in range(2)
                ]
                rows = jnp.concatenate(rows, axis=1).reshape(128, C)
                at = pair * 512 + xh * 128
                cot_t[parity * C : parity * C + C, at : at + 128] = rows.T.astype(BF16)

    def arrive(i, carry):
        step = step_of(i)
        source = source_of(step)
        drain(arrived.at[source], tile_sems.at[step])
        drain(arrived_label.at[source], label_sems.at[step])

        @pl.when(i + WINDOW < peers - 1)
        def _():
            send(i + WINDOW, 0)

        land(arrived_label[source], arrived.at[source])
        return carry

    lax.fori_loop(0, peers - 1, arrive, 0)
    for quarter in range(4 * BLK):
        planes = landed[quarter].astype(BF16).reshape(2, 64, C)
        x = 2 * (quarter % 4)
        field[BLK + quarter // 4, x : x + 2] = planes

    sub_row = lax.broadcasted_iota(jnp.int32, (8, C), 0)

    def pack_ends(source, block, ends):
        packed = []
        for x in range(1, 7):
            columns = source[BLK + block, x, 16:48].astype(F32).reshape(4, 8, C)
            total = columns[0]
            for i in range(4):
                total = jnp.where(sub_row == i, pltpu.roll(columns[i], i, 0), total)
                total = jnp.where(sub_row == 4 + i, pltpu.roll(columns[i], (i + 5) % 8, 0), total)
            packed.append(total)
        ends[block] = jnp.concatenate(packed, axis=0).astype(BF16)

    def unpack_ends(ends_in, target):
        def body(at, carry):
            side_of, block = at // BLK, lax.rem(at, BLK)
            packed = ends_in[side_of, block].astype(F32).reshape(6, 8, C)
            for x in range(1, 7):
                ends = packed[x - 1]
                columns = [
                    jnp.where(
                        sub_row == 7, pltpu.roll(ends, 3 - i, 0), pltpu.roll(ends, (8 - i) % 8, 0)
                    )
                    for i in range(4)
                ]
                target[2 * BLK * side_of + block, x, 16:48] = jnp.concatenate(
                    columns, axis=0
                ).astype(BF16)
            return carry

        lax.fori_loop(0, 2 * BLK, body, 0)

    def plane_moves(ref, first, count, sems):
        moves = []
        for base, where in ((0, right), (2 * BLK, left)):
            source, target = pl.ds(BLK + first, count), pl.ds(base + first, count)
            for x in (0, 7):
                moves.append(
                    remote(
                        ref.at[source, x], ref.at[target, x], sems.at[0], sems.at[1], at_blk(where)
                    )
                )
        return moves

    def row_moves(ref, sems):
        moves = []
        for base, where in ((0, right), (2 * BLK, left)):
            source, target = pl.ds(BLK, BLK), pl.ds(base, BLK)
            for y in (0, 48):
                at = pl.ds(y, 16)
                moves.append(
                    remote(
                        ref.at[source, 1:7, at],
                        ref.at[target, 1:7, at],
                        sems.at[2],
                        sems.at[3],
                        at_blk(where),
                    )
                )
        return moves

    def ends_moves(ends, ends_in, sems):
        return [
            remote(ends, ends_in.at[side_of], sems.at[4], sems.at[5], at_blk(where))
            for side_of, where in ((0, right), (1, left))
        ]

    def shell_drain(ref, ends_in, sems, which):
        drain(ref.at[0 : 2 * BLK, 0:2], sems.at[which])
        drain(ref.at[0 : 2 * BLK, 1:7, 0:32], sems.at[2 + which])
        drain(ends_in, sems.at[4 + which])

    for move in plane_moves(field, 0, BLK, halo_sems) + row_moves(field, halo_sems):
        move.start()

    def pack_own(block, carry):
        pack_ends(field, block, ends)
        return carry

    lax.fori_loop(0, BLK, pack_own, 0)
    for move in ends_moves(ends, ends_in, halo_sems):
        move.start()
    shell_drain(field, ends_in, halo_sems, 1)
    unpack_ends(ends_in, field)
    shell_drain(field, ends_in, halo_sems, 0)

    fill_shifts(table_s, field, shifts)
    level = lax.broadcasted_iota(jnp.int32, (8, C), 0)
    even = lax.rem(level, 2) == 0

    def sibling_move(pair, where, kind):
        piece = pooled.at[turn, pl.ds(2 * pair, 2)]
        return remote(
            piece, piece, sibling_sems.at[0], sibling_sems.at[1 + kind], at_blk(where)
        )

    def encode(pair, carry):
        total = convolve(shifts, big, pair)
        rounded = jnp.maximum(total, 0.0).astype(BF16).astype(F32)
        for j in range(2):
            for xh in range(4):
                for half_x in range(2):
                    encoded[BLK + 2 * pair + j, 2 * xh + half_x] = (
                        rounded[xh, :, j, :, half_x * C : half_x * C + C]
                        .reshape(64, C)
                        .astype(BF16)
                    )
                flat = rounded[xh, :, j, :, :C] + rounded[xh, :, j, :, C:]
                flat = flat.reshape(4, 2, 8, C)
                flat = flat[:, 0] + flat[:, 1]
                folded = [
                    flat[y]
                    + jnp.where(even, pltpu.roll(flat[y], 7, 0), pltpu.roll(flat[y], 1, 0))
                    for y in range(4)
                ]
                packed = [
                    jnp.where(even, folded[2 * y], folded[2 * y + 1]) * 0.125 for y in range(2)
                ]
                pooled[turn, 2 * pair + j, xh] = jnp.concatenate(packed, axis=0).astype(BF16)
        sibling_move(pair, across, pair).start()
        sibling_move(pair, other, 2).start()
        for move in plane_moves(encoded, 2 * pair, 2, encoded_sems):
            move.start()

        @pl.when(pair == 1)
        def _():
            for move in row_moves(encoded, encoded_sems):
                move.start()

        for j in range(2):
            pack_ends(encoded, 2 * pair + j, ends2)
        return carry

    lax.fori_loop(0, 2, encode, 0)
    for move in ends_moves(ends2, ends2_in, encoded_sems):
        move.start()

    opposite = lax.rem(turn + 2, SIB)
    for pair in range(2):
        piece = pooled.at[opposite, 2 * pair : 2 * pair + 2]
        drain(piece, sibling_sems.at[1 + pair])
        remote(piece, piece, sibling_sems.at[0], sibling_sems.at[4], at_blk(other)).start()
    drain(pooled.at[0], sibling_sems.at[3])
    drain(pooled.at[0], sibling_sems.at[4])
    mean = pooled[0].astype(F32)
    for step in range(1, SIB):
        mean = mean + pooled[step].astype(F32)
    means[1] = (mean * (1.0 / SIB)).astype(BF16)

    def mean_move(side_of, where):
        return remote(
            means.at[1], means.at[side_of], mean_sems.at[0], mean_sems.at[1], at_blk(where)
        )

    @pl.when(turn == SIB - 1)
    def _():
        mean_move(0, right).start()
        means[0] = means[1]

    @pl.when(turn == 0)
    def _():
        mean_move(2, left).start()
        means[2] = means[1]

    @pl.when((turn != 0) & (turn != SIB - 1))
    def _():
        means[0] = means[1]
        means[2] = means[1]

    def join(side_of):
        coarse = jnp.dot(
            means[side_of].reshape(BLK * 64, C), wcoarse_ref[...], preferred_element_type=F32
        )
        coarse = jnp.maximum(coarse, 0.0).reshape(BLK, 4, 2, 8, C)
        for block in range(BLK):
            for xh in range(4):
                ups = []
                for y in range(2):
                    tile = coarse[block, xh, y]
                    for up in (
                        jnp.where(even, tile, pltpu.roll(tile, 1, 0)),
                        jnp.where(even, pltpu.roll(tile, 7, 0), tile),
                    ):
                        ups += [up, up]
                ups = jnp.concatenate(ups, axis=0)
                for half_x in range(2):
                    x = 2 * xh + half_x
                    at = BLK * side_of + block
                    field[at, x] = (encoded[at, x].astype(F32) + ups).astype(BF16)

    join(1)

    @pl.when((turn == 0) | (turn == SIB - 1))
    def _():
        drain(means.at[1], mean_sems.at[0])
        drain(means.at[1], mean_sems.at[1])

    shell_drain(encoded, ends2_in, encoded_sems, 1)
    unpack_ends(ends2_in, encoded)
    join(0)
    join(2)
    fill_shifts(table_s, field, shifts)

    group_half = half_in.shape[1]
    piece_rows = piece_own.shape[1]
    active = group_half // piece_rows

    def swap(group):
        return remote(
            part.at[group, pl.ds(pl.multiple_of((1 - core) * group_half, 16), group_half)],
            half_in.at[group],
            core_sems.at[0],
            core_sems.at[1 + group],
            at_blk(other),
        )

    def piece_at(index):
        return pl.ds(pl.multiple_of(index * piece_rows, 16), piece_rows)

    def final_at(group, side_of, index):
        start = side_of * group_half + index * piece_rows
        start = start // (3 * C) * (9 * C) + group * (3 * C) + lax.rem(start, 3 * C)
        return pl.ds(pl.multiple_of(start, 16), piece_rows)

    def to_chip(step):
        return lax.rem(chip + step, chips)

    def from_chip(step):
        return lax.rem(chip + chips - step, chips)

    def scatter(group, step):
        return remote(
            half.at[group, piece_at(to_chip(step))],
            piece_in.at[group, chip],
            plane_sems.at[0],
            plane_sems.at[1 + group],
            at_blk(plane_peer(step)),
        )

    def gather(group, step):
        return remote(
            piece_own.at[group],
            grad_ref.at[final_at(group, core, chip)],
            gather_sems.at[0],
            gather_sems.at[1 + group if group < 2 else 2 + step],
            at_blk(plane_peer(step)),
        )

    def forward(group, index, source=None):
        at = final_at(group, core, index)
        return remote(
            grad_ref.at[at] if source is None else source,
            grad_ref.at[at], forward_sems.at[0],
            forward_sems.at[1],
            at_blk(other),

        )

    def each_step(action):
        def body(step, carry):
            action(step)
            return carry

        lax.fori_loop(1, chips, body, 0)

    def halve(group):
        drain(half_in.at[group], core_sems.at[1 + group])
        mine = pl.ds(pl.multiple_of(core * group_half, 16), group_half)
        half[group] = (part[group, mine].astype(F32) + half_in[group].astype(F32)).astype(BF16)

        def start(step):
            @pl.when(to_chip(step) < active)
            def _():
                scatter(group, step).start()

        each_step(start)

    def tap_row(dy, carry):
        @pl.when(dy < 3)
        def _():
            rows = [
                jnp.concatenate(
                    [
                        shifts[pair, u % 2, u // 2 : u // 2 + 4, pl.ds(dy, 8)].reshape(512, 3 * C)
                        for pair in range(2)
                    ],
                    axis=0,
                )
                for u in range(4)
            ]
            sums = jnp.dot(
                cot_t[...], jnp.concatenate(rows, axis=1), preferred_element_type=F32
            )
            for tap in range(9):
                at = tap * C
                total = sums[:C, at : at + C] + sums[C:, at + 3 * C : at + 4 * C]
                part[dy, at : at + C] = total.astype(BF16).T
            swap(dy).start()

        @pl.when(dy > 0)
        def _():
            halve(dy - 1)

        return carry

    lax.fori_loop(0, 4, tap_row, 0)

    def decode(pair):
        total = convolve(shifts, big2, pair)
        for j in range(2):
            for xh in range(4):
                for half_x in range(2):
                    x = 2 * xh + half_x
                    piece = total[xh, :, j, :, half_x * C : half_x * C + C].reshape(64, C)
                    block = 2 * pair + j
                    dec_ref[block, x] = (piece + field[BLK + block, x].astype(F32)).astype(BF16)

    def x_moves(group):
        return [
            remote(
                piece_x.at[group, rep],
                piece_x.at[group, rep],
                x_sems.at[0],
                x_sems.at[1 + group],
                at_rep(rep_peer(step)),
            )
            for step in range(1, reps)
        ]

    def reduce_piece(group):
        @pl.when(chip < active)
        def _():
            drain(piece_in.at[group, 0 : chips - 1], plane_sems.at[1 + group])
            piece_in[group, chip] = half[group, piece_at(chip)]

            def add(index, total):
                return total + piece_in[group, index].astype(F32)

            total = lax.fori_loop(0, chips, add, jnp.zeros((piece_rows, C), F32))
            piece_x[group, rep] = total.astype(BF16)
            for move in x_moves(group):
                move.start()

    def spread_piece(group):
        @pl.when(chip < active)
        def _():
            drain(piece_x.at[group, 0 : reps - 1], x_sems.at[1 + group])
            total = piece_x[group, 0].astype(F32)
            for index in range(1, reps):
                total = total + piece_x[group, index].astype(F32)
            piece_own[group] = total.astype(BF16)

            def start(step):
                gather(group, step).start()

            each_step(start)
            pltpu.make_async_copy(
                piece_own.at[group],
                grad_ref.at[final_at(group, core, chip)],
                load_sems.at[9 + group],
            ).start()
            forward(group, chip, piece_own.at[group]).start()

    def forward_pieces(group):
        if group < 2:

            @pl.when(chip < active)
            def _():
                drain(piece_in.at[group, 0 : active - 1], gather_sems.at[1 + group])

            @pl.when(chip >= active)
            def _():
                drain(piece_in.at[group, 0:active], gather_sems.at[1 + group])

        def come(step):
            @pl.when(from_chip(step) < active)
            def _():
                if group == 2:
                    drain(piece_own.at[group], gather_sems.at[2 + step])
                forward(group, from_chip(step)).start()

        each_step(come)

    def finish():
        drain(half_in, forward_sems.at[1])
        drain(half_in, forward_sems.at[0])
        drain(arrived_label.at[0 : peers - 1], label_sems.at[0])
        drain(arrived.at[0 : peers - 1], tile_sems.at[0])
        drain(pooled.at[0:3], sibling_sems.at[0])
        shell_drain(encoded, ends2_in, encoded_sems, 0)
        drain(half_in, core_sems.at[0])

        @pl.when(chip < active)
        def _():
            drain(piece_in.at[:, 0 : active - 1], plane_sems.at[0])
            drain(piece_x.at[:, 0 : reps - 1], x_sems.at[0])
            drain(piece_in.at[:, 0 : chips - 1], gather_sems.at[0])
            for group in range(3):
                drain(piece_own.at[group], load_sems.at[9 + group])

        @pl.when(chip >= active)
        def _():
            drain(piece_in.at[:, 0:active], plane_sems.at[0])

    decode(0)
    reduce_piece(0)
    reduce_piece(1)
    decode(1)
    reduce_piece(2)
    spread_piece(0)
    spread_piece(1)
    spread_piece(2)
    for group in range(3):
        forward_pieces(group)
    finish()


def local(
    peers,
    reps,
    tiles,
    tile_rows,
    tile_owner,
    tile_slot,
    neighbors,
    w_enc,
    w_coarse,
    w_dec,
    cotangent,
):
    count = tiles.shape[1]
    chips = peers // 2
    group_half = 9 * C // 2
    piece_rows = min(
        rows for rows in (16, 48, 64, 192, 576) if rows * chips >= group_half
    )
    vmem = pl.BlockSpec(memory_space=pltpu.VMEM)
    anywhere = pl.BlockSpec(memory_space=pltpu.HBM)
    dma = pltpu.SemaphoreType.DMA
    decoded, grads = pl.pallas_call(
        functools.partial(kernel, count, peers, reps),
        out_shape=(
            jax.ShapeDtypeStruct((BLK, 8, 64, C), BF16),
            jax.ShapeDtypeStruct((27 * C, C), BF16),
        ),
        in_specs=[anywhere] * 6 + [vmem] + [anywhere] * 2,
        out_specs=(vmem, anywhere),
        scratch_shapes=[
            pltpu.SMEM((1, count), jnp.int32),
            pltpu.SMEM((1, count), jnp.int32),
            pltpu.SMEM((1, count), jnp.int32),
            pltpu.SMEM((BLK, 27), jnp.int32),
            pltpu.SMEM((BLK * 27,), jnp.int32),
            pltpu.VMEM((8, C), jnp.int32),
            pltpu.SMEM((8, C), jnp.int32),
            pltpu.VMEM((count, C, C), BF16),
            pltpu.VMEM((peers, CAP, C, C), BF16),
            pltpu.VMEM((peers, CAP, C), jnp.int32),
            pltpu.VMEM((peers, CAP, C, C), BF16),
            pltpu.VMEM((peers, CAP, C), jnp.int32),
            pltpu.VMEM((4 * BLK, C, C), F32),
            pltpu.VMEM((3 * BLK + 1, 8, 64, C), BF16),
            pltpu.VMEM((3 * BLK, 8, 64, C), BF16),
            pltpu.VMEM((2, 2, 5, 10, 16, 3 * C), BF16),
            pltpu.VMEM((12, 3 * C, 2 * C), BF16),
            pltpu.VMEM((12, 3 * C, 2 * C), BF16),
            pltpu.VMEM((27, C, C), BF16),
            pltpu.VMEM((27, C, C), BF16),
            pltpu.VMEM((BLK, 8, 64, C), BF16),
            pltpu.VMEM((2 * C, 1024), BF16),
            pltpu.VMEM((SIB, BLK, 4, 16, C), BF16),
            pltpu.VMEM((3, BLK, 4, 16, C), BF16),
            pltpu.VMEM((3, 9 * C, C), BF16),
            pltpu.VMEM((3, group_half, C), BF16),
            pltpu.VMEM((3, group_half, C), BF16),
            pltpu.VMEM((3, chips, piece_rows, C), BF16),
            pltpu.VMEM((3, reps, piece_rows, C), BF16),
            pltpu.VMEM((3, piece_rows, C), BF16),
            pltpu.VMEM((BLK, 48, C), BF16),
            pltpu.VMEM((2, BLK, 48, C), BF16),
            pltpu.VMEM((BLK, 48, C), BF16),
            pltpu.VMEM((2, BLK, 48, C), BF16),
            dma((12,)),
            dma((peers,)),
            dma((peers,)),
            dma((6,)),
            dma((6,)),
            dma((5,)),
            dma((2,)),
            dma((4,)),
            dma((4,)),
            dma((4,)),
            dma((2 + chips,)),
            dma((2,)),
        ],
        compiler_params=pltpu.CompilerParams(
            collective_id=0, has_side_effects=True, vmem_limit_bytes=VMEM_LIMIT
        ),
        name="level",
    )(
        *[
            pltpu.with_memory_space_constraint(operand, pltpu.HBM)
            for operand in (
                tile_rows,
                tile_owner.reshape(1, count),
                tile_slot,
                neighbors[0],
                tiles[0],
                w_enc,
                w_coarse,
                w_dec,
                cotangent[0].reshape(BLK, 8, 64, C),
            )
        ]
    )
    return decoded.reshape(1, BLK, 512, C), grads.astype(F32).reshape(27, C, C)


def solution(mesh):
    placed = (
        P("rep", "blk", None, None),
        P("rep", "blk"),
        P("rep", "blk", None),
        P("rep", "blk"),
        P("rep", "blk", None),
        P(),
        P(),
        P(),
        P("rep", "blk", None, None),
    )
    return jax.shard_map(
        functools.partial(local, mesh.shape["blk"], mesh.shape["rep"]),
        mesh=mesh,
        in_specs=placed,
        out_specs=(P("rep", "blk", None, None), P()),
        check_vma=False,
    )
```

```python
import functools
import math

import jax
import jax.numpy as jnp
from jax import lax
from jax.experimental import pallas as pl
from jax.experimental.pallas import tpu as pltpu
from jax.sharding import PartitionSpec as P

C = 128
CAP = 2
BLK = 4
SIB = 4
F32 = jnp.float32
BF16 = jnp.bfloat16
MESH = pl.DeviceIdType.MESH
WINDOW = 16
VMEM_LIMIT = 48 * 1024 * 1024


def at_blk(index):
    return {"blk": index}


def at_rep(index):
    return {"rep": index}


def fill_weights(w_ref, big):
    zero = jnp.zeros((C, C), BF16)
    for u in range(4):
        for dy in range(3):
            for dz in range(3):
                for half in range(2):
                    dx = u - half
                    tap = w_ref[dx * 9 + dy * 3 + dz] if 0 <= dx <= 2 else zero
                    big[u * 3 + dy, dz * C : dz * C + C, half * C : half * C + C] = tap


def fill_shifts(tab_ref, field, shifts):
    level = lax.broadcasted_iota(jnp.int32, (10, 8, C), 1)

    def body(i, carry):
        pair, plane = i // 10, i % 10
        first = jnp.where(plane == 0, 0, jnp.where(plane == 9, 2, 1))
        at = lax.rem(plane + 7, 8)
        parts = []
        for j in range(2):
            base = (2 * pair + j) * 27 + first * 9
            cells = []
            for c in range(3):
                low = field[tab_ref[base + c], at, 48:64].astype(F32)[8:16]
                mid = field[tab_ref[base + 3 + c], at].astype(F32)
                high = field[tab_ref[base + 6 + c], at, 0:16].astype(F32)[0:8]
                cells.append(jnp.concatenate([low, mid, high], axis=0).reshape(10, 8, C))
            parts.append(
                (
                    pltpu.roll(jnp.where(level == 7, cells[0], cells[1]), 1, 1),
                    cells[1],
                    pltpu.roll(jnp.where(level == 0, cells[2], cells[1]), 7, 1),
                )
            )
        for c in range(3):
            both = jnp.concatenate([parts[0][c], parts[1][c]], axis=1).astype(BF16)
            shifts[pair, lax.rem(plane, 2), plane // 2, :, :, c * C : c * C + C] = both
        return carry

    lax.fori_loop(0, 20, body, 0)


def operand(shifts, pair, u, dy):
    return shifts[pair, u % 2, u // 2 : u // 2 + 4, dy : dy + 8].reshape(512, 3 * C)


def convolve(shifts, big, pair):
    taps = [operand(shifts, pair, u, dy) for u in range(4) for dy in range(3)]
    total = jnp.dot(
        jnp.concatenate(taps, axis=1),
        big[...].reshape(36 * C, 2 * C),
        preferred_element_type=F32,
    )
    return total.reshape(4, 8, 2, 8, 2 * C)


def kernel(
    count,
    peers,
    reps,
    rows_hbm,
    owner_hbm,
    slot_hbm,
    neighbors_hbm,
    tiles_hbm,
    wenc_hbm,
    wcoarse_ref,
    wdec_hbm,
    cot_hbm,
    dec_ref,
    grad_ref,
    rows_s,
    owner_s,
    slot_s,
    neighbors_s,
    table_s,
    places_v,
    places_s,
    tiles,
    outgoing,
    outgoing_label,
    arrived,
    arrived_label,
    landed,
    field,
    encoded,
    shifts,
    big,
    big2,
    wenc,
    wdec,
    cot,
    cot_t,
    pooled,
    sums,
    means,
    part,
    half_in,
    half,
    piece_in,
    piece_x,
    piece_own,
    ends,
    ends_in,
    ends2,
    ends2_in,
    load_sems,
    tile_sems,
    label_sems,
    halo_sems,
    encoded_sems,
    sibling_sems,
    core_sems,
    plane_sems,
    x_sems,
    gather_sems,
    forward_sems,
):
    me = lax.axis_index("blk")
    rep = lax.axis_index("rep")
    chips = peers // 2
    side = math.isqrt(chips)
    core, chip = lax.rem(me, 2), me // 2
    chip_y, chip_z = lax.rem(chip, side), chip // side
    other = me + 1 - 2 * core
    right, left = lax.rem(me + 1, peers), lax.rem(me + peers - 1, peers)

    loads = [
        pltpu.make_async_copy(source, target, load_sems.at[i])
        for i, (source, target) in enumerate(
            [
                (owner_hbm, owner_s),
                (rows_hbm, rows_s),
                (slot_hbm, slot_s),
                (tiles_hbm, tiles),
                (neighbors_hbm, neighbors_s),
                (wenc_hbm, wenc),
                (wdec_hbm, wdec),
                (cot_hbm, cot),
            ]
        )
    ]
    for load in loads:
        load.start()

    def remote(source, target, send_sem, recv_sem, where):
        return pltpu.make_async_remote_copy(
            src_ref=source,
            dst_ref=target,
            send_sem=send_sem,
            recv_sem=recv_sem,
            device_id=where,
            device_id_type=MESH,
        )

    def drain(ref, sem):
        pltpu.make_async_copy(ref, ref, sem).wait()

    turn = lax.rem(me, SIB)
    across = me - turn + lax.rem(turn + 2, SIB)

    def plane_peer(step):
        return 2 * lax.rem(chip + step, chips) + core

    def rep_peer(step):
        return lax.rem(rep + step, reps)

    barrier = pltpu.get_barrier_semaphore()

    def greet(step, carry):
        pl.semaphore_signal(
            barrier, inc=1, device_id=at_blk(lax.rem(me + step, peers)), device_id_type=MESH
        )
        return carry

    lax.fori_loop(1, peers, greet, 0)
    for step in range(1, reps):
        pl.semaphore_signal(
            barrier, inc=1, device_id=at_rep(rep_peer(step)), device_id_type=MESH
        )

    loads[0].wait()
    lane = lax.broadcasted_iota(jnp.int32, (8, C), 1)

    def note(t, carry):
        first, second = carry
        hit = lane == owner_s[0, t]
        second = jnp.where(hit & (first >= 0), t, second)
        first = jnp.where(hit & (first < 0), t, first)
        return first, second

    none = jnp.full((8, C), -1, jnp.int32)
    first, second = lax.fori_loop(0, count, note, (none, none))
    places_v[...] = jnp.where(lax.broadcasted_iota(jnp.int32, (8, C), 0) == 0, first, second)
    move = pltpu.make_async_copy(places_v, places_s, load_sems.at[8])
    move.start()
    loads[1].wait()
    loads[2].wait()
    move.wait()
    loads[3].wait()
    row = lax.broadcasted_iota(jnp.int32, (C, C), 0)

    def bucket(owner):
        for rank in range(CAP):
            tile = places_s[rank, owner]
            at = jnp.maximum(tile, 0)
            live = jnp.where(tile >= 0, rows_s[0, at], 0)
            outgoing[owner, rank] = jnp.where(row < live, tiles[at].astype(F32), 0.0).astype(BF16)
            outgoing_label[owner, rank : rank + 1] = jnp.full((1, C), slot_s[0, at], jnp.int32)

    def chip_beside(step, sign):
        k = step // 2
        move_y = lax.rem(k, side)
        move_z = lax.rem(k // side + move_y, side)
        return side * lax.rem(chip_z + side + sign * move_z, side) + lax.rem(
            chip_y + side + sign * move_y, side
        )

    def target_of(step):
        return 2 * chip_beside(step, 1 - 2 * core) + lax.rem(core + step, 2)

    def source_of(step):
        from_core = lax.rem(core + step, 2)
        return 2 * chip_beside(step, 2 * from_core - 1) + from_core

    def label_move(step):
        peer = target_of(step)
        return remote(
            outgoing_label.at[peer],
            arrived_label.at[me],
            label_sems.at[0],
            label_sems.at[step],
            at_blk(peer),
        )

    def tile_move(step):
        peer = target_of(step)
        return remote(
            outgoing.at[peer], arrived.at[me], tile_sems.at[0], tile_sems.at[step], at_blk(peer)
        )

    pl.semaphore_wait(barrier, peers - 1 + reps - 1)

    def step_of(i):
        return 1 + lax.rem(i + 1, peers - 1)

    def send(i, carry):
        step = step_of(i)
        bucket(target_of(step))
        label_move(step).start()
        tile_move(step).start()
        return carry

    lax.fori_loop(0, WINDOW, send, 0)
    bucket(me)

    landed[...] = jnp.zeros_like(landed)

    def land(labels, tiles_at):
        rows = [labels[rank : rank + 1] for rank in range(CAP)]
        for at in range(0, C, 32):
            pieces = [tiles_at[rank, at : at + 32].astype(F32) for rank in range(CAP)]
            for quarter in range(4 * BLK):
                total = landed[quarter, at : at + 32]
                for rank in range(CAP):
                    total = total + jnp.where(rows[rank] == quarter, pieces[rank], 0.0)
                landed[quarter, at : at + 32] = total

    land(outgoing_label[me], outgoing.at[me])
    loads[4].wait()

    def look(block, carry):
        for column in range(27):
            entry = neighbors_s[block, column]
            beside = me + entry // BLK - 1
            keep = (entry >= 0) & (beside >= 0) & (beside < peers)
            table_s[block * 27 + column] = jnp.where(keep, entry, 3 * BLK)
        return carry

    lax.fori_loop(0, BLK, look, 0)
    field[3 * BLK] = jnp.zeros((8, 64, C), BF16)
    loads[5].wait()
    fill_weights(wenc, big)
    loads[6].wait()
    fill_weights(wdec, big2)
    loads[7].wait()
    for pair in range(2):
        for parity in range(2):
            for xh in range(4):
                rows = [
                    cot[2 * pair + j, parity + 2 * xh].astype(F32).reshape(8, 1, 8, C)
                    for j in range(2)
                ]
                rows = jnp.concatenate(rows, axis=1).reshape(128, C)
                at = pair * 512 + xh * 128
                cot_t[parity * C : parity * C + C, at : at + 128] = rows.T.astype(BF16)

    def arrive(i, carry):
        step = step_of(i)
        source = source_of(step)
        drain(arrived.at[source], tile_sems.at[step])
        drain(arrived_label.at[source], label_sems.at[step])

        @pl.when(i + WINDOW < peers - 1)
        def _():
            send(i + WINDOW, 0)

        land(arrived_label[source], arrived.at[source])
        return carry

    lax.fori_loop(0, peers - 1, arrive, 0)
    for quarter in range(4 * BLK):
        planes = landed[quarter].astype(BF16).reshape(2, 64, C)
        x = 2 * (quarter % 4)
        field[BLK + quarter // 4, x : x + 2] = planes

    sub_row = lax.broadcasted_iota(jnp.int32, (8, C), 0)

    def pack_ends(source, block, ends):
        packed = []
        for x in range(1, 7):
            columns = source[BLK + block, x, 16:48].astype(F32).reshape(4, 8, C)
            total = columns[0]
            for i in range(4):
                total = jnp.where(sub_row == i, pltpu.roll(columns[i], i, 0), total)
                total = jnp.where(sub_row == 4 + i, pltpu.roll(columns[i], (i + 5) % 8, 0), total)
            packed.append(total)
        ends[block] = jnp.concatenate(packed, axis=0).astype(BF16)

    def unpack_ends(ends_in, target):
        def body(at, carry):
            side_of, block = at // BLK, lax.rem(at, BLK)
            packed = ends_in[side_of, block].astype(F32).reshape(6, 8, C)
            for x in range(1, 7):
                ends = packed[x - 1]
                columns = [
                    jnp.where(
                        sub_row == 7, pltpu.roll(ends, 3 - i, 0), pltpu.roll(ends, (8 - i) % 8, 0)
                    )
                    for i in range(4)
                ]
                target[2 * BLK * side_of + block, x, 16:48] = jnp.concatenate(
                    columns, axis=0
                ).astype(BF16)
            return carry

        lax.fori_loop(0, 2 * BLK, body, 0)

    def plane_moves(ref, first, count, sems):
        moves = []
        for base, where in ((0, right), (2 * BLK, left)):
            source, target = pl.ds(BLK + first, count), pl.ds(base + first, count)
            for x in (0, 7):
                moves.append(
                    remote(
                        ref.at[source, x], ref.at[target, x], sems.at[0], sems.at[1], at_blk(where)
                    )
                )
        return moves

    def row_moves(ref, first, count, sems):
        moves = []
        for base, where in ((0, right), (2 * BLK, left)):
            source, target = pl.ds(BLK + first, count), pl.ds(base + first, count)
            for y in (0, 48):
                at = pl.ds(y, 16)
                moves.append(
                    remote(
                        ref.at[source, 1:7, at],
                        ref.at[target, 1:7, at],
                        sems.at[2],
                        sems.at[3],
                        at_blk(where),
                    )
                )
        return moves

    def ends_moves(ends, ends_in, sems):
        return [
            remote(ends, ends_in.at[side_of], sems.at[4], sems.at[5], at_blk(where))
            for side_of, where in ((0, right), (1, left))
        ]

    def shell_drain(ref, ends_in, sems, which):
        drain(ref.at[0 : 2 * BLK, 0:2], sems.at[which])
        drain(ref.at[0 : 2 * BLK, 1:7, 0:32], sems.at[2 + which])
        drain(ends_in, sems.at[4 + which])

    for move in plane_moves(field, 0, BLK, halo_sems) + row_moves(field, 0, BLK, halo_sems):
        move.start()

    def pack_own(block, carry):
        pack_ends(field, block, ends)
        return carry

    lax.fori_loop(0, BLK, pack_own, 0)
    for move in ends_moves(ends, ends_in, halo_sems):
        move.start()
    shell_drain(field, ends_in, halo_sems, 1)
    unpack_ends(ends_in, field)
    shell_drain(field, ends_in, halo_sems, 0)

    fill_shifts(table_s, field, shifts)
    level = lax.broadcasted_iota(jnp.int32, (8, C), 0)
    even = lax.rem(level, 2) == 0

    in_group = turn // 2
    base = me - turn
    beyond = lax.rem(base + jnp.where(core == 0, peers - 1, SIB), peers)

    def swap_pooled(pair):
        piece = pooled.at[core, pl.ds(2 * pair, 2)]
        return remote(
            piece, piece, sibling_sems.at[0], sibling_sems.at[1 + pair], at_blk(other)
        )

    def sum_chip(pair):
        at = pl.ds(2 * pair, 2)
        drain(pooled.at[0, 0:2], sibling_sems.at[1 + pair])
        sums[2 + in_group, at] = (
            pooled[0, at].astype(F32) + pooled[1, at].astype(F32)
        ).astype(BF16)
        source = sums.at[2 + in_group, at]
        remote(
            source, source, sibling_sems.at[0], sibling_sems.at[3 + pair], at_blk(across)
        ).start()
        remote(
            source,
            sums.at[4 * (1 - core) + in_group, at],
            sibling_sems.at[0],
            sibling_sems.at[5],
            at_blk(beyond),
        ).start()

    def encode(pair, carry):
        total = convolve(shifts, big, pair)

        @pl.when(pair == 1)
        def _():
            sum_chip(0)

        rounded = jnp.maximum(total, 0.0).astype(BF16).astype(F32)
        for j in range(2):
            for xh in range(4):
                for half_x in range(2):
                    encoded[BLK + 2 * pair + j, 2 * xh + half_x] = (
                        rounded[xh, :, j, :, half_x * C : half_x * C + C]
                        .reshape(64, C)
                        .astype(BF16)
                    )
                flat = rounded[xh, :, j, :, :C] + rounded[xh, :, j, :, C:]
                flat = flat.reshape(4, 2, 8, C)
                flat = flat[:, 0] + flat[:, 1]
                folded = [
                    flat[y]
                    + jnp.where(even, pltpu.roll(flat[y], 7, 0), pltpu.roll(flat[y], 1, 0))
                    for y in range(4)
                ]
                packed = [
                    jnp.where(even, folded[2 * y], folded[2 * y + 1]) * 0.125 for y in range(2)
                ]
                pooled[core, 2 * pair + j, xh] = jnp.concatenate(packed, axis=0).astype(BF16)
        swap_pooled(pair).start()
        for move in plane_moves(encoded, 2 * pair, 2, encoded_sems):
            move.start()

        @pl.when(pair == 0)
        def _():
            for move in row_moves(encoded, 0, 2, encoded_sems):
                move.start()

        for j in range(2):
            pack_ends(encoded, 2 * pair + j, ends2)
        return carry

    lax.fori_loop(0, 2, encode, 0)
    sum_chip(1)
    for move in row_moves(encoded, 2, 2, encoded_sems) + ends_moves(ends2, ends2_in, encoded_sems):
        move.start()

    def mean_of(group):
        total = sums[2 * group].astype(F32) + sums[2 * group + 1].astype(F32)
        means[group] = (total * (1.0 / SIB)).astype(BF16)

    for pair in range(2):
        drain(pooled.at[0, 0:2], sibling_sems.at[3 + pair])
    mean_of(1)

    def join(side_of):
        coarse = jnp.dot(
            means[side_of].reshape(BLK * 64, C), wcoarse_ref[...], preferred_element_type=F32
        )
        coarse = jnp.maximum(coarse, 0.0).reshape(BLK, 4, 2, 8, C)
        for block in range(BLK):
            for xh in range(4):
                ups = []
                for y in range(2):
                    tile = coarse[block, xh, y]
                    for up in (
                        jnp.where(even, tile, pltpu.roll(tile, 1, 0)),
                        jnp.where(even, pltpu.roll(tile, 7, 0), tile),
                    ):
                        ups += [up, up]
                ups = jnp.concatenate(ups, axis=0)
                for half_x in range(2):
                    x = 2 * xh + half_x
                    at = BLK * side_of + block
                    field[at, x] = (encoded[at, x].astype(F32) + ups).astype(BF16)

    join(1)

    means[0] = means[1]
    means[2] = means[1]

    @pl.when((turn == 0) | (turn == SIB - 1))
    def _():
        drain(sums.at[0:2], sibling_sems.at[5])

    @pl.when(turn == 0)
    def _():
        mean_of(0)

    @pl.when(turn == SIB - 1)
    def _():
        mean_of(2)

    shell_drain(encoded, ends2_in, encoded_sems, 1)
    unpack_ends(ends2_in, encoded)
    join(0)
    join(2)
    fill_shifts(table_s, field, shifts)

    group_half = half_in.shape[1]
    piece_rows = piece_own.shape[1]
    active = group_half // piece_rows

    def swap(group):
        return remote(
            part.at[group, pl.ds(pl.multiple_of((1 - core) * group_half, 16), group_half)],
            half_in.at[group],
            core_sems.at[0],
            core_sems.at[1 + group],
            at_blk(other),
        )

    def piece_at(index):
        return pl.ds(pl.multiple_of(index * piece_rows, 16), piece_rows)

    def final_at(group, side_of, index):
        start = side_of * group_half + index * piece_rows
        start = start // (3 * C) * (9 * C) + group * (3 * C) + lax.rem(start, 3 * C)
        return pl.ds(pl.multiple_of(start, 16), piece_rows)

    def to_chip(step):
        return lax.rem(chip + step, chips)

    def from_chip(step):
        return lax.rem(chip + chips - step, chips)

    def scatter(group, step):
        return remote(
            half.at[group, piece_at(to_chip(step))],
            piece_in.at[group, chip],
            plane_sems.at[0],
            plane_sems.at[1 + group],
            at_blk(plane_peer(step)),
        )

    def gather(group, step):
        return remote(
            piece_own.at[group],
            grad_ref.at[final_at(group, core, chip)],
            gather_sems.at[0],
            gather_sems.at[1 + group if group < 2 else 2 + step],
            at_blk(plane_peer(step)),
        )

    def forward(group, index, source=None):
        at = final_at(group, core, index)
        return remote(
            grad_ref.at[at] if source is None else source,
            grad_ref.at[at], forward_sems.at[0],
            forward_sems.at[1],
            at_blk(other),

        )

    def each_step(action):
        def body(step, carry):
            action(step)
            return carry

        lax.fori_loop(1, chips, body, 0)

    def halve(group):
        drain(half_in.at[group], core_sems.at[1 + group])
        mine = pl.ds(pl.multiple_of(core * group_half, 16), group_half)
        half[group] = (part[group, mine].astype(F32) + half_in[group].astype(F32)).astype(BF16)

        def start(step):
            @pl.when(to_chip(step) < active)
            def _():
                scatter(group, step).start()

        each_step(start)

    def tap_row(dy, carry):
        @pl.when(dy < 3)
        def _():
            rows = [
                jnp.concatenate(
                    [
                        shifts[pair, u % 2, u // 2 : u // 2 + 4, pl.ds(dy, 8)].reshape(512, 3 * C)
                        for pair in range(2)
                    ],
                    axis=0,
                )
                for u in range(4)
            ]
            taps = jnp.dot(
                cot_t[...], jnp.concatenate(rows, axis=1), preferred_element_type=F32
            )
            for tap in range(9):
                at = tap * C
                total = taps[:C, at : at + C] + taps[C:, at + 3 * C : at + 4 * C]
                part[dy, at : at + C] = total.astype(BF16).T
            swap(dy).start()

        @pl.when(dy > 0)
        def _():
            halve(dy - 1)

        return carry

    lax.fori_loop(0, 4, tap_row, 0)

    def decode(pair):
        total = convolve(shifts, big2, pair)
        for j in range(2):
            for xh in range(4):
                for half_x in range(2):
                    x = 2 * xh + half_x
                    piece = total[xh, :, j, :, half_x * C : half_x * C + C].reshape(64, C)
                    block = 2 * pair + j
                    dec_ref[block, x] = (piece + field[BLK + block, x].astype(F32)).astype(BF16)

    def x_moves(group):
        return [
            remote(
                piece_x.at[group, rep],
                piece_x.at[group, rep],
                x_sems.at[0],
                x_sems.at[1 + group],
                at_rep(rep_peer(step)),
            )
            for step in range(1, reps)
        ]

    def reduce_piece(group):
        @pl.when(chip < active)
        def _():
            drain(piece_in.at[group, 0 : chips - 1], plane_sems.at[1 + group])
            piece_in[group, chip] = half[group, piece_at(chip)]

            def add(index, total):
                return total + piece_in[group, index].astype(F32)

            total = lax.fori_loop(0, chips, add, jnp.zeros((piece_rows, C), F32))
            piece_x[group, rep] = total.astype(BF16)
            for move in x_moves(group):
                move.start()

    def spread_piece(group):
        @pl.when(chip < active)
        def _():
            drain(piece_x.at[group, 0 : reps - 1], x_sems.at[1 + group])
            total = piece_x[group, 0].astype(F32)
            for index in range(1, reps):
                total = total + piece_x[group, index].astype(F32)
            piece_own[group] = total.astype(BF16)

            def start(step):
                gather(group, step).start()

            each_step(start)
            pltpu.make_async_copy(
                piece_own.at[group],
                grad_ref.at[final_at(group, core, chip)],
                load_sems.at[9 + group],
            ).start()
            forward(group, chip, piece_own.at[group]).start()

    def forward_pieces(group):
        if group < 2:

            @pl.when(chip < active)
            def _():
                drain(piece_in.at[group, 0 : active - 1], gather_sems.at[1 + group])

            @pl.when(chip >= active)
            def _():
                drain(piece_in.at[group, 0:active], gather_sems.at[1 + group])

        def come(step):
            @pl.when(from_chip(step) < active)
            def _():
                if group == 2:
                    drain(piece_own.at[group], gather_sems.at[2 + step])
                forward(group, from_chip(step)).start()

        each_step(come)

    def finish():
        drain(half_in, forward_sems.at[1])
        drain(half_in, forward_sems.at[0])
        drain(arrived_label.at[0 : peers - 1], label_sems.at[0])
        drain(arrived.at[0 : peers - 1], tile_sems.at[0])
        drain(sums.at[0:3], sibling_sems.at[0])
        shell_drain(encoded, ends2_in, encoded_sems, 0)
        drain(half_in, core_sems.at[0])

        @pl.when(chip < active)
        def _():
            drain(piece_in.at[:, 0 : active - 1], plane_sems.at[0])
            drain(piece_x.at[:, 0 : reps - 1], x_sems.at[0])
            drain(piece_in.at[:, 0 : chips - 1], gather_sems.at[0])
            for group in range(3):
                drain(piece_own.at[group], load_sems.at[9 + group])

        @pl.when(chip >= active)
        def _():
            drain(piece_in.at[:, 0:active], plane_sems.at[0])

    decode(0)
    reduce_piece(0)
    reduce_piece(1)
    decode(1)
    reduce_piece(2)
    spread_piece(0)
    spread_piece(1)
    spread_piece(2)
    for group in range(3):
        forward_pieces(group)
    finish()


def local(
    peers,
    reps,
    tiles,
    tile_rows,
    tile_owner,
    tile_slot,
    neighbors,
    w_enc,
    w_coarse,
    w_dec,
    cotangent,
):
    count = tiles.shape[1]
    chips = peers // 2
    group_half = 9 * C // 2
    piece_rows = min(
        rows for rows in (16, 48, 64, 192, 576) if rows * chips >= group_half
    )
    vmem = pl.BlockSpec(memory_space=pltpu.VMEM)
    anywhere = pl.BlockSpec(memory_space=pltpu.HBM)
    dma = pltpu.SemaphoreType.DMA
    decoded, grads = pl.pallas_call(
        functools.partial(kernel, count, peers, reps),
        out_shape=(
            jax.ShapeDtypeStruct((BLK, 8, 64, C), BF16),
            jax.ShapeDtypeStruct((27 * C, C), BF16),
        ),
        in_specs=[anywhere] * 6 + [vmem] + [anywhere] * 2,
        out_specs=(vmem, anywhere),
        scratch_shapes=[
            pltpu.SMEM((1, count), jnp.int32),
            pltpu.SMEM((1, count), jnp.int32),
            pltpu.SMEM((1, count), jnp.int32),
            pltpu.SMEM((BLK, 27), jnp.int32),
            pltpu.SMEM((BLK * 27,), jnp.int32),
            pltpu.VMEM((8, C), jnp.int32),
            pltpu.SMEM((8, C), jnp.int32),
            pltpu.VMEM((count, C, C), BF16),
            pltpu.VMEM((peers, CAP, C, C), BF16),
            pltpu.VMEM((peers, CAP, C), jnp.int32),
            pltpu.VMEM((peers, CAP, C, C), BF16),
            pltpu.VMEM((peers, CAP, C), jnp.int32),
            pltpu.VMEM((4 * BLK, C, C), F32),
            pltpu.VMEM((3 * BLK + 1, 8, 64, C), BF16),
            pltpu.VMEM((3 * BLK, 8, 64, C), BF16),
            pltpu.VMEM((2, 2, 5, 10, 16, 3 * C), BF16),
            pltpu.VMEM((12, 3 * C, 2 * C), BF16),
            pltpu.VMEM((12, 3 * C, 2 * C), BF16),
            pltpu.VMEM((27, C, C), BF16),
            pltpu.VMEM((27, C, C), BF16),
            pltpu.VMEM((BLK, 8, 64, C), BF16),
            pltpu.VMEM((2 * C, 1024), BF16),
            pltpu.VMEM((2, BLK, 4, 16, C), BF16),
            pltpu.VMEM((6, BLK, 4, 16, C), BF16),
            pltpu.VMEM((3, BLK, 4, 16, C), BF16),
            pltpu.VMEM((3, 9 * C, C), BF16),
            pltpu.VMEM((3, group_half, C), BF16),
            pltpu.VMEM((3, group_half, C), BF16),
            pltpu.VMEM((3, chips, piece_rows, C), BF16),
            pltpu.VMEM((3, reps, piece_rows, C), BF16),
            pltpu.VMEM((3, piece_rows, C), BF16),
            pltpu.VMEM((BLK, 48, C), BF16),
            pltpu.VMEM((2, BLK, 48, C), BF16),
            pltpu.VMEM((BLK, 48, C), BF16),
            pltpu.VMEM((2, BLK, 48, C), BF16),
            dma((12,)),
            dma((peers,)),
            dma((peers,)),
            dma((6,)),
            dma((6,)),
            dma((6,)),
            dma((4,)),
            dma((4,)),
            dma((4,)),
            dma((2 + chips,)),
            dma((2,)),
        ],
        compiler_params=pltpu.CompilerParams(
            collective_id=0, has_side_effects=True, vmem_limit_bytes=VMEM_LIMIT
        ),
        name="level",
    )(
        *[
            pltpu.with_memory_space_constraint(operand, pltpu.HBM)
            for operand in (
                tile_rows,
                tile_owner.reshape(1, count),
                tile_slot,
                neighbors[0],
                tiles[0],
                w_enc,
                w_coarse,
                w_dec,
                cotangent[0].reshape(BLK, 8, 64, C),
            )
        ]
    )
    return decoded.reshape(1, BLK, 512, C), grads.astype(F32).reshape(27, C, C)


def solution(mesh):
    placed = (
        P("rep", "blk", None, None),
        P("rep", "blk"),
        P("rep", "blk", None),
        P("rep", "blk"),
        P("rep", "blk", None),
        P(),
        P(),
        P(),
        P("rep", "blk", None, None),
    )
    return jax.shard_map(
        functools.partial(local, mesh.shape["blk"], mesh.shape["rep"]),
        mesh=mesh,
        in_specs=placed,
        out_specs=(P("rep", "blk", None, None), P()),
        check_vma=False,
    )
```

```python
import functools
import math

import jax
import jax.numpy as jnp
from jax import lax
from jax.experimental import pallas as pl
from jax.experimental.pallas import tpu as pltpu
from jax.sharding import PartitionSpec as P

C = 128
CAP = 2
BLK = 4
SIB = 4
F32 = jnp.float32
BF16 = jnp.bfloat16
MESH = pl.DeviceIdType.MESH
WINDOW = 16
MOVES_Y = (1, 1, 2, 1, 0, 2, 1, 3, 3, 2, 0, 2, 3, 3, 0)
MOVES_Z = (1, 3, 2, 0, 1, 1, 2, 1, 3, 0, 2, 3, 2, 0, 3)
VMEM_LIMIT = 48 * 1024 * 1024


def at_blk(index):
    return {"blk": index}


def at_rep(index):
    return {"rep": index}


def fill_weights(w_ref, big):
    zero = jnp.zeros((C, C), BF16)
    for u in range(4):
        for dy in range(3):
            for dz in range(3):
                for half in range(2):
                    dx = u - half
                    tap = w_ref[dx * 9 + dy * 3 + dz] if 0 <= dx <= 2 else zero
                    big[u * 3 + dy, dz * C : dz * C + C, half * C : half * C + C] = tap


def fill_shifts(tab_ref, field, shifts):
    level = lax.broadcasted_iota(jnp.int32, (10, 8, C), 1)

    def body(i, carry):
        pair, plane = i // 10, i % 10
        first = jnp.where(plane == 0, 0, jnp.where(plane == 9, 2, 1))
        at = lax.rem(plane + 7, 8)
        parts = []
        for j in range(2):
            base = (2 * pair + j) * 27 + first * 9
            cells = []
            for c in range(3):
                low = field[tab_ref[base + c], at, 48:64].astype(F32)[8:16]
                mid = field[tab_ref[base + 3 + c], at].astype(F32)
                high = field[tab_ref[base + 6 + c], at, 0:16].astype(F32)[0:8]
                cells.append(jnp.concatenate([low, mid, high], axis=0).reshape(10, 8, C))
            parts.append(
                (
                    pltpu.roll(jnp.where(level == 7, cells[0], cells[1]), 1, 1),
                    cells[1],
                    pltpu.roll(jnp.where(level == 0, cells[2], cells[1]), 7, 1),
                )
            )
        for c in range(3):
            both = jnp.concatenate([parts[0][c], parts[1][c]], axis=1).astype(BF16)
            shifts[pair, lax.rem(plane, 2), plane // 2, :, :, c * C : c * C + C] = both
        return carry

    lax.fori_loop(0, 20, body, 0)


def operand(shifts, pair, u, dy):
    return shifts[pair, u % 2, u // 2 : u // 2 + 4, dy : dy + 8].reshape(512, 3 * C)


def convolve(shifts, big, pair):
    taps = [operand(shifts, pair, u, dy) for u in range(4) for dy in range(3)]
    total = jnp.dot(
        jnp.concatenate(taps, axis=1),
        big[...].reshape(36 * C, 2 * C),
        preferred_element_type=F32,
    )
    return total.reshape(4, 8, 2, 8, 2 * C)


def kernel(
    count,
    peers,
    reps,
    rows_hbm,
    owner_hbm,
    slot_hbm,
    neighbors_hbm,
    tiles_hbm,
    wenc_hbm,
    wcoarse_ref,
    wdec_hbm,
    cot_hbm,
    dec_ref,
    grad_ref,
    rows_s,
    owner_s,
    slot_s,
    neighbors_s,
    table_s,
    places_v,
    places_s,
    tiles,
    outgoing,
    outgoing_label,
    arrived,
    arrived_label,
    landed,
    field,
    encoded,
    shifts,
    big,
    big2,
    wenc,
    wdec,
    cot,
    cot_t,
    pooled,
    sums,
    means,
    part,
    half_in,
    half,
    piece_in,
    piece_x,
    piece_own,
    ends,
    ends_in,
    ends2,
    ends2_in,
    load_sems,
    tile_sems,
    label_sems,
    halo_sems,
    encoded_sems,
    sibling_sems,
    core_sems,
    plane_sems,
    x_sems,
    gather_sems,
    forward_sems,
):
    me = lax.axis_index("blk")
    rep = lax.axis_index("rep")
    chips = peers // 2
    side = math.isqrt(chips)
    core, chip = lax.rem(me, 2), me // 2
    chip_y, chip_z = lax.rem(chip, side), chip // side
    other = me + 1 - 2 * core
    right, left = lax.rem(me + 1, peers), lax.rem(me + peers - 1, peers)

    loads = [
        pltpu.make_async_copy(source, target, load_sems.at[i])
        for i, (source, target) in enumerate(
            [
                (owner_hbm, owner_s),
                (rows_hbm, rows_s),
                (slot_hbm, slot_s),
                (tiles_hbm, tiles),
                (neighbors_hbm, neighbors_s),
                (wenc_hbm, wenc),
                (wdec_hbm, wdec),
                (cot_hbm, cot),
            ]
        )
    ]
    for load in loads:
        load.start()

    def remote(source, target, send_sem, recv_sem, where):
        return pltpu.make_async_remote_copy(
            src_ref=source,
            dst_ref=target,
            send_sem=send_sem,
            recv_sem=recv_sem,
            device_id=where,
            device_id_type=MESH,
        )

    def drain(ref, sem):
        pltpu.make_async_copy(ref, ref, sem).wait()

    turn = lax.rem(me, SIB)
    across = me - turn + lax.rem(turn + 2, SIB)

    def plane_peer(step):
        return 2 * lax.rem(chip + step, chips) + core

    def rep_peer(step):
        return lax.rem(rep + step, reps)

    barrier = pltpu.get_barrier_semaphore()

    def greet(step, carry):
        pl.semaphore_signal(
            barrier, inc=1, device_id=at_blk(lax.rem(me + step, peers)), device_id_type=MESH
        )
        return carry

    lax.fori_loop(1, peers, greet, 0)
    for step in range(1, reps):
        pl.semaphore_signal(
            barrier, inc=1, device_id=at_rep(rep_peer(step)), device_id_type=MESH
        )

    loads[0].wait()
    lane = lax.broadcasted_iota(jnp.int32, (8, C), 1)

    def note(t, carry):
        first, second = carry
        hit = lane == owner_s[0, t]
        second = jnp.where(hit & (first >= 0), t, second)
        first = jnp.where(hit & (first < 0), t, first)
        return first, second

    none = jnp.full((8, C), -1, jnp.int32)
    first, second = lax.fori_loop(0, count, note, (none, none))
    places_v[...] = jnp.where(lax.broadcasted_iota(jnp.int32, (8, C), 0) == 0, first, second)
    move = pltpu.make_async_copy(places_v, places_s, load_sems.at[8])
    move.start()
    loads[1].wait()
    loads[2].wait()
    move.wait()
    loads[3].wait()
    row = lax.broadcasted_iota(jnp.int32, (C, C), 0)

    def bucket(owner):
        for rank in range(CAP):
            tile = places_s[rank, owner]
            at = jnp.maximum(tile, 0)
            live = jnp.where(tile >= 0, rows_s[0, at], 0)
            outgoing[owner, rank] = jnp.where(row < live, tiles[at].astype(F32), 0.0).astype(BF16)
            outgoing_label[owner, rank : rank + 1] = jnp.full((1, C), slot_s[0, at], jnp.int32)

    def pick(table, k):
        value = 0
        for at, entry in enumerate(table):
            value = jnp.where(k == at, entry, value)
        return value

    def chip_beside(step, sign):
        k = lax.rem(step - 1, chips - 1)
        if side == 4:
            move_y, move_z = pick(MOVES_Y, k), pick(MOVES_Z, k)
        else:
            move_y = lax.rem(k + 1, side)
            move_z = lax.rem((k + 1) // side + move_y, side)
        away = step < peers - 1
        move_y, move_z = jnp.where(away, move_y, 0), jnp.where(away, move_z, 0)
        return side * lax.rem(chip_z + side + sign * move_z, side) + lax.rem(
            chip_y + side + sign * move_y, side
        )

    def turned(step):
        return jnp.where(step < chips, core, 1 - core)

    def target_of(step):
        return 2 * chip_beside(step, 1 - 2 * core) + turned(step)

    def source_of(step):
        from_core = turned(step)
        return 2 * chip_beside(step, 2 * from_core - 1) + from_core

    def label_move(step):
        peer = target_of(step)
        return remote(
            outgoing_label.at[peer],
            arrived_label.at[me],
            label_sems.at[0],
            label_sems.at[step],
            at_blk(peer),
        )

    def tile_move(step):
        peer = target_of(step)
        return remote(
            outgoing.at[peer], arrived.at[me], tile_sems.at[0], tile_sems.at[step], at_blk(peer)
        )

    pl.semaphore_wait(barrier, peers - 1 + reps - 1)

    def step_of(i):
        return 1 + i

    def send(i, carry):
        step = step_of(i)
        bucket(target_of(step))
        label_move(step).start()
        tile_move(step).start()
        return carry

    lax.fori_loop(0, WINDOW, send, 0)
    bucket(me)

    landed[...] = jnp.zeros_like(landed)

    def land(labels, tiles_at):
        rows = [labels[rank : rank + 1] for rank in range(CAP)]
        for at in range(0, C, 32):
            pieces = [tiles_at[rank, at : at + 32].astype(F32) for rank in range(CAP)]
            for quarter in range(4 * BLK):
                total = landed[quarter, at : at + 32]
                for rank in range(CAP):
                    total = total + jnp.where(rows[rank] == quarter, pieces[rank], 0.0)
                landed[quarter, at : at + 32] = total

    land(outgoing_label[me], outgoing.at[me])
    loads[4].wait()

    def look(block, carry):
        for column in range(27):
            entry = neighbors_s[block, column]
            beside = me + entry // BLK - 1
            keep = (entry >= 0) & (beside >= 0) & (beside < peers)
            table_s[block * 27 + column] = jnp.where(keep, entry, 3 * BLK)
        return carry

    lax.fori_loop(0, BLK, look, 0)
    field[3 * BLK] = jnp.zeros((8, 64, C), BF16)
    loads[5].wait()
    fill_weights(wenc, big)
    loads[6].wait()
    fill_weights(wdec, big2)
    loads[7].wait()
    for pair in range(2):
        for parity in range(2):
            for xh in range(4):
                rows = [
                    cot[2 * pair + j, parity + 2 * xh].astype(F32).reshape(8, 1, 8, C)
                    for j in range(2)
                ]
                rows = jnp.concatenate(rows, axis=1).reshape(128, C)
                at = pair * 512 + xh * 128
                cot_t[parity * C : parity * C + C, at : at + 128] = rows.T.astype(BF16)

    def arrive(i, carry):
        step = step_of(i)
        source = source_of(step)
        drain(arrived.at[source], tile_sems.at[step])
        drain(arrived_label.at[source], label_sems.at[step])

        @pl.when(i + WINDOW < peers - 1)
        def _():
            send(i + WINDOW, 0)

        land(arrived_label[source], arrived.at[source])
        return carry

    lax.fori_loop(0, peers - 1, arrive, 0)
    for quarter in range(4 * BLK):
        planes = landed[quarter].astype(BF16).reshape(2, 64, C)
        x = 2 * (quarter % 4)
        field[BLK + quarter // 4, x : x + 2] = planes

    sub_row = lax.broadcasted_iota(jnp.int32, (8, C), 0)

    def pack_ends(source, block, ends):
        packed = []
        for x in range(1, 7):
            columns = source[BLK + block, x, 16:48].astype(F32).reshape(4, 8, C)
            total = columns[0]
            for i in range(4):
                total = jnp.where(sub_row == i, pltpu.roll(columns[i], i, 0), total)
                total = jnp.where(sub_row == 4 + i, pltpu.roll(columns[i], (i + 5) % 8, 0), total)
            packed.append(total)
        ends[block] = jnp.concatenate(packed, axis=0).astype(BF16)

    def unpack_ends(ends_in, target):
        def body(at, carry):
            side_of, block = at // BLK, lax.rem(at, BLK)
            packed = ends_in[side_of, block].astype(F32).reshape(6, 8, C)
            for x in range(1, 7):
                ends = packed[x - 1]
                columns = [
                    jnp.where(
                        sub_row == 7, pltpu.roll(ends, 3 - i, 0), pltpu.roll(ends, (8 - i) % 8, 0)
                    )
                    for i in range(4)
                ]
                target[2 * BLK * side_of + block, x, 16:48] = jnp.concatenate(
                    columns, axis=0
                ).astype(BF16)
            return carry

        lax.fori_loop(0, 2 * BLK, body, 0)

    def plane_moves(ref, first, count, sems):
        moves = []
        for base, where in ((0, right), (2 * BLK, left)):
            source, target = pl.ds(BLK + first, count), pl.ds(base + first, count)
            for x in (0, 7):
                moves.append(
                    remote(
                        ref.at[source, x], ref.at[target, x], sems.at[0], sems.at[1], at_blk(where)
                    )
                )
        return moves

    def row_moves(ref, first, count, sems):
        moves = []
        for base, where in ((0, right), (2 * BLK, left)):
            source, target = pl.ds(BLK + first, count), pl.ds(base + first, count)
            for y in (0, 48):
                at = pl.ds(y, 16)
                moves.append(
                    remote(
                        ref.at[source, 1:7, at],
                        ref.at[target, 1:7, at],
                        sems.at[2],
                        sems.at[3],
                        at_blk(where),
                    )
                )
        return moves

    def ends_moves(ends, ends_in, sems):
        return [
            remote(ends, ends_in.at[side_of], sems.at[4], sems.at[5], at_blk(where))
            for side_of, where in ((0, right), (1, left))
        ]

    def shell_drain(ref, ends_in, sems, which):
        drain(ref.at[0 : 2 * BLK, 0:2], sems.at[which])
        drain(ref.at[0 : 2 * BLK, 1:7, 0:32], sems.at[2 + which])
        drain(ends_in, sems.at[4 + which])

    for move in plane_moves(field, 0, BLK, halo_sems) + row_moves(field, 0, BLK, halo_sems):
        move.start()

    def pack_own(block, carry):
        pack_ends(field, block, ends)
        return carry

    lax.fori_loop(0, BLK, pack_own, 0)
    for move in ends_moves(ends, ends_in, halo_sems):
        move.start()
    shell_drain(field, ends_in, halo_sems, 1)
    unpack_ends(ends_in, field)
    shell_drain(field, ends_in, halo_sems, 0)

    fill_shifts(table_s, field, shifts)
    level = lax.broadcasted_iota(jnp.int32, (8, C), 0)
    even = lax.rem(level, 2) == 0

    in_group = turn // 2
    base = me - turn
    beyond = lax.rem(base + jnp.where(core == 0, peers - 1, SIB), peers)

    def swap_pooled(pair):
        piece = pooled.at[core, pl.ds(2 * pair, 2)]
        return remote(
            piece, piece, sibling_sems.at[0], sibling_sems.at[1 + pair], at_blk(other)
        )

    def sum_chip(pair):
        at = pl.ds(2 * pair, 2)
        drain(pooled.at[0, 0:2], sibling_sems.at[1 + pair])
        sums[2 + in_group, at] = (
            pooled[0, at].astype(F32) + pooled[1, at].astype(F32)
        ).astype(BF16)
        source = sums.at[2 + in_group, at]
        remote(
            source, source, sibling_sems.at[0], sibling_sems.at[3 + pair], at_blk(across)
        ).start()
        remote(
            source,
            sums.at[4 * (1 - core) + in_group, at],
            sibling_sems.at[0],
            sibling_sems.at[5],
            at_blk(beyond),
        ).start()

    def encode(pair, carry):
        total = convolve(shifts, big, pair)

        @pl.when(pair == 1)
        def _():
            sum_chip(0)

        rounded = jnp.maximum(total, 0.0).astype(BF16).astype(F32)
        for j in range(2):
            for xh in range(4):
                for half_x in range(2):
                    encoded[BLK + 2 * pair + j, 2 * xh + half_x] = (
                        rounded[xh, :, j, :, half_x * C : half_x * C + C]
                        .reshape(64, C)
                        .astype(BF16)
                    )
                flat = rounded[xh, :, j, :, :C] + rounded[xh, :, j, :, C:]
                flat = flat.reshape(4, 2, 8, C)
                flat = flat[:, 0] + flat[:, 1]
                folded = [
                    flat[y]
                    + jnp.where(even, pltpu.roll(flat[y], 7, 0), pltpu.roll(flat[y], 1, 0))
                    for y in range(4)
                ]
                packed = [
                    jnp.where(even, folded[2 * y], folded[2 * y + 1]) * 0.125 for y in range(2)
                ]
                pooled[core, 2 * pair + j, xh] = jnp.concatenate(packed, axis=0).astype(BF16)
        swap_pooled(pair).start()
        for move in plane_moves(encoded, 2 * pair, 2, encoded_sems):
            move.start()

        @pl.when(pair == 0)
        def _():
            for move in row_moves(encoded, 0, 2, encoded_sems):
                move.start()

        for j in range(2):
            pack_ends(encoded, 2 * pair + j, ends2)
        return carry

    lax.fori_loop(0, 2, encode, 0)
    sum_chip(1)
    for move in row_moves(encoded, 2, 2, encoded_sems) + ends_moves(ends2, ends2_in, encoded_sems):
        move.start()

    def mean_of(group):
        total = sums[2 * group].astype(F32) + sums[2 * group + 1].astype(F32)
        means[group] = (total * (1.0 / SIB)).astype(BF16)

    for pair in range(2):
        drain(pooled.at[0, 0:2], sibling_sems.at[3 + pair])
    mean_of(1)

    def join(side_of):
        coarse = jnp.dot(
            means[side_of].reshape(BLK * 64, C), wcoarse_ref[...], preferred_element_type=F32
        )
        coarse = jnp.maximum(coarse, 0.0).reshape(BLK, 4, 2, 8, C)
        for block in range(BLK):
            for xh in range(4):
                ups = []
                for y in range(2):
                    tile = coarse[block, xh, y]
                    for up in (
                        jnp.where(even, tile, pltpu.roll(tile, 1, 0)),
                        jnp.where(even, pltpu.roll(tile, 7, 0), tile),
                    ):
                        ups += [up, up]
                ups = jnp.concatenate(ups, axis=0)
                for half_x in range(2):
                    x = 2 * xh + half_x
                    at = BLK * side_of + block
                    field[at, x] = (encoded[at, x].astype(F32) + ups).astype(BF16)

    join(1)

    means[0] = means[1]
    means[2] = means[1]

    @pl.when((turn == 0) | (turn == SIB - 1))
    def _():
        drain(sums.at[0:2], sibling_sems.at[5])

    @pl.when(turn == 0)
    def _():
        mean_of(0)

    @pl.when(turn == SIB - 1)
    def _():
        mean_of(2)

    shell_drain(encoded, ends2_in, encoded_sems, 1)
    unpack_ends(ends2_in, encoded)
    join(0)
    join(2)
    fill_shifts(table_s, field, shifts)

    group_half = half_in.shape[1]
    piece_rows = piece_own.shape[1]
    active = group_half // piece_rows

    def swap(group):
        return remote(
            part.at[group, pl.ds(pl.multiple_of((1 - core) * group_half, 16), group_half)],
            half_in.at[group],
            core_sems.at[0],
            core_sems.at[1 + group],
            at_blk(other),
        )

    def piece_at(index):
        return pl.ds(pl.multiple_of(index * piece_rows, 16), piece_rows)

    def final_at(group, side_of, index):
        start = side_of * group_half + index * piece_rows
        start = start // (3 * C) * (9 * C) + group * (3 * C) + lax.rem(start, 3 * C)
        return pl.ds(pl.multiple_of(start, 16), piece_rows)

    def to_chip(step):
        return lax.rem(chip + step, chips)

    def from_chip(step):
        return lax.rem(chip + chips - step, chips)

    def scatter(group, step):
        return remote(
            half.at[group, piece_at(to_chip(step))],
            piece_in.at[group, chip],
            plane_sems.at[0],
            plane_sems.at[1 + group],
            at_blk(plane_peer(step)),
        )

    def gather(group, step):
        return remote(
            piece_own.at[group],
            grad_ref.at[final_at(group, core, chip)],
            gather_sems.at[0],
            gather_sems.at[1 + group if group < 2 else 2 + step],
            at_blk(plane_peer(step)),
        )

    def forward(group, index, source=None):
        at = final_at(group, core, index)
        return remote(
            grad_ref.at[at] if source is None else source,
            grad_ref.at[at], forward_sems.at[0],
            forward_sems.at[1],
            at_blk(other),

        )

    def each_step(action):
        def body(step, carry):
            action(step)
            return carry

        lax.fori_loop(1, chips, body, 0)

    def halve(group):
        drain(half_in.at[group], core_sems.at[1 + group])
        mine = pl.ds(pl.multiple_of(core * group_half, 16), group_half)
        half[group] = (part[group, mine].astype(F32) + half_in[group].astype(F32)).astype(BF16)

        def start(step):
            @pl.when(to_chip(step) < active)
            def _():
                scatter(group, step).start()

        each_step(start)

    def tap_row(dy, carry):
        @pl.when(dy < 3)
        def _():
            rows = [
                jnp.concatenate(
                    [
                        shifts[pair, u % 2, u // 2 : u // 2 + 4, pl.ds(dy, 8)].reshape(512, 3 * C)
                        for pair in range(2)
                    ],
                    axis=0,
                )
                for u in range(4)
            ]
            taps = jnp.dot(
                cot_t[...], jnp.concatenate(rows, axis=1), preferred_element_type=F32
            )
            for tap in range(9):
                at = tap * C
                total = taps[:C, at : at + C] + taps[C:, at + 3 * C : at + 4 * C]
                part[dy, at : at + C] = total.astype(BF16).T
            swap(dy).start()

        @pl.when(dy > 0)
        def _():
            halve(dy - 1)

        return carry

    lax.fori_loop(0, 4, tap_row, 0)

    def decode(pair):
        total = convolve(shifts, big2, pair)
        for j in range(2):
            for xh in range(4):
                for half_x in range(2):
                    x = 2 * xh + half_x
                    piece = total[xh, :, j, :, half_x * C : half_x * C + C].reshape(64, C)
                    block = 2 * pair + j
                    dec_ref[block, x] = (piece + field[BLK + block, x].astype(F32)).astype(BF16)

    def x_moves(group):
        return [
            remote(
                piece_x.at[group, rep],
                piece_x.at[group, rep],
                x_sems.at[0],
                x_sems.at[1 + group],
                at_rep(rep_peer(step)),
            )
            for step in range(1, reps)
        ]

    def reduce_piece(group):
        @pl.when(chip < active)
        def _():
            drain(piece_in.at[group, 0 : chips - 1], plane_sems.at[1 + group])
            piece_in[group, chip] = half[group, piece_at(chip)]

            def add(index, total):
                return total + piece_in[group, index].astype(F32)

            total = lax.fori_loop(0, chips, add, jnp.zeros((piece_rows, C), F32))
            piece_x[group, rep] = total.astype(BF16)
            for move in x_moves(group):
                move.start()

    def spread_piece(group):
        @pl.when(chip < active)
        def _():
            drain(piece_x.at[group, 0 : reps - 1], x_sems.at[1 + group])
            total = piece_x[group, 0].astype(F32)
            for index in range(1, reps):
                total = total + piece_x[group, index].astype(F32)
            piece_own[group] = total.astype(BF16)

            def start(step):
                gather(group, step).start()

            each_step(start)
            pltpu.make_async_copy(
                piece_own.at[group],
                grad_ref.at[final_at(group, core, chip)],
                load_sems.at[9 + group],
            ).start()
            forward(group, chip, piece_own.at[group]).start()

    def forward_pieces(group):
        if group < 2:

            @pl.when(chip < active)
            def _():
                drain(piece_in.at[group, 0 : active - 1], gather_sems.at[1 + group])

            @pl.when(chip >= active)
            def _():
                drain(piece_in.at[group, 0:active], gather_sems.at[1 + group])

        def come(step):
            @pl.when(from_chip(step) < active)
            def _():
                if group == 2:
                    drain(piece_own.at[group], gather_sems.at[2 + step])
                forward(group, from_chip(step)).start()

        each_step(come)

    def finish():
        drain(half_in, forward_sems.at[1])
        drain(half_in, forward_sems.at[0])
        drain(arrived_label.at[0 : peers - 1], label_sems.at[0])
        drain(arrived.at[0 : peers - 1], tile_sems.at[0])
        drain(sums.at[0:3], sibling_sems.at[0])
        shell_drain(encoded, ends2_in, encoded_sems, 0)
        drain(half_in, core_sems.at[0])

        @pl.when(chip < active)
        def _():
            drain(piece_in.at[:, 0 : active - 1], plane_sems.at[0])
            drain(piece_x.at[:, 0 : reps - 1], x_sems.at[0])
            drain(piece_in.at[:, 0 : chips - 1], gather_sems.at[0])
            for group in range(3):
                drain(piece_own.at[group], load_sems.at[9 + group])

        @pl.when(chip >= active)
        def _():
            drain(piece_in.at[:, 0:active], plane_sems.at[0])

    decode(0)
    reduce_piece(0)
    reduce_piece(1)
    decode(1)
    reduce_piece(2)
    spread_piece(0)
    spread_piece(1)
    spread_piece(2)
    for group in range(3):
        forward_pieces(group)
    finish()


def local(
    peers,
    reps,
    tiles,
    tile_rows,
    tile_owner,
    tile_slot,
    neighbors,
    w_enc,
    w_coarse,
    w_dec,
    cotangent,
):
    count = tiles.shape[1]
    chips = peers // 2
    group_half = 9 * C // 2
    piece_rows = min(
        rows for rows in (16, 48, 64, 192, 576) if rows * chips >= group_half
    )
    vmem = pl.BlockSpec(memory_space=pltpu.VMEM)
    anywhere = pl.BlockSpec(memory_space=pltpu.HBM)
    dma = pltpu.SemaphoreType.DMA
    decoded, grads = pl.pallas_call(
        functools.partial(kernel, count, peers, reps),
        out_shape=(
            jax.ShapeDtypeStruct((BLK, 8, 64, C), BF16),
            jax.ShapeDtypeStruct((27 * C, C), BF16),
        ),
        in_specs=[anywhere] * 6 + [vmem] + [anywhere] * 2,
        out_specs=(vmem, anywhere),
        scratch_shapes=[
            pltpu.SMEM((1, count), jnp.int32),
            pltpu.SMEM((1, count), jnp.int32),
            pltpu.SMEM((1, count), jnp.int32),
            pltpu.SMEM((BLK, 27), jnp.int32),
            pltpu.SMEM((BLK * 27,), jnp.int32),
            pltpu.VMEM((8, C), jnp.int32),
            pltpu.SMEM((8, C), jnp.int32),
            pltpu.VMEM((count, C, C), BF16),
            pltpu.VMEM((peers, CAP, C, C), BF16),
            pltpu.VMEM((peers, CAP, C), jnp.int32),
            pltpu.VMEM((peers, CAP, C, C), BF16),
            pltpu.VMEM((peers, CAP, C), jnp.int32),
            pltpu.VMEM((4 * BLK, C, C), F32),
            pltpu.VMEM((3 * BLK + 1, 8, 64, C), BF16),
            pltpu.VMEM((3 * BLK, 8, 64, C), BF16),
            pltpu.VMEM((2, 2, 5, 10, 16, 3 * C), BF16),
            pltpu.VMEM((12, 3 * C, 2 * C), BF16),
            pltpu.VMEM((12, 3 * C, 2 * C), BF16),
            pltpu.VMEM((27, C, C), BF16),
            pltpu.VMEM((27, C, C), BF16),
            pltpu.VMEM((BLK, 8, 64, C), BF16),
            pltpu.VMEM((2 * C, 1024), BF16),
            pltpu.VMEM((2, BLK, 4, 16, C), BF16),
            pltpu.VMEM((6, BLK, 4, 16, C), BF16),
            pltpu.VMEM((3, BLK, 4, 16, C), BF16),
            pltpu.VMEM((3, 9 * C, C), BF16),
            pltpu.VMEM((3, group_half, C), BF16),
            pltpu.VMEM((3, group_half, C), BF16),
            pltpu.VMEM((3, chips, piece_rows, C), BF16),
            pltpu.VMEM((3, reps, piece_rows, C), BF16),
            pltpu.VMEM((3, piece_rows, C), BF16),
            pltpu.VMEM((BLK, 48, C), BF16),
            pltpu.VMEM((2, BLK, 48, C), BF16),
            pltpu.VMEM((BLK, 48, C), BF16),
            pltpu.VMEM((2, BLK, 48, C), BF16),
            dma((12,)),
            dma((peers,)),
            dma((peers,)),
            dma((6,)),
            dma((6,)),
            dma((6,)),
            dma((4,)),
            dma((4,)),
            dma((4,)),
            dma((2 + chips,)),
            dma((2,)),
        ],
        compiler_params=pltpu.CompilerParams(
            collective_id=0, has_side_effects=True, vmem_limit_bytes=VMEM_LIMIT
        ),
        name="level",
    )(
        *[
            pltpu.with_memory_space_constraint(operand, pltpu.HBM)
            for operand in (
                tile_rows,
                tile_owner.reshape(1, count),
                tile_slot,
                neighbors[0],
                tiles[0],
                w_enc,
                w_coarse,
                w_dec,
                cotangent[0].reshape(BLK, 8, 64, C),
            )
        ]
    )
    return decoded.reshape(1, BLK, 512, C), grads.astype(F32).reshape(27, C, C)


def solution(mesh):
    placed = (
        P("rep", "blk", None, None),
        P("rep", "blk"),
        P("rep", "blk", None),
        P("rep", "blk"),
        P("rep", "blk", None),
        P(),
        P(),
        P(),
        P("rep", "blk", None, None),
    )
    return jax.shard_map(
        functools.partial(local, mesh.shape["blk"], mesh.shape["rep"]),
        mesh=mesh,
        in_specs=placed,
        out_specs=(P("rep", "blk", None, None), P()),
        check_vma=False,
    )
```

```python
import functools
import math

import jax
import jax.numpy as jnp
from jax import lax
from jax.experimental import pallas as pl
from jax.experimental.pallas import tpu as pltpu
from jax.sharding import PartitionSpec as P

C = 128
CAP = 2
BLK = 4
SIB = 4
F32 = jnp.float32
BF16 = jnp.bfloat16
MESH = pl.DeviceIdType.MESH
WINDOW = 20
MOVES_Y = (1, 1, 2, 1, 0, 2, 1, 3, 3, 2, 0, 2, 3, 3, 0)
MOVES_Z = (1, 3, 2, 0, 1, 1, 2, 1, 3, 0, 2, 3, 2, 0, 3)
VMEM_LIMIT = 48 * 1024 * 1024


def at_blk(index):
    return {"blk": index}


def at_rep(index):
    return {"rep": index}


def fill_weights(w_ref, big):
    zero = jnp.zeros((C, C), BF16)
    for u in range(4):
        for dy in range(3):
            for dz in range(3):
                for half in range(2):
                    dx = u - half
                    tap = w_ref[dx * 9 + dy * 3 + dz] if 0 <= dx <= 2 else zero
                    big[u * 3 + dy, dz * C : dz * C + C, half * C : half * C + C] = tap


def fill_shifts(tab_ref, field, shifts):
    level = lax.broadcasted_iota(jnp.int32, (10, 8, C), 1)

    def body(i, carry):
        pair, plane = i // 10, i % 10
        first = jnp.where(plane == 0, 0, jnp.where(plane == 9, 2, 1))
        at = lax.rem(plane + 7, 8)
        parts = []
        for j in range(2):
            base = (2 * pair + j) * 27 + first * 9
            cells = []
            for c in range(3):
                low = field[tab_ref[base + c], at, 48:64].astype(F32)[8:16]
                mid = field[tab_ref[base + 3 + c], at].astype(F32)
                high = field[tab_ref[base + 6 + c], at, 0:16].astype(F32)[0:8]
                cells.append(jnp.concatenate([low, mid, high], axis=0).reshape(10, 8, C))
            parts.append(
                (
                    pltpu.roll(jnp.where(level == 7, cells[0], cells[1]), 1, 1),
                    cells[1],
                    pltpu.roll(jnp.where(level == 0, cells[2], cells[1]), 7, 1),
                )
            )
        for c in range(3):
            both = jnp.concatenate([parts[0][c], parts[1][c]], axis=1).astype(BF16)
            shifts[pair, lax.rem(plane, 2), plane // 2, :, :, c * C : c * C + C] = both
        return carry

    lax.fori_loop(0, 20, body, 0)


def operand(shifts, pair, u, dy):
    return shifts[pair, u % 2, u // 2 : u // 2 + 4, dy : dy + 8].reshape(512, 3 * C)


def convolve(shifts, big, pair):
    taps = [operand(shifts, pair, u, dy) for u in range(4) for dy in range(3)]
    total = jnp.dot(
        jnp.concatenate(taps, axis=1),
        big[...].reshape(36 * C, 2 * C),
        preferred_element_type=F32,
    )
    return total.reshape(4, 8, 2, 8, 2 * C)


def kernel(
    count,
    peers,
    reps,
    rows_hbm,
    owner_hbm,
    slot_hbm,
    neighbors_hbm,
    tiles_hbm,
    wenc_hbm,
    wcoarse_ref,
    wdec_hbm,
    cot_hbm,
    dec_ref,
    grad_ref,
    rows_s,
    owner_s,
    slot_s,
    neighbors_s,
    table_s,
    places_v,
    places_s,
    tiles,
    outgoing,
    outgoing_label,
    arrived,
    arrived_label,
    landed,
    field,
    encoded,
    shifts,
    big,
    big2,
    wenc,
    wdec,
    cot,
    cot_t,
    pooled,
    sums,
    means,
    part,
    half_in,
    half,
    piece_in,
    piece_x,
    piece_own,
    ends,
    ends_in,
    ends2,
    ends2_in,
    load_sems,
    tile_sems,
    label_sems,
    halo_sems,
    encoded_sems,
    sibling_sems,
    core_sems,
    plane_sems,
    x_sems,
    gather_sems,
    forward_sems,
):
    me = lax.axis_index("blk")
    rep = lax.axis_index("rep")
    chips = peers // 2
    side = math.isqrt(chips)
    core, chip = lax.rem(me, 2), me // 2
    chip_y, chip_z = lax.rem(chip, side), chip // side
    other = me + 1 - 2 * core
    right, left = lax.rem(me + 1, peers), lax.rem(me + peers - 1, peers)

    loads = [
        pltpu.make_async_copy(source, target, load_sems.at[i])
        for i, (source, target) in enumerate(
            [
                (owner_hbm, owner_s),
                (rows_hbm, rows_s),
                (slot_hbm, slot_s),
                (tiles_hbm, tiles),
                (neighbors_hbm, neighbors_s),
                (wenc_hbm, wenc),
                (wdec_hbm, wdec),
                (cot_hbm, cot),
            ]
        )
    ]
    for load in loads:
        load.start()

    def remote(source, target, send_sem, recv_sem, where):
        return pltpu.make_async_remote_copy(
            src_ref=source,
            dst_ref=target,
            send_sem=send_sem,
            recv_sem=recv_sem,
            device_id=where,
            device_id_type=MESH,
        )

    def drain(ref, sem):
        pltpu.make_async_copy(ref, ref, sem).wait()

    turn = lax.rem(me, SIB)
    across = me - turn + lax.rem(turn + 2, SIB)

    def plane_peer(step):
        return 2 * lax.rem(chip + step, chips) + core

    def rep_peer(step):
        return lax.rem(rep + step, reps)

    barrier = pltpu.get_barrier_semaphore()

    def greet(step, carry):
        pl.semaphore_signal(
            barrier, inc=1, device_id=at_blk(lax.rem(me + step, peers)), device_id_type=MESH
        )
        return carry

    lax.fori_loop(1, peers, greet, 0)
    for step in range(1, reps):
        pl.semaphore_signal(
            barrier, inc=1, device_id=at_rep(rep_peer(step)), device_id_type=MESH
        )

    loads[0].wait()
    lane = lax.broadcasted_iota(jnp.int32, (8, C), 1)

    def note(t, carry):
        first, second = carry
        hit = lane == owner_s[0, t]
        second = jnp.where(hit & (first >= 0), t, second)
        first = jnp.where(hit & (first < 0), t, first)
        return first, second

    none = jnp.full((8, C), -1, jnp.int32)
    first, second = lax.fori_loop(0, count, note, (none, none))
    places_v[...] = jnp.where(lax.broadcasted_iota(jnp.int32, (8, C), 0) == 0, first, second)
    move = pltpu.make_async_copy(places_v, places_s, load_sems.at[8])
    move.start()
    loads[1].wait()
    loads[2].wait()
    move.wait()
    loads[3].wait()
    row = lax.broadcasted_iota(jnp.int32, (C, C), 0)

    def bucket(owner):
        for rank in range(CAP):
            tile = places_s[rank, owner]
            at = jnp.maximum(tile, 0)
            live = jnp.where(tile >= 0, rows_s[0, at], 0)
            outgoing[owner, rank] = jnp.where(row < live, tiles[at].astype(F32), 0.0).astype(BF16)
            outgoing_label[owner, rank : rank + 1] = jnp.full((1, C), slot_s[0, at], jnp.int32)

    def pick(table, k):
        value = 0
        for at, entry in enumerate(table):
            value = jnp.where(k == at, entry, value)
        return value

    def chip_beside(step, sign):
        k = lax.rem(step - 1, chips - 1)
        if side == 4:
            move_y, move_z = pick(MOVES_Y, k), pick(MOVES_Z, k)
        else:
            move_y = lax.rem(k + 1, side)
            move_z = lax.rem((k + 1) // side + move_y, side)
        away = step < peers - 1
        move_y, move_z = jnp.where(away, move_y, 0), jnp.where(away, move_z, 0)
        return side * lax.rem(chip_z + side + sign * move_z, side) + lax.rem(
            chip_y + side + sign * move_y, side
        )

    def turned(step):
        return jnp.where(step < chips, core, 1 - core)

    def target_of(step):
        return 2 * chip_beside(step, 1 - 2 * core) + turned(step)

    def source_of(step):
        from_core = turned(step)
        return 2 * chip_beside(step, 2 * from_core - 1) + from_core

    def label_move(step):
        peer = target_of(step)
        return remote(
            outgoing_label.at[peer],
            arrived_label.at[me],
            label_sems.at[0],
            label_sems.at[step],
            at_blk(peer),
        )

    def tile_move(step):
        peer = target_of(step)
        return remote(
            outgoing.at[peer], arrived.at[me], tile_sems.at[0], tile_sems.at[step], at_blk(peer)
        )

    pl.semaphore_wait(barrier, peers - 1 + reps - 1)

    def step_of(i):
        return 1 + i

    def send(i, carry):
        step = step_of(i)
        bucket(target_of(step))
        label_move(step).start()
        tile_move(step).start()
        return carry

    lax.fori_loop(0, WINDOW, send, 0)
    bucket(me)

    landed[...] = jnp.zeros_like(landed)

    def land(labels, tiles_at):
        rows = [labels[rank : rank + 1] for rank in range(CAP)]
        for at in range(0, C, 32):
            pieces = [tiles_at[rank, at : at + 32].astype(F32) for rank in range(CAP)]
            for quarter in range(4 * BLK):
                total = landed[quarter, at : at + 32]
                for rank in range(CAP):
                    total = total + jnp.where(rows[rank] == quarter, pieces[rank], 0.0)
                landed[quarter, at : at + 32] = total

    land(outgoing_label[me], outgoing.at[me])
    loads[4].wait()

    def look(block, carry):
        for column in range(27):
            entry = neighbors_s[block, column]
            beside = me + entry // BLK - 1
            keep = (entry >= 0) & (beside >= 0) & (beside < peers)
            table_s[block * 27 + column] = jnp.where(keep, entry, 3 * BLK)
        return carry

    lax.fori_loop(0, BLK, look, 0)
    field[3 * BLK] = jnp.zeros((8, 64, C), BF16)
    loads[5].wait()
    fill_weights(wenc, big)
    loads[6].wait()
    fill_weights(wdec, big2)
    loads[7].wait()
    for pair in range(2):
        for parity in range(2):
            for xh in range(4):
                rows = [
                    cot[2 * pair + j, parity + 2 * xh].astype(F32).reshape(8, 1, 8, C)
                    for j in range(2)
                ]
                rows = jnp.concatenate(rows, axis=1).reshape(128, C)
                at = pair * 512 + xh * 128
                cot_t[parity * C : parity * C + C, at : at + 128] = rows.T.astype(BF16)

    def arrive(i, carry):
        step = step_of(i)
        source = source_of(step)
        drain(arrived.at[source], tile_sems.at[step])
        drain(arrived_label.at[source], label_sems.at[step])

        @pl.when(i + WINDOW < peers - 1)
        def _():
            send(i + WINDOW, 0)

        land(arrived_label[source], arrived.at[source])
        return carry

    lax.fori_loop(0, peers - 1, arrive, 0)
    for quarter in range(4 * BLK):
        planes = landed[quarter].astype(BF16).reshape(2, 64, C)
        x = 2 * (quarter % 4)
        field[BLK + quarter // 4, x : x + 2] = planes

    sub_row = lax.broadcasted_iota(jnp.int32, (8, C), 0)

    def pack_ends(source, block, ends):
        packed = []
        for x in range(1, 7):
            columns = source[BLK + block, x, 16:48].astype(F32).reshape(4, 8, C)
            total = columns[0]
            for i in range(4):
                total = jnp.where(sub_row == i, pltpu.roll(columns[i], i, 0), total)
                total = jnp.where(sub_row == 4 + i, pltpu.roll(columns[i], (i + 5) % 8, 0), total)
            packed.append(total)
        ends[block] = jnp.concatenate(packed, axis=0).astype(BF16)

    def unpack_ends(ends_in, target):
        def body(at, carry):
            side_of, block = at // BLK, lax.rem(at, BLK)
            packed = ends_in[side_of, block].astype(F32).reshape(6, 8, C)
            for x in range(1, 7):
                ends = packed[x - 1]
                columns = [
                    jnp.where(
                        sub_row == 7, pltpu.roll(ends, 3 - i, 0), pltpu.roll(ends, (8 - i) % 8, 0)
                    )
                    for i in range(4)
                ]
                target[2 * BLK * side_of + block, x, 16:48] = jnp.concatenate(
                    columns, axis=0
                ).astype(BF16)
            return carry

        lax.fori_loop(0, 2 * BLK, body, 0)

    def plane_moves(ref, first, count, sems):
        moves = []
        for base, where in ((0, right), (2 * BLK, left)):
            source, target = pl.ds(BLK + first, count), pl.ds(base + first, count)
            for x in (0, 7):
                moves.append(
                    remote(
                        ref.at[source, x], ref.at[target, x], sems.at[0], sems.at[1], at_blk(where)
                    )
                )
        return moves

    def row_moves(ref, first, count, sems):
        moves = []
        for base, where in ((0, right), (2 * BLK, left)):
            source, target = pl.ds(BLK + first, count), pl.ds(base + first, count)
            for y in (0, 48):
                at = pl.ds(y, 16)
                moves.append(
                    remote(
                        ref.at[source, 1:7, at],
                        ref.at[target, 1:7, at],
                        sems.at[2],
                        sems.at[3],
                        at_blk(where),
                    )
                )
        return moves

    def ends_moves(ends, ends_in, sems):
        return [
            remote(ends, ends_in.at[side_of], sems.at[4], sems.at[5], at_blk(where))
            for side_of, where in ((0, right), (1, left))
        ]

    def shell_drain(ref, ends_in, sems, which):
        drain(ref.at[0 : 2 * BLK, 0:2], sems.at[which])
        drain(ref.at[0 : 2 * BLK, 1:7, 0:32], sems.at[2 + which])
        drain(ends_in, sems.at[4 + which])

    for move in plane_moves(field, 0, BLK, halo_sems) + row_moves(field, 0, BLK, halo_sems):
        move.start()

    def pack_own(block, carry):
        pack_ends(field, block, ends)
        return carry

    lax.fori_loop(0, BLK, pack_own, 0)
    for move in ends_moves(ends, ends_in, halo_sems):
        move.start()
    shell_drain(field, ends_in, halo_sems, 1)
    unpack_ends(ends_in, field)
    shell_drain(field, ends_in, halo_sems, 0)

    fill_shifts(table_s, field, shifts)
    level = lax.broadcasted_iota(jnp.int32, (8, C), 0)
    even = lax.rem(level, 2) == 0

    in_group = turn // 2
    base = me - turn
    beyond = lax.rem(base + jnp.where(core == 0, peers - 1, SIB), peers)

    def swap_pooled(pair):
        piece = pooled.at[core, pl.ds(2 * pair, 2)]
        return remote(
            piece, piece, sibling_sems.at[0], sibling_sems.at[1 + pair], at_blk(other)
        )

    def sum_chip(pair):
        at = pl.ds(2 * pair, 2)
        drain(pooled.at[0, 0:2], sibling_sems.at[1 + pair])
        sums[2 + in_group, at] = (
            pooled[0, at].astype(F32) + pooled[1, at].astype(F32)
        ).astype(BF16)
        source = sums.at[2 + in_group, at]
        remote(
            source, source, sibling_sems.at[0], sibling_sems.at[3 + pair], at_blk(across)
        ).start()
        remote(
            source,
            sums.at[4 * (1 - core) + in_group, at],
            sibling_sems.at[0],
            sibling_sems.at[5],
            at_blk(beyond),
        ).start()

    def encode(pair, carry):
        total = convolve(shifts, big, pair)

        @pl.when(pair == 1)
        def _():
            sum_chip(0)

        rounded = jnp.maximum(total, 0.0).astype(BF16).astype(F32)
        for j in range(2):
            for xh in range(4):
                for half_x in range(2):
                    encoded[BLK + 2 * pair + j, 2 * xh + half_x] = (
                        rounded[xh, :, j, :, half_x * C : half_x * C + C]
                        .reshape(64, C)
                        .astype(BF16)
                    )
                flat = rounded[xh, :, j, :, :C] + rounded[xh, :, j, :, C:]
                flat = flat.reshape(4, 2, 8, C)
                flat = flat[:, 0] + flat[:, 1]
                folded = [
                    flat[y]
                    + jnp.where(even, pltpu.roll(flat[y], 7, 0), pltpu.roll(flat[y], 1, 0))
                    for y in range(4)
                ]
                packed = [
                    jnp.where(even, folded[2 * y], folded[2 * y + 1]) * 0.125 for y in range(2)
                ]
                pooled[core, 2 * pair + j, xh] = jnp.concatenate(packed, axis=0).astype(BF16)
        swap_pooled(pair).start()
        for move in plane_moves(encoded, 2 * pair, 2, encoded_sems):
            move.start()

        @pl.when(pair == 0)
        def _():
            for move in row_moves(encoded, 0, 2, encoded_sems):
                move.start()

        for j in range(2):
            pack_ends(encoded, 2 * pair + j, ends2)
        return carry

    lax.fori_loop(0, 2, encode, 0)
    sum_chip(1)
    for move in row_moves(encoded, 2, 2, encoded_sems) + ends_moves(ends2, ends2_in, encoded_sems):
        move.start()

    def mean_of(group):
        total = sums[2 * group].astype(F32) + sums[2 * group + 1].astype(F32)
        means[group] = (total * (1.0 / SIB)).astype(BF16)

    for pair in range(2):
        drain(pooled.at[0, 0:2], sibling_sems.at[3 + pair])
    mean_of(1)

    def join(side_of):
        coarse = jnp.dot(
            means[side_of].reshape(BLK * 64, C), wcoarse_ref[...], preferred_element_type=F32
        )
        coarse = jnp.maximum(coarse, 0.0).reshape(BLK, 4, 2, 8, C)
        for block in range(BLK):
            for xh in range(4):
                ups = []
                for y in range(2):
                    tile = coarse[block, xh, y]
                    for up in (
                        jnp.where(even, tile, pltpu.roll(tile, 1, 0)),
                        jnp.where(even, pltpu.roll(tile, 7, 0), tile),
                    ):
                        ups += [up, up]
                ups = jnp.concatenate(ups, axis=0)
                for half_x in range(2):
                    x = 2 * xh + half_x
                    at = BLK * side_of + block
                    field[at, x] = (encoded[at, x].astype(F32) + ups).astype(BF16)

    join(1)

    means[0] = means[1]
    means[2] = means[1]

    @pl.when((turn == 0) | (turn == SIB - 1))
    def _():
        drain(sums.at[0:2], sibling_sems.at[5])

    @pl.when(turn == 0)
    def _():
        mean_of(0)

    @pl.when(turn == SIB - 1)
    def _():
        mean_of(2)

    shell_drain(encoded, ends2_in, encoded_sems, 1)
    unpack_ends(ends2_in, encoded)
    join(0)
    join(2)
    fill_shifts(table_s, field, shifts)

    group_half = half_in.shape[1]
    piece_rows = piece_own.shape[1]
    active = group_half // piece_rows

    def swap(group):
        return remote(
            part.at[group, pl.ds(pl.multiple_of((1 - core) * group_half, 16), group_half)],
            half_in.at[group],
            core_sems.at[0],
            core_sems.at[1 + group],
            at_blk(other),
        )

    def piece_at(index):
        return pl.ds(pl.multiple_of(index * piece_rows, 16), piece_rows)

    def final_at(group, side_of, index):
        start = side_of * group_half + index * piece_rows
        start = start // (3 * C) * (9 * C) + group * (3 * C) + lax.rem(start, 3 * C)
        return pl.ds(pl.multiple_of(start, 16), piece_rows)

    def to_chip(step):
        return lax.rem(chip + step, chips)

    def from_chip(step):
        return lax.rem(chip + chips - step, chips)

    def scatter(group, step):
        return remote(
            half.at[group, piece_at(to_chip(step))],
            piece_in.at[group, chip],
            plane_sems.at[0],
            plane_sems.at[1 + group],
            at_blk(plane_peer(step)),
        )

    def gather(group, step):
        return remote(
            piece_own.at[group],
            grad_ref.at[final_at(group, core, chip)],
            gather_sems.at[0],
            gather_sems.at[1 + group if group < 2 else 2 + step],
            at_blk(plane_peer(step)),
        )

    def forward(group, index, source=None):
        at = final_at(group, core, index)
        return remote(
            grad_ref.at[at] if source is None else source,
            grad_ref.at[at], forward_sems.at[0],
            forward_sems.at[1],
            at_blk(other),

        )

    def each_step(action):
        def body(step, carry):
            action(step)
            return carry

        lax.fori_loop(1, chips, body, 0)

    def halve(group):
        drain(half_in.at[group], core_sems.at[1 + group])
        mine = pl.ds(pl.multiple_of(core * group_half, 16), group_half)
        half[group] = (part[group, mine].astype(F32) + half_in[group].astype(F32)).astype(BF16)

        def start(step):
            @pl.when(to_chip(step) < active)
            def _():
                scatter(group, step).start()

        each_step(start)

    def tap_row(dy, carry):
        @pl.when(dy < 3)
        def _():
            rows = [
                jnp.concatenate(
                    [
                        shifts[pair, u % 2, u // 2 : u // 2 + 4, pl.ds(dy, 8)].reshape(512, 3 * C)
                        for pair in range(2)
                    ],
                    axis=0,
                )
                for u in range(4)
            ]
            taps = jnp.dot(
                cot_t[...], jnp.concatenate(rows, axis=1), preferred_element_type=F32
            )
            for tap in range(9):
                at = tap * C
                total = taps[:C, at : at + C] + taps[C:, at + 3 * C : at + 4 * C]
                part[dy, at : at + C] = total.astype(BF16).T
            swap(dy).start()

        @pl.when(dy > 0)
        def _():
            halve(dy - 1)

        return carry

    lax.fori_loop(0, 4, tap_row, 0)

    def decode(pair):
        total = convolve(shifts, big2, pair)
        for j in range(2):
            for xh in range(4):
                for half_x in range(2):
                    x = 2 * xh + half_x
                    piece = total[xh, :, j, :, half_x * C : half_x * C + C].reshape(64, C)
                    block = 2 * pair + j
                    dec_ref[block, x] = (piece + field[BLK + block, x].astype(F32)).astype(BF16)

    def x_moves(group):
        return [
            remote(
                piece_x.at[group, rep],
                piece_x.at[group, rep],
                x_sems.at[0],
                x_sems.at[1 + group],
                at_rep(rep_peer(step)),
            )
            for step in range(1, reps)
        ]

    def reduce_piece(group):
        @pl.when(chip < active)
        def _():
            drain(piece_in.at[group, 0 : chips - 1], plane_sems.at[1 + group])
            piece_in[group, chip] = half[group, piece_at(chip)]

            def add(index, total):
                return total + piece_in[group, index].astype(F32)

            total = lax.fori_loop(0, chips, add, jnp.zeros((piece_rows, C), F32))
            piece_x[group, rep] = total.astype(BF16)
            for move in x_moves(group):
                move.start()

    def spread_piece(group):
        @pl.when(chip < active)
        def _():
            drain(piece_x.at[group, 0 : reps - 1], x_sems.at[1 + group])
            total = piece_x[group, 0].astype(F32)
            for index in range(1, reps):
                total = total + piece_x[group, index].astype(F32)
            piece_own[group] = total.astype(BF16)

            def start(step):
                gather(group, step).start()

            each_step(start)
            pltpu.make_async_copy(
                piece_own.at[group],
                grad_ref.at[final_at(group, core, chip)],
                load_sems.at[9 + group],
            ).start()
            forward(group, chip, piece_own.at[group]).start()

    def forward_pieces(group):
        if group < 2:

            @pl.when(chip < active)
            def _():
                drain(piece_in.at[group, 0 : active - 1], gather_sems.at[1 + group])

            @pl.when(chip >= active)
            def _():
                drain(piece_in.at[group, 0:active], gather_sems.at[1 + group])

        def come(step):
            @pl.when(from_chip(step) < active)
            def _():
                if group == 2:
                    drain(piece_own.at[group], gather_sems.at[2 + step])
                forward(group, from_chip(step)).start()

        each_step(come)

    def finish():
        drain(half_in, forward_sems.at[1])
        drain(half_in, forward_sems.at[0])
        drain(arrived_label.at[0 : peers - 1], label_sems.at[0])
        drain(arrived.at[0 : peers - 1], tile_sems.at[0])
        drain(sums.at[0:3], sibling_sems.at[0])
        shell_drain(encoded, ends2_in, encoded_sems, 0)
        drain(half_in, core_sems.at[0])

        @pl.when(chip < active)
        def _():
            drain(piece_in.at[:, 0 : active - 1], plane_sems.at[0])
            drain(piece_x.at[:, 0 : reps - 1], x_sems.at[0])
            drain(piece_in.at[:, 0 : chips - 1], gather_sems.at[0])
            for group in range(3):
                drain(piece_own.at[group], load_sems.at[9 + group])

        @pl.when(chip >= active)
        def _():
            drain(piece_in.at[:, 0:active], plane_sems.at[0])

    decode(0)
    reduce_piece(0)
    reduce_piece(1)
    decode(1)
    reduce_piece(2)
    spread_piece(0)
    spread_piece(1)
    spread_piece(2)
    for group in range(3):
        forward_pieces(group)
    finish()


def local(
    peers,
    reps,
    tiles,
    tile_rows,
    tile_owner,
    tile_slot,
    neighbors,
    w_enc,
    w_coarse,
    w_dec,
    cotangent,
):
    count = tiles.shape[1]
    chips = peers // 2
    group_half = 9 * C // 2
    piece_rows = min(
        rows for rows in (16, 48, 64, 192, 576) if rows * chips >= group_half
    )
    vmem = pl.BlockSpec(memory_space=pltpu.VMEM)
    anywhere = pl.BlockSpec(memory_space=pltpu.HBM)
    dma = pltpu.SemaphoreType.DMA
    decoded, grads = pl.pallas_call(
        functools.partial(kernel, count, peers, reps),
        out_shape=(
            jax.ShapeDtypeStruct((BLK, 8, 64, C), BF16),
            jax.ShapeDtypeStruct((27 * C, C), BF16),
        ),
        in_specs=[anywhere] * 6 + [vmem] + [anywhere] * 2,
        out_specs=(vmem, anywhere),
        scratch_shapes=[
            pltpu.SMEM((1, count), jnp.int32),
            pltpu.SMEM((1, count), jnp.int32),
            pltpu.SMEM((1, count), jnp.int32),
            pltpu.SMEM((BLK, 27), jnp.int32),
            pltpu.SMEM((BLK * 27,), jnp.int32),
            pltpu.VMEM((8, C), jnp.int32),
            pltpu.SMEM((8, C), jnp.int32),
            pltpu.VMEM((count, C, C), BF16),
            pltpu.VMEM((peers, CAP, C, C), BF16),
            pltpu.VMEM((peers, CAP, C), jnp.int32),
            pltpu.VMEM((peers, CAP, C, C), BF16),
            pltpu.VMEM((peers, CAP, C), jnp.int32),
            pltpu.VMEM((4 * BLK, C, C), F32),
            pltpu.VMEM((3 * BLK + 1, 8, 64, C), BF16),
            pltpu.VMEM((3 * BLK, 8, 64, C), BF16),
            pltpu.VMEM((2, 2, 5, 10, 16, 3 * C), BF16),
            pltpu.VMEM((12, 3 * C, 2 * C), BF16),
            pltpu.VMEM((12, 3 * C, 2 * C), BF16),
            pltpu.VMEM((27, C, C), BF16),
            pltpu.VMEM((27, C, C), BF16),
            pltpu.VMEM((BLK, 8, 64, C), BF16),
            pltpu.VMEM((2 * C, 1024), BF16),
            pltpu.VMEM((2, BLK, 4, 16, C), BF16),
            pltpu.VMEM((6, BLK, 4, 16, C), BF16),
            pltpu.VMEM((3, BLK, 4, 16, C), BF16),
            pltpu.VMEM((3, 9 * C, C), BF16),
            pltpu.VMEM((3, group_half, C), BF16),
            pltpu.VMEM((3, group_half, C), BF16),
            pltpu.VMEM((3, chips, piece_rows, C), BF16),
            pltpu.VMEM((3, reps, piece_rows, C), BF16),
            pltpu.VMEM((3, piece_rows, C), BF16),
            pltpu.VMEM((BLK, 48, C), BF16),
            pltpu.VMEM((2, BLK, 48, C), BF16),
            pltpu.VMEM((BLK, 48, C), BF16),
            pltpu.VMEM((2, BLK, 48, C), BF16),
            dma((12,)),
            dma((peers,)),
            dma((peers,)),
            dma((6,)),
            dma((6,)),
            dma((6,)),
            dma((4,)),
            dma((4,)),
            dma((4,)),
            dma((2 + chips,)),
            dma((2,)),
        ],
        compiler_params=pltpu.CompilerParams(
            collective_id=0, has_side_effects=True, vmem_limit_bytes=VMEM_LIMIT
        ),
        name="level",
    )(
        *[
            pltpu.with_memory_space_constraint(operand, pltpu.HBM)
            for operand in (
                tile_rows,
                tile_owner.reshape(1, count),
                tile_slot,
                neighbors[0],
                tiles[0],
                w_enc,
                w_coarse,
                w_dec,
                cotangent[0].reshape(BLK, 8, 64, C),
            )
        ]
    )
    return decoded.reshape(1, BLK, 512, C), grads.astype(F32).reshape(27, C, C)


def solution(mesh):
    placed = (
        P("rep", "blk", None, None),
        P("rep", "blk"),
        P("rep", "blk", None),
        P("rep", "blk"),
        P("rep", "blk", None),
        P(),
        P(),
        P(),
        P("rep", "blk", None, None),
    )
    return jax.shard_map(
        functools.partial(local, mesh.shape["blk"], mesh.shape["rep"]),
        mesh=mesh,
        in_specs=placed,
        out_specs=(P("rep", "blk", None, None), P()),
        check_vma=False,
    )
```
